32 devices in a mesh: seq: 8 (over z, x), head: 4 (over y, core).
Axes of the slice: x: 2, y: 2, z: 4, core: 2. Of those that a mesh axis runs over, the one named last changes fastest.
Arguments:
- tokens: bfloat16 [6, 2048, 2048], P(None, 'seq'), may hold values from -6 to 6
- segments: int32 [6, 2048], P(None, 'seq'), may hold values from 0 to 1, as said below
- norm_gain: float32 [2048], replicated, may hold values from 0.1 to 1.9
- w_zx: bfloat16 [2048, 2, 4096], P(None, None, 'head'), may hold values from -0.125 to 0.125
- w_bc: bfloat16 [2048, 256], replicated, may hold values from -0.125 to 0.125
- w_dt: bfloat16 [2048, 64], P(None, 'head'), may hold values from -0.125 to 0.125
- conv_x: float32 [4, 4096], P(None, 'head'), may hold values from -3 to 3
- conv_x_bias: float32 [4096], P('head'), may hold values from -0.5 to 0.5
- conv_bc: float32 [4, 256], replicated, may hold values from -3 to 3
- conv_bc_bias: float32 [256], replicated, may hold values from -0.5 to 0.5
- dt_bias: float32 [64], P('head'), may hold values from -2 to 1
- a_log: float32 [64], P('head'), may hold values from -9 to -2
- d_skip: float32 [64], P('head'), may hold values from 0.5 to 1.5
- gate_gain: float32 [4096], P('head'), may hold values from 0.1 to 1.9
- w_out: bfloat16 [2048, 4096], P(None, 'head'), may hold values from -0.09375 to 0.09375
- cotangent: bfloat16 [6, 2048, 2048], P(None, 'seq', 'head'), may hold values from -6 to 6
Outputs:
- layer_out: bfloat16 [6, 2048, 2048], P(None, 'seq', 'head')
- input_grad: bfloat16 [6, 2048, 2048], P(None, 'seq', 'head')
- norm_gain_grad: float32 [2048], P('head')
- w_zx_grad: float32 [2048, 2, 4096], P('seq', None, 'head')
- w_bc_grad: float32 [2048, 256], P('seq')
- w_dt_grad: float32 [2048, 64], P('seq', 'head')
- conv_x_grad: float32 [4, 4096], P(None, 'head')
- conv_x_bias_grad: float32 [4096], P('head')
- conv_bc_grad: float32 [4, 256], replicated
- conv_bc_bias_grad: float32 [256], replicated
- dt_bias_grad: float32 [64], P('head')
- a_log_grad: float32 [64], P('head')
- d_skip_grad: float32 [64], P('head')
- gate_gain_grad: float32 [4096], P('head')
- w_out_grad: float32 [2048, 4096], P('seq', 'head')
The draws below stay inside these ranges and needn't reach their ends.
Inputs may be any that keep to these rules, and one draw needn't show every extreme that they name: `segments`: within a sequence the segment numbers start at 0 and rise by 0 or 1 from one position to the next; every sequence holds exactly 2 documents, each of 200 to 2000 positions, and its longest document has exactly min(2000, 1848) positions.
All inputs are finite; a program needn't handle non-finite values.
Results may differ from the reference program's by a relative error of at most 0.03.
The reference program's roundings to bfloat16 on the way count: a program that leaves them out, or rounds other values in their place, can miss the bound.
Values may be sent and summed in bfloat16 or wider, within the bound.
No kernel may reach another device: no remote copies, remote signals or barrier semaphores. Data moves between devices by JAX's collectives and lax.ppermute only.
A program may use at most 256 MiB of HBM per device.

```python
from functools import partial
import jax
import jax.numpy as jnp
from jax import lax

MODEL = 2048
HEADS = 64
HEAD_DIM = 64
STATE = 128
KERNEL = 4
BLOCK_LEN = 256
SEQS = 6
DOC_MIN = 200
DOC_MAX = 2000
INNER = 4096
LENGTH = 2048
DOC_COUNT = 2


def draw_segments(key, part):
    key = jax.random.fold_in(key, 11)
    weight_key, place_key = jax.random.split(key)
    others = DOC_COUNT - 1
    longest = min(DOC_MAX, LENGTH - others * DOC_MIN)
    spare = LENGTH - longest - others * DOC_MIN
    doc_index = jnp.arange(DOC_COUNT, dtype=jnp.int32)
    long_place = jax.random.randint(place_key, (SEQS, 1), 0, DOC_COUNT).astype(jnp.int32)
    is_long = doc_index[None, :] == long_place
    doc_weights = jax.random.randint(weight_key, (SEQS, DOC_COUNT), 2, 4).astype(jnp.int32)
    doc_weights = jnp.where(is_long, 0, doc_weights)
    weight_sums = jnp.cumsum(doc_weights, axis=1)
    weight_total = jnp.maximum(weight_sums[:, -1:], 1)
    base_len = jnp.where(is_long, longest, DOC_MIN).astype(jnp.int32)
    doc_ends = jnp.cumsum(base_len, axis=1) + spare * weight_sums // weight_total
    places = jnp.arange(LENGTH, dtype=jnp.int32)
    return jnp.sum((doc_ends[:, None, :] <= places[None, :, None]).astype(jnp.int32), axis=-1)


def shard_levels(key, dims, cuts, smallest, top_value):
    loudness, own = 1.0, jax.random.fold_in(key, 6)
    for axis_at, parts in cuts:
        heights = jnp.exp(jax.random.uniform(jax.random.fold_in(own, axis_at), (parts,), jnp.float32, smallest / len(cuts), top_value / len(cuts)))
        loudness = loudness * jnp.repeat(heights, dims[axis_at] // parts).reshape([-1 if axis == axis_at else 1 for axis in range(len(dims))])
    return loudness


def noise(stream_key, dims, width, limit, cuts=(), held_as=jnp.bfloat16):
    factor_of = shard_levels(stream_key, dims, cuts, -0.22, 0.18) if cuts else 1.0
    values = jax.random.normal(stream_key, dims, jnp.float32) * width * factor_of
    return jnp.minimum(jnp.maximum(values, -limit), limit).astype(held_as)


def setup_inputs(seed: int = 0) -> dict:
    seeds = jax.random.split(jax.random.key(seed), 17)
    tokens = noise(seeds[0], (SEQS, LENGTH, MODEL), 1.0, 6.0, ((1, 8),))
    segments = draw_segments(jax.random.fold_in(seeds[16], 71), 0)
    norm_gain = jnp.clip(1.0 + 0.18 * jax.random.normal(seeds[2], (MODEL,), jnp.float32), 0.1, 1.9)
    w_zx = noise(seeds[3], (MODEL, 2, INNER), MODEL ** -0.5, 0.125, ((2, 4),))
    w_bc = noise(seeds[4], (MODEL, 2 * STATE), MODEL ** -0.5, 0.125)
    w_dt = noise(seeds[5], (MODEL, HEADS), MODEL ** -0.5, 0.125, ((1, 4),))
    conv_x = noise(seeds[6], (KERNEL, INNER), KERNEL ** -0.5, 3.0, ((1, 4),), jnp.float32)
    conv_x_bias = jnp.clip(jax.random.uniform(seeds[7], (INNER,), jnp.float32, -0.5, 0.5) * shard_levels(seeds[7], (INNER,), ((0, 4),), -0.4, 0.0), -0.5, 0.5)
    conv_bc = noise(seeds[8], (KERNEL, 2 * STATE), KERNEL ** -0.5, 3.0, (), jnp.float32)
    conv_bc_bias = jnp.clip(jax.random.uniform(seeds[9], (2 * STATE,), jnp.float32, -0.5, 0.5), -0.5, 0.5)
    dt_bias = jnp.clip(-2.0 + 3.0 * jax.random.uniform(seeds[10], (HEADS,), jnp.float32) ** shard_levels(seeds[10], (HEADS,), ((0, 4),), -0.2, 0.2), -2.0, 1.0)
    a_log = jnp.clip(-9.0 + 7.0 * jax.random.uniform(seeds[11], (HEADS,), jnp.float32) ** shard_levels(seeds[11], (HEADS,), ((0, 4),), -0.2, 0.2), -9.0, -2.0)
    d_skip = jnp.clip(0.5 + 1.0 * jax.random.uniform(seeds[12], (HEADS,), jnp.float32) ** shard_levels(seeds[12], (HEADS,), ((0, 4),), -0.2, 0.2), 0.5, 1.5)
    gate_gain = jnp.clip(1.0 + 0.18 * jax.random.normal(seeds[13], (INNER,), jnp.float32), 0.1, 1.9)
    w_out = noise(seeds[14], (MODEL, INNER), INNER ** -0.5, 0.09375, ((1, 4),))
    cotangent = noise(seeds[15], (SEQS, LENGTH, MODEL), 1.0, 6.0, ((1, 8), (2, 4)))
    return {"tokens": tokens, "segments": segments, "norm_gain": norm_gain, "w_zx": w_zx, "w_bc": w_bc, "w_dt": w_dt, "conv_x": conv_x, "conv_x_bias": conv_x_bias, "conv_bc": conv_bc, "conv_bc_bias": conv_bc_bias, "dt_bias": dt_bias, "a_log": a_log, "d_skip": d_skip, "gate_gain": gate_gain, "w_out": w_out, "cotangent": cotangent}


EPS = 1e-05
HIGHEST_PREC = lax.Precision.HIGHEST

@jax.custom_vjp
def low(v):
    return lax.optimization_barrier(v.astype(jnp.bfloat16)).astype(jnp.float32)

@jax.custom_vjp
def low_back(v):
    return v

def low_keep(v):
    return (low(v), None)

def low_pass(kept, grad):
    return (grad,)

def back_keep(v):
    return (v, None)

def back_low(kept, grad):
    return (low(grad),)
low.defvjp(low_keep, low_pass)
low_back.defvjp(back_keep, back_low)

def silu(value):
    return value * jax.nn.sigmoid(value)

def causal_conv(pre_conv, seg_ids, weight, bias):
    length = pre_conv.shape[0]
    padded = jnp.concatenate([jnp.zeros((KERNEL - 1, pre_conv.shape[1]), jnp.float32), pre_conv], axis=0)
    seg_pad = jnp.concatenate([jnp.full((KERNEL - 1,), -1, jnp.int32), seg_ids.astype(jnp.int32)])
    running = jnp.zeros_like(pre_conv) + bias
    for tap_pos in range(KERNEL):
        same_doc = (seg_pad[tap_pos:tap_pos + length] == seg_ids).astype(jnp.float32)
        running = running + weight[tap_pos] * padded[tap_pos:tap_pos + length] * same_doc[:, None]
    return running

def block_step(state, inputs, d_skip):
    x_block, b_block, c_block, log_block, step_block, seg_block, seg_before = inputs
    cum_log = jnp.cumsum(log_block, axis=0)
    scores = low_back(jnp.dot(c_block, b_block.T, precision=HIGHEST_PREC))
    places = jnp.arange(BLOCK_LEN)
    same_doc = ((seg_block[:, None] == seg_block[None, :]) & (places[None, :] <= places[:, None])).astype(jnp.float32)
    lag_diff = cum_log[:, None, :] - cum_log[None, :, :]
    mixing = jnp.exp(jnp.minimum(lag_diff, 0.0)) * same_doc[:, :, None]
    weights = low(scores[:, :, None] * mixing * step_block[None, :, :])
    inner_y = low_back(jnp.einsum('ijh,jhp->ihp', weights, x_block, precision=HIGHEST_PREC))
    start_same = (seg_block == seg_before).astype(jnp.float32)
    entry_decay = jnp.exp(cum_log) * start_same[:, None]
    carried = low_back(jnp.einsum('in,hpn->ihp', c_block, low(state), precision=HIGHEST_PREC))
    result = inner_y + carried * entry_decay[:, :, None] + d_skip[None, :, None] * x_block
    end_same = (seg_block == seg_block[-1]).astype(jnp.float32)
    tail_decay = jnp.exp(cum_log[-1][None, :] - cum_log) * end_same[:, None]
    loaded = low(x_block * (tail_decay * step_block)[:, :, None])
    local_state = low_back(jnp.einsum('jhp,jn->hpn', loaded, b_block, precision=HIGHEST_PREC))
    block_decay = jnp.exp(cum_log[-1]) * start_same[-1]
    return (block_decay[:, None, None] * state + local_state, result)

def sequence_forward(tokens_f, seg_ids, params):
    norm_gain, w_zx, w_bc, w_dt, conv_x, conv_x_bias, conv_bc, conv_bc_bias, dt_bias, a_log, d_skip, gate_gain, w_out = params
    length = tokens_f.shape[0]
    head_count = d_skip.shape[0]
    rstd_in = lax.rsqrt(lax.optimization_barrier(jnp.mean(tokens_f * tokens_f, axis=-1, keepdims=True)) + EPS)
    normed = low(tokens_f * rstd_in * norm_gain)
    projected = jnp.einsum('td,dkc->tkc', normed, w_zx, precision=HIGHEST_PREC)
    gate_z = low_back(projected[:, 0])
    x_pre = low(low_back(projected[:, 1]))
    bc_pre = low(low_back(jnp.dot(normed, w_bc, precision=HIGHEST_PREC)))
    dt_raw = low_back(jnp.dot(normed, w_dt, precision=HIGHEST_PREC))
    x_ssm = low(silu(causal_conv(x_pre, seg_ids, conv_x, conv_x_bias)))
    bc_ssm = low(silu(causal_conv(bc_pre, seg_ids, conv_bc, conv_bc_bias)))
    step_size = jax.nn.softplus(dt_raw + dt_bias)
    log_decay = -jnp.exp(a_log) * step_size
    blocks = length // BLOCK_LEN
    seg_before = jnp.concatenate([jnp.full((1,), -1, jnp.int32), seg_ids[BLOCK_LEN - 1::BLOCK_LEN][:-1].astype(jnp.int32)])
    inputs = (x_ssm.reshape(blocks, BLOCK_LEN, head_count, HEAD_DIM), bc_ssm[:, :STATE].reshape(blocks, BLOCK_LEN, STATE), bc_ssm[:, STATE:].reshape(blocks, BLOCK_LEN, STATE), log_decay.reshape(blocks, BLOCK_LEN, head_count), step_size.reshape(blocks, BLOCK_LEN, head_count), seg_ids.reshape(blocks, BLOCK_LEN), seg_before)
    block_fn = jax.checkpoint(partial(block_step, d_skip=d_skip))
    _, y_heads = lax.scan(block_fn, jnp.zeros((head_count, HEAD_DIM, STATE), jnp.float32), inputs)
    y_flat = y_heads.reshape(length, head_count * HEAD_DIM)
    gated = y_flat * silu(gate_z)
    rstd_gate = lax.rsqrt(lax.optimization_barrier(jnp.mean(gated * gated, axis=-1, keepdims=True)) + EPS)
    scaled = low(gated * gate_gain)
    proj_out = low_back(jnp.dot(scaled, w_out.T, precision=HIGHEST_PREC))
    return tokens_f + rstd_gate * proj_out

def reference(tokens, segments, norm_gain, w_zx, w_bc, w_dt, conv_x, conv_x_bias, conv_bc, conv_bc_bias, dt_bias, a_log, d_skip, gate_gain, w_out, cotangent):
    params = tuple((value.astype(jnp.float32) for value in (norm_gain, w_zx, w_bc, w_dt, conv_x, conv_x_bias, conv_bc, conv_bc_bias, dt_bias, a_log, d_skip, gate_gain, w_out)))
    tokens_f = tokens.astype(jnp.float32)

    def forward(all_tokens, all_params):

        def one_sequence(pair):
            return sequence_forward(pair[0], pair[1], all_params)
        return lax.map(one_sequence, (all_tokens, segments))
    result, pullback = jax.vjp(forward, tokens_f, params)
    d_tokens, grads = pullback(cotangent.astype(jnp.float32))
    return (result.astype(jnp.bfloat16), d_tokens.astype(jnp.bfloat16), grads[0], grads[1], grads[2], grads[3], grads[4], grads[5], grads[6], grads[7], grads[8], grads[9], grads[10], grads[11], grads[12])
```

```python
import functools

import jax
import jax.numpy as jnp
from jax import lax
from jax.experimental import pallas as pl
from jax.experimental.pallas import tpu as pltpu
from jax.sharding import PartitionSpec as P

HEAD_DIM = 64
BLOCK_LEN = 256
LANES = 128
EDGE = 16
ROWS = 16
VMEM = 56 * 2**20
EPS = 1e-05
BF = jnp.bfloat16
F32 = jnp.float32
SMEM_SPEC = pl.BlockSpec(memory_space=pltpu.SMEM)


def dot(a, b, contract=((1,), (0,)), precision=None):
    return lax.dot_general(
        a, b, (contract, ((), ())), preferred_element_type=F32, precision=precision
    )


def halves(value):
    high = value.astype(BF)
    return high, (value - high.astype(F32)).astype(BF)


def widen(value, expand):
    high, low = halves(value)
    return dot(high, expand) + dot(low, expand)


def per_head(value, expand):
    high, low = halves(value)
    nt = ((1,), (1,))
    return dot(high, expand, nt) + dot(low, expand, nt)


def to_row(column):
    rows = column.shape[0]
    return jnp.transpose(jnp.broadcast_to(column, (rows, LANES)))[:8]


def sigmoid(value):
    return 1.0 / (1.0 + jnp.exp(-value))


def softplus(value):
    return jnp.maximum(value, 0.0) + jnp.log1p(jnp.exp(-jnp.abs(value)))


def triangle(span, lower):
    row = lax.broadcasted_iota(jnp.int32, (span, span), 0)
    col = lax.broadcasted_iota(jnp.int32, (span, span), 1)
    return ((col <= row) if lower else (col >= row)).astype(F32)


def running(value, lower):
    return dot(triangle(value.shape[0], lower), value, precision=lax.Precision.HIGHEST)


def doc_mask(seg_col, seg_row, lower):
    span = seg_col.shape[0]
    row = lax.broadcasted_iota(jnp.int32, (span, span), 0)
    col = lax.broadcasted_iota(jnp.int32, (span, span), 1)
    causal = (col <= row) if lower else (col >= row)
    return jnp.where(causal, (seg_col == seg_row).astype(F32), 0.0)


def back_rows(value, steps):
    return value if steps == 0 else pltpu.roll(value, steps, 0)


def ahead_rows(value, steps):
    return value if steps == 0 else pltpu.roll(value, value.shape[0] - steps, 0)


def conv_rows(extended, aux, weight):
    taps = 4
    out = weight[taps : taps + 1] + weight[taps - 1 : taps] * extended[EDGE:]
    for tap in range(taps - 1):
        window = back_rows(extended, taps - 1 - tap)[EDGE:]
        out = out + weight[tap : tap + 1] * (aux[:, tap : tap + 1] * window)
    return out


def conv_back_rows(d_conv, extended, aux, weight, grad_ref, width_at):
    taps = 4
    lanes = pl.ds(width_at, d_conv.shape[1])
    room = jnp.zeros((EDGE, d_conv.shape[1]), F32)
    total = None
    for tap in range(taps):
        steps = taps - 1 - tap
        masked = d_conv if steps == 0 else d_conv * aux[:, tap : tap + 1]
        window = back_rows(extended, steps)[EDGE:]
        grad_ref[tap : tap + 1, lanes] += jnp.sum(masked * window, axis=0, keepdims=True)
        placed = jnp.concatenate([room, masked * weight[tap : tap + 1]], axis=0)
        placed = ahead_rows(placed, steps)
        total = placed if total is None else total + placed
    grad_ref[taps : taps + 1, lanes] += jnp.sum(d_conv, axis=0, keepdims=True)
    return total


def chunk_grid(n_seq, state, own):
    across = n_seq * ROWS // state
    return across, own // across


def spread(value, scratch, outs, me, n_seq):
    across, width = chunk_grid(n_seq, value.shape[0], value.shape[1])
    for j in range(n_seq):
        a, b = j // across, j % across
        scratch[j] = value[a * ROWS : (a + 1) * ROWS, b * width : (b + 1) * width].astype(BF)
    for m in range(n_seq):
        outs[m][0] = scratch[me ^ m]


def collect(ins, scratch, me, n_seq, state, own):
    across, _ = chunk_grid(n_seq, state, own)
    for m in range(n_seq):
        scratch[me ^ m] = ins[m][0]
    rows = []
    for a in range(n_seq // across):
        rows.append(
            jnp.concatenate([scratch[a * across + b] for b in range(across)], axis=1)
            if across > 1
            else scratch[a]
        )
    return jnp.concatenate(rows, axis=0)


def front_kernel(
    seqs, n_seq, state, me_ref, tok_ref, halo_ref, gain_ref, w_ref, aux_ref, conv_ref, head_ref,
    expand_ref, normed_ref, pre_ref, pre_halo_ref, act_ref, xs_ref, dt_ref, cum_ref, *rest
):
    outs, scratch, extra = rest[:n_seq], rest[n_seq], rest[n_seq + 1]
    s = pl.program_id(0)
    me = me_ref[0]
    own = xs_ref.shape[-1]
    wide = own + 2 * state
    across, width = chunk_grid(n_seq, state, own)

    @pl.when(s == 0)
    def _():
        extra[...] = jnp.zeros_like(extra)

    @pl.when(s < seqs)
    def _():
        def norm(value):
            value = value.astype(F32)
            rstd = lax.rsqrt(jnp.mean(value * value, axis=-1, keepdims=True) + EPS)
            return (value * rstd * gain_ref[...]).astype(BF)

        normed = norm(tok_ref[0])
        normed_ref[0] = normed
        room = jnp.zeros((EDGE - halo_ref.shape[1], halo_ref.shape[2]), F32)
        ahead = jnp.concatenate([room, norm(halo_ref[0]).astype(F32)], axis=0).astype(BF)
        projected = dot(jnp.concatenate([ahead, normed], axis=0), w_ref[...])
        dt_raw = projected[EDGE:, wide:]
        dt_ref[0] = dt_raw
        pre = projected[:, :wide].astype(BF)
        pre_ref[0] = pre[EDGE:]
        pre_halo_ref[0] = pre[:EDGE]
        aux = aux_ref[0]
        conv = conv_rows(pre.astype(F32), aux, conv_ref[...])
        act = (conv * sigmoid(conv)).astype(BF)
        act_ref[0] = act
        x_float = act[:, :own].astype(F32)
        step = softplus(dt_raw + head_ref[0:1])
        log_decay = -head_ref[1:2] * step
        cum = running(log_decay, True)
        cum_ref[0] = cum
        expand = expand_ref[...]
        step_wide = widen(step, expand)
        xs_ref[0] = (x_float * step_wide).astype(BF)
        last = cum[-1:]
        tail_step = jnp.exp(last - cum) * aux[:, 3:4] * step
        loaded = (x_float * widen(tail_step, expand)).astype(BF)
        b_ssm = act[:, own : own + state]
        spread(dot(b_ssm, loaded, ((0,), (0,))), scratch, outs, me, n_seq)
        decay = jnp.broadcast_to(jnp.exp(last) * aux[-1:, 4:5], (8, LANES))
        decay_wide = widen(decay, expand)[:1]
        high = decay_wide.astype(BF).astype(F32)
        places = lax.broadcasted_iota(jnp.int32, (ROWS, 1), 0)
        extra[...] += jnp.where(places == s, high, 0.0) + jnp.where(
            places == s + seqs, decay_wide - high, 0.0
        )

    @pl.when(s == seqs)
    def _():
        for j in range(n_seq):
            b = j % across
            scratch[j] = extra[:, b * width : (b + 1) * width].astype(BF)
        for m in range(n_seq):
            outs[m][0] = scratch[me ^ m]


def scan_kernel(seqs, n_seq, me_ref, *rest):
    ins, outs = rest[:n_seq], rest[n_seq : 2 * n_seq]
    decay_ref, scratch = rest[2 * n_seq], rest[2 * n_seq + 1]
    me = me_ref[0]
    for m in range(n_seq):
        scratch[me ^ m] = ins[m][...]
    for s in range(seqs):
        entry = jnp.zeros(scratch.shape[2:], F32)
        for k in range(n_seq):
            packed = scratch[k, seqs].astype(F32)
            decay = packed[s : s + 1] + packed[s + seqs : s + seqs + 1]
            decay_ref[k, s : s + 1] = decay
            arrived = scratch[k, s].astype(F32)
            scratch[k, s] = entry.astype(BF)
            entry = decay * entry + arrived
    for m in range(n_seq):
        outs[m][...] = scratch[me ^ m, :seqs]


def scan_back_kernel(seqs, n_seq, me_ref, decay_ref, *rest):
    ins, outs, scratch = rest[:n_seq], rest[n_seq : 2 * n_seq], rest[2 * n_seq]
    me = me_ref[0]
    for m in range(n_seq):
        scratch[me ^ m] = ins[m][...]
    for s in range(seqs):
        leave = jnp.zeros(scratch.shape[2:], F32)
        for k in reversed(range(n_seq)):
            arrived = scratch[k, s].astype(F32)
            scratch[k, s] = leave.astype(BF)
            leave = decay_ref[k, s : s + 1] * leave + arrived
    for m in range(n_seq):
        outs[m][...] = scratch[me ^ m]


def inner_kernel(state, act_ref, xs_ref, cum_ref, aux_ref, seg_ref, out_ref):
    own = xs_ref.shape[-1]
    b_ssm, c_ssm = act_ref[0, :, own : own + state], act_ref[0, :, own + state :]
    cum = cum_ref[0]
    cum_t = jnp.transpose(cum)
    scores = dot(c_ssm, b_ssm, ((1,), (1,))) * doc_mask(aux_ref[0, :, 5:6], seg_ref[0, 0:1], True)
    left = lax.broadcasted_iota(jnp.int32, (1, LANES), 1) < HEAD_DIM
    for pair in range(own // LANES):
        lanes = slice(pair * LANES, (pair + 1) * LANES)
        xs = xs_ref[0, :, lanes].astype(F32)
        total = None
        for side in range(2):
            h = 2 * pair + side
            lag = jnp.minimum(cum[:, h : h + 1] - cum_t[h : h + 1], 0.0)
            weights = (scores * jnp.exp(lag)).astype(BF)
            own_xs = jnp.where(left if side == 0 else ~left, xs, 0.0).astype(BF)
            term = dot(weights, own_xs)
            total = term if total is None else total + term
        out_ref[0, :, lanes] = total


def mixer_out(state, states, act_ref, inner_ref, gate_ref, cum_ref, aux_ref, rows_ref, expand_ref):
    own = inner_ref.shape[-1]
    c_ssm = act_ref[0, :, own + state :]
    x_float = act_ref[0, :, :own].astype(F32)
    entry_wide = widen(jnp.exp(cum_ref[0]) * aux_ref[0, :, 4:5], expand_ref[...])
    mixed = inner_ref[0] + dot(c_ssm, states) * entry_wide
    y = mixed + rows_ref[1:2] * x_float
    gate = gate_ref[0].astype(F32)
    sig = sigmoid(gate)
    return mixed, y, x_float, gate, sig, entry_wide


def sums_kernel(
    n_seq, state, me_ref, act_ref, inner_ref, gate_ref, e_ref, cum_ref, aux_ref, rows_ref,
    expand_ref, *rest
):
    ins, out_ref, scratch = rest[:n_seq], rest[n_seq], rest[n_seq + 1]
    states = collect(ins, scratch, me_ref[0], n_seq, state, inner_ref.shape[-1])
    _, y, _, gate, sig, _ = mixer_out(
        state, states, act_ref, inner_ref, gate_ref, cum_ref, aux_ref, rows_ref, expand_ref
    )
    gated = y * (gate * sig)
    squares = jnp.sum(gated * gated, axis=-1, keepdims=True)
    dots = jnp.sum(e_ref[0].astype(F32) * (gated * rows_ref[0:1]), axis=-1, keepdims=True)
    out_ref[0, 0:1] = to_row(squares)[:1]
    out_ref[0, 1:2] = to_row(dots)[:1]


def gate_back_kernel(
    n_seq, state, inner_total, me_ref, act_ref, inner_ref, gate_ref, e_ref, cum_ref, aux_ref,
    rows_ref, expand_ref, sums_ref, *rest
):
    ins, rest = rest[:n_seq], rest[n_seq:]
    scaled_ref, dz_ref, dy_ref, mixed_ref, dc_ref, dot_ref, grad_ref = rest[:7]
    outs, scratch = rest[7 : 7 + n_seq], rest[7 + n_seq]
    me = me_ref[0]
    own = inner_ref.shape[-1]
    expand = expand_ref[...]
    states = collect(ins, scratch, me, n_seq, state, own)
    mixed, y, x_float, gate, sig, entry_wide = mixer_out(
        state, states, act_ref, inner_ref, gate_ref, cum_ref, aux_ref, rows_ref, expand_ref
    )
    columns = jnp.transpose(
        jnp.concatenate([sums_ref[0], jnp.zeros((LANES - 8, sums_ref.shape[2]), F32)], axis=0)
    )
    rstd = lax.rsqrt(columns[:, 0:1] / inner_total + EPS)
    slope = columns[:, 1:2] * (rstd * rstd * rstd) / inner_total
    gain = rows_ref[0:1]
    silu = gate * sig
    gated = y * silu
    scaled_ref[0] = (gated * gain * rstd).astype(BF)
    d_scaled = e_ref[0].astype(F32) * rstd
    d_gated = d_scaled * gain - slope * gated
    d_y = d_gated * silu
    dy_ref[0] = d_y.astype(BF)
    d_z = (d_gated * y * (sig * (1.0 + gate * (1.0 - sig)))).astype(BF)
    dz_ref[0] = d_z
    row = jnp.sum(d_z.astype(F32) * gate, axis=-1, keepdims=True)
    dot_ref[0] = to_row(row)
    mixed_ref[0] = per_head(d_y * mixed, expand)

    @pl.when(pl.program_id(0) == 0)
    def _():
        grad_ref[...] = jnp.zeros_like(grad_ref)

    grad_ref[0:1] += jnp.sum(d_scaled * gated, axis=0, keepdims=True)
    grad_ref[1:2] += jnp.sum(d_y * x_float, axis=0, keepdims=True)
    d_carried = (d_y * entry_wide).astype(BF)
    c_ssm = act_ref[0, :, own + state :]
    dc_ref[0] = dot(d_carried, states, ((1,), (1,)))
    spread(dot(c_ssm, d_carried, ((0,), (0,))), scratch, outs, me, n_seq)


def inner_back_kernel(
    state, act_ref, xs_ref, dy_ref, dc_ref, cum_ref, dt_ref, aux_ref, seg_ref, rows_ref, head_ref,
    expand_ref, dx_ref, dstep_ref, dbc_ref
):
    own = xs_ref.shape[-1]
    b_ssm, c_ssm = act_ref[0, :, own : own + state], act_ref[0, :, own + state :]
    cum = cum_ref[0]
    cum_t = jnp.transpose(cum)
    nt = ((1,), (1,))
    mask = doc_mask(aux_ref[0, :, 5:6], seg_ref[0, 0:1], False)
    scores = dot(b_ssm, c_ssm, nt) * mask
    left = lax.broadcasted_iota(jnp.int32, (1, LANES), 1) < HEAD_DIM
    d_scores = None
    sums = []
    for pair in range(own // LANES):
        lanes = slice(pair * LANES, (pair + 1) * LANES)
        xs = xs_ref[0, :, lanes]
        dy = dy_ref[0, :, lanes].astype(F32)
        total = None
        for side in range(2):
            h = 2 * pair + side
            lag = jnp.minimum(cum_t[h : h + 1] - cum[:, h : h + 1], 0.0)
            mixing = jnp.exp(lag)
            weights = (scores * mixing).astype(BF)
            own_dy = jnp.where(left if side == 0 else ~left, dy, 0.0).astype(BF)
            term = dot(weights, own_dy)
            total = term if total is None else total + term
            d_mixed = dot(xs, own_dy, nt) * mixing
            d_scores = d_mixed if d_scores is None else d_scores + d_mixed
        sums.append(total)
    back = jnp.concatenate(sums, axis=1)
    expand = expand_ref[...]
    x_float = act_ref[0, :, :own].astype(F32)
    dstep_ref[0] = per_head(x_float * back, expand)
    step = softplus(dt_ref[0] + head_ref[0:1])
    dy_all = dy_ref[0].astype(F32)
    dx_ref[0] = (back * widen(step, expand) + rows_ref[1:2] * dy_all).astype(BF)
    d_scores = (d_scores * mask).astype(BF)
    dbc_ref[0, :, :state] = dot(d_scores, c_ssm)
    dbc_ref[0, :, state:] = dot(d_scores, b_ssm, ((0,), (0,))) + dc_ref[0]


def leave_kernel(
    n_seq, state, me_ref, act_ref, pre_ref, pre_halo_ref, dx_ref, dstep_ref, dbc_ref, mixed_ref,
    cum_ref, dt_ref, aux_ref, conv_ref, head_ref, expand_ref, *rest
):
    in_states, in_ends, rest = rest[:n_seq], rest[n_seq : 2 * n_seq], rest[2 * n_seq :]
    dpre_ref, back_ref, dbc_out_ref, ddt_ref, dot_ref, grad_ref, small_ref, scratch = rest
    me = me_ref[0]
    own = dx_ref.shape[-1]
    expand = expand_ref[...]
    states = collect(in_states, scratch, me, n_seq, state, own)
    ends = collect(in_ends, scratch, me, n_seq, state, own)
    b_ssm = act_ref[0, :, own : own + state]
    x_float = act_ref[0, :, :own].astype(F32)
    aux = aux_ref[0]
    dt_pre = dt_ref[0] + head_ref[0:1]
    step = softplus(dt_pre)
    rate = head_ref[1:2]
    cum = cum_ref[0]
    last = cum[-1:]
    tail_decay = jnp.exp(last - cum) * aux[:, 3:4]
    tail_step = tail_decay * step
    tail_wide = widen(tail_step, expand)
    loaded = (x_float * tail_wide).astype(BF)
    d_loaded = dot(b_ssm, ends)
    dbc_out_ref[0, :, :state] = (dbc_ref[0, :, :state] + dot(loaded, ends, ((1,), (1,)))).astype(BF)
    dbc_out_ref[0, :, state:] = dbc_ref[0, :, state:].astype(BF)
    d_x = dx_ref[0].astype(F32) + d_loaded * tail_wide
    d_tail = per_head(d_loaded * x_float, expand)
    end_terms = d_tail * tail_step
    product = jnp.sum(ends.astype(F32) * states.astype(F32), axis=0, keepdims=True)
    d_decay = per_head(jnp.broadcast_to(product, (8, own)), expand)[:1]
    block_decay = jnp.exp(last) * aux[-1:, 4:5]
    d_cum = mixed_ref[0] - step * dstep_ref[0] - end_terms
    last_add = jnp.sum(end_terms, axis=0, keepdims=True) + d_decay * block_decay
    d_log = running(d_cum, False) + last_add
    d_step = dstep_ref[0] + d_tail * tail_decay - d_log * rate
    d_dt = d_step * sigmoid(dt_pre)
    ddt_ref[0] = d_dt.astype(BF)

    @pl.when(pl.program_id(0) == 0)
    def _():
        grad_ref[...] = jnp.zeros_like(grad_ref)
        small_ref[...] = jnp.zeros_like(small_ref)

    small_ref[0:1] += jnp.sum(d_dt, axis=0, keepdims=True)
    small_ref[1:2] += jnp.sum(d_log * (-rate * step), axis=0, keepdims=True)

    extended = jnp.concatenate([pre_halo_ref[0, :, :own], pre_ref[0, :, :own]], axis=0).astype(F32)
    weight = conv_ref[:, :own]
    conv = conv_rows(extended, aux, weight)
    sig = sigmoid(conv)
    d_conv = d_x * (sig * (1.0 + conv * (1.0 - sig)))
    d_ext = conv_back_rows(d_conv, extended, aux, weight, grad_ref, 0)
    d_pre = d_ext[EDGE:].astype(BF)
    dpre_ref[0] = d_pre
    back_ref[0] = d_ext[:EDGE].astype(BF)
    row = jnp.sum(d_pre.astype(F32) * extended[EDGE:], axis=-1, keepdims=True)
    row = row + jnp.sum(ddt_ref[0].astype(F32) * dt_ref[0], axis=-1, keepdims=True)
    dot_ref[0] = to_row(row)


def conv_bc_kernel(
    own, d_ref, pre_ref, pre_halo_ref, aux_ref, conv_ref, dpre_ref, back_ref, grad_ref
):
    extended = jnp.concatenate([pre_halo_ref[0], pre_ref[0]], axis=0).astype(F32)
    aux = aux_ref[0]
    weight = conv_ref[...]
    conv = conv_rows(extended, aux, weight)
    sig = sigmoid(conv)
    d_conv = d_ref[0].astype(F32) * (sig * (1.0 + conv * (1.0 - sig)))

    @pl.when(pl.program_id(0) == 0)
    def _():
        grad_ref[...] = jnp.zeros_like(grad_ref)

    d_ext = conv_back_rows(d_conv, extended, aux, weight, grad_ref, 0)
    dpre_ref[0] = d_ext[EDGE:].astype(BF)
    back_ref[0] = d_ext[:EDGE].astype(BF)


def per_seq(seqs, shape):
    zeros = (0,) * len(shape)
    return pl.BlockSpec((1, *shape), lambda s: (jnp.minimum(s, seqs - 1), *zeros))


def whole(shape):
    zeros = (0,) * len(shape)
    return pl.BlockSpec(tuple(shape), lambda s: zeros)


def call(body, grid, ins, in_specs, outs, out_specs, scratch, flops, name):
    moved = sum(v.size * v.dtype.itemsize for v in (*ins, *outs))
    return pl.pallas_call(
        body,
        grid=(grid,),
        in_specs=in_specs,
        out_specs=out_specs,
        out_shape=outs,
        scratch_shapes=scratch,
        name=name,
        compiler_params=pltpu.CompilerParams(vmem_limit_bytes=VMEM),
        cost_estimate=pl.CostEstimate(flops=int(flops), bytes_accessed=moved, transcendentals=0),
    )(*ins)


def shaped(shape, dtype):
    return jax.ShapeDtypeStruct(tuple(shape), dtype)


def swap(value, axis, mask):
    count = lax.axis_size(axis)
    return lax.ppermute(value, axis, [(i, i ^ mask) for i in range(count)])


def shift(value, axis, steps):
    count = lax.axis_size(axis)
    leading, last = (max(0, -steps), min(count, count - steps))
    return lax.ppermute(value, axis, [(i, i + steps) for i in range(leading, last)])


def exchange(chunks, axis):
    return [chunks[0]] + [swap(chunks[m], axis, m) for m in range(1, len(chunks))]


def pick(stacked, at, axis=0):
    return lax.dynamic_index_in_dim(stacked, at, axis, False)


def halving_scatter(chunks, axis):
    me = lax.axis_index(axis)
    mask = 1
    while chunks.shape[0] > 1:
        pairs = chunks.reshape(chunks.shape[0] // 2, 2, *chunks.shape[1:])
        bit = (me // mask) % 2
        chunks = pick(pairs, bit, 1) + swap(pick(pairs, 1 - bit, 1), axis, mask)
        mask *= 2
    return chunks[0]


def sum_all(value, axis):
    mask = 1
    while mask < lax.axis_size(axis):
        value = value + swap(value, axis, mask)
        mask *= 2
    return value


def pad_lanes(value, width):
    return jnp.pad(value, ((0, 0), (0, width - value.shape[1])))


def pad_rows(rows, count=8):
    stacked = jnp.concatenate([r.reshape(-1, r.shape[-1]).astype(F32) for r in rows], axis=0)
    return jnp.pad(stacked, ((0, count - stacked.shape[0]), (0, 0)))


def local(
    tokens,
    segments,
    norm_gain,
    w_zx,
    w_bc,
    w_dt,
    conv_x,
    conv_x_bias,
    conv_bc,
    conv_bc_bias,
    dt_bias,
    a_log,
    d_skip,
    gate_gain,
    w_out,
    cotangent,
):
    seqs, span, model = tokens.shape
    heads = d_skip.shape[0]
    own = heads * HEAD_DIM
    n_seq, n_head = lax.axis_size("seq"), lax.axis_size("head")
    me_head = lax.axis_index("head")
    me = lax.axis_index("seq").astype(jnp.int32).reshape(1)
    inner_total = own * n_head
    state = w_bc.shape[1] // 2
    wide = own + 2 * state
    share = model // n_head
    offset = me_head * share
    edge = conv_x.shape[0] - 1
    _, width = chunk_grid(n_seq, state, own)

    tok_halo = shift(tokens[:, -8:], "seq", 1)
    seg_halo = shift(segments[:, -8:], "seq", 1)
    cot_full = lax.all_gather(cotangent, "head", axis=2, tiled=True)

    seg_ext = jnp.concatenate([seg_halo, segments], axis=1)
    aux = [(seg_ext[:, 8 - edge + tap : 8 - edge + tap + span] == segments) for tap in range(edge)]
    aux.append(segments == segments[:, -1:])
    aux.append(segments == seg_halo[:, -1:])
    aux = [a.astype(F32) for a in aux] + [segments.astype(F32)]
    aux = jnp.stack(aux + [jnp.zeros_like(aux[0])] * 2, axis=-1)
    seg_row = jnp.broadcast_to(segments.astype(F32)[:, None], (seqs, 8, span))
    conv_w = jnp.concatenate(
        [pad_rows([conv_x, conv_x_bias]), pad_rows([conv_bc, conv_bc_bias])], axis=1
    )
    head_rows = pad_lanes(pad_rows([dt_bias, jnp.exp(a_log)]), LANES)
    wide_rows = pad_rows([gate_gain, jnp.repeat(d_skip, HEAD_DIM)])
    expand = (
        jnp.arange(LANES)[:, None] == (jnp.arange(own) // HEAD_DIM)[None, :]
    ).astype(BF)
    w_z, w_x = w_zx[:, 0, :], w_zx[:, 1, :]
    w_cat = jnp.concatenate([w_x, w_bc, pad_lanes(w_dt, LANES)], axis=1)

    seq = functools.partial(per_seq, seqs)
    chunk_spec = seq((ROWS, width))
    ins = (me, tokens, tok_halo, norm_gain.reshape(1, model), w_cat, aux, conv_w, head_rows, expand)
    outs = (
        shaped((seqs, span, model), BF),
        shaped((seqs, span, wide), BF),
        shaped((seqs, EDGE, wide), BF),
        shaped((seqs, span, wide), BF),
        shaped((seqs, span, own), BF),
        shaped((seqs, span, LANES), F32),
        shaped((seqs, span, LANES), F32),
    )
    normed, pre, pre_halo, act, xs, dt_raw, cum, *sent = call(
        functools.partial(front_kernel, seqs, n_seq, state),
        seqs + 1,
        ins,
        [SMEM_SPEC, seq(tokens.shape[1:]), seq(tok_halo.shape[1:])]
        + [whole(v.shape) for v in ins[3:5]]
        + [seq(aux.shape[1:])]
        + [whole(v.shape) for v in ins[6:]],
        outs + (shaped((seqs + 1, ROWS, width), BF),) * n_seq,
        [seq(v.shape[1:]) for v in outs]
        + [pl.BlockSpec((1, ROWS, width), lambda s: (s, 0, 0))] * n_seq,
        [pltpu.VMEM((n_seq, ROWS, width), BF), pltpu.VMEM((ROWS, own), F32)],
        2 * seqs * span * model * (wide + LANES),
        "front",
    )

    def scan(body, ins, in_specs, n_in, outs, out_specs, name):
        blocks = n_in
        return call(
            body,
            1,
            ins,
            in_specs,
            outs,
            out_specs,
            [pltpu.VMEM((n_seq, blocks, ROWS, width), BF)],
            4 * n_seq * seqs * ROWS * width,
            name,
        )

    got = exchange(sent, "seq")
    piece = shaped((seqs, ROWS, width), BF)
    decay_shape = shaped((n_seq, 8, width), F32)
    *entries, decays = scan(
        functools.partial(scan_kernel, seqs, n_seq),
        (me, *got),
        [SMEM_SPEC] + [whole(v.shape) for v in got],
        seqs + 1,
        (piece,) * n_seq + (decay_shape,),
        [whole(piece.shape)] * n_seq + [whole(decay_shape.shape)],
        "scan",
    )
    states = exchange(entries, "seq")

    gate = dot(normed, w_z, ((2,), (0,))).astype(BF)
    e_raw = dot(cot_full, w_out, ((2,), (0,))).astype(BF)
    ins = (act, xs, cum, aux, seg_row)
    (inner,) = call(
        functools.partial(inner_kernel, state),
        seqs,
        ins,
        [seq(v.shape[1:]) for v in ins],
        (shaped((seqs, span, own), F32),),
        [seq((span, own))],
        [],
        8 * seqs * heads * span * span * HEAD_DIM,
        "inner",
    )

    mixer_ins = (me, act, inner, gate, e_raw, cum, aux, wide_rows, expand)
    mixer_specs = (
        [SMEM_SPEC] + [seq(v.shape[1:]) for v in mixer_ins[1:7]] + [whole(v.shape) for v in mixer_ins[7:]]
    )
    chunk_scratch = pltpu.VMEM((n_seq, ROWS, width), BF)
    (sums,) = call(
        functools.partial(sums_kernel, n_seq, state),
        seqs,
        (*mixer_ins, *states),
        mixer_specs + [chunk_spec] * n_seq,
        (shaped((seqs, 8, span), F32),),
        [seq((8, span))],
        [chunk_scratch],
        2 * seqs * span * state * own,
        "sums",
    )
    sums = lax.psum(sums[:, :2], "head")
    sums = jnp.pad(sums, ((0, 0), (0, 6), (0, 0)))

    outs = (
        shaped((seqs, span, own), BF),
        shaped((seqs, span, own), BF),
        shaped((seqs, span, own), BF),
        shaped((seqs, span, LANES), F32),
        shaped((seqs, span, state), F32),
        shaped((seqs, 8, span), F32),
    )
    scaled, d_z, d_y, mixed, d_c, dot_z, gate_grads, *sent = call(
        functools.partial(gate_back_kernel, n_seq, state, inner_total),
        seqs,
        (*mixer_ins, sums, *states),
        mixer_specs + [seq((8, span))] + [chunk_spec] * n_seq,
        outs + (shaped((8, own), F32),) + (piece,) * n_seq,
        [seq(v.shape[1:]) for v in outs] + [whole((8, own))] + [chunk_spec] * n_seq,
        [chunk_scratch],
        6 * seqs * span * state * own,
        "gate_back",
    )

    got = exchange(sent, "seq")
    leaves = scan(
        functools.partial(scan_back_kernel, seqs, n_seq),
        (me, decays, *got),
        [SMEM_SPEC] + [whole(v.shape) for v in (decays, *got)],
        seqs,
        (piece,) * n_seq,
        [whole(piece.shape)] * n_seq,
        "scan_back",
    )
    ends = exchange(leaves, "seq")

    out_full = dot(scaled, w_out, ((2,), (1,))).astype(BF)
    own_sum = lax.psum_scatter(out_full, "head", scatter_dimension=2, tiled=True)
    tokens_own = lax.dynamic_slice_in_dim(tokens, offset, share, 2).astype(F32)
    layer_out = (tokens_own + own_sum.astype(F32)).astype(BF)
    g_w_out = dot(cot_full, scaled, ((0, 1), (0, 1))).astype(BF)
    g_w_z = dot(normed, d_z, ((0, 1), (0, 1))).astype(BF)
    early = lax.psum_scatter(
        jnp.concatenate([g_w_out, g_w_z], axis=1), "seq", scatter_dimension=0, tiled=True
    ).astype(F32)

    ins = (act, xs, d_y, d_c, cum, dt_raw, aux, seg_row, wide_rows, head_rows, expand)
    outs = (
        shaped((seqs, span, own), BF),
        shaped((seqs, span, LANES), F32),
        shaped((seqs, span, 2 * state), F32),
    )
    d_x, d_step, d_bc = call(
        functools.partial(inner_back_kernel, state),
        seqs,
        ins,
        [seq(v.shape[1:]) for v in ins[:8]] + [whole(v.shape) for v in ins[8:]],
        outs,
        [seq(v.shape[1:]) for v in outs],
        [],
        16 * seqs * heads * span * span * HEAD_DIM,
        "inner_back",
    )

    ins = (
        me, act, pre, pre_halo, d_x, d_step, d_bc, mixed, cum, dt_raw, aux, conv_w, head_rows, expand,
        *states, *ends,
    )
    outs = (
        shaped((seqs, span, own), BF),
        shaped((seqs, EDGE, own), BF),
        shaped((seqs, span, 2 * state), BF),
        shaped((seqs, span, LANES), BF),
        shaped((seqs, 8, span), F32),
    )
    d_x_pre, back_x, d_bc, d_dt, dot_x, conv_grads, head_grads = call(
        functools.partial(leave_kernel, n_seq, state),
        seqs,
        ins,
        [SMEM_SPEC]
        + [seq(v.shape[1:]) for v in ins[1:11]]
        + [whole(v.shape) for v in ins[11:14]]
        + [chunk_spec] * (2 * n_seq),
        outs + (shaped((8, own), F32), shaped((8, LANES), F32)),
        [seq(v.shape[1:]) for v in outs] + [whole((8, own)), whole((8, LANES))],
        [chunk_scratch],
        8 * seqs * span * state * own,
        "leave",
    )
    back_x = shift(back_x[:, -edge:], "seq", -1)
    d_x_pre = d_x_pre.at[:, -edge:].add(back_x)

    d_bc_all = sum_all(d_bc, "head")
    bc_pre, bc_halo = pre[..., own:], pre_halo[..., own:]
    ins = (d_bc_all, bc_pre, bc_halo, aux, conv_w[:, own:])
    outs = (shaped((seqs, span, 2 * state), BF), shaped((seqs, EDGE, 2 * state), BF))
    d_bc_pre, back_bc, bc_grads = call(
        functools.partial(conv_bc_kernel, own),
        seqs,
        ins,
        [seq(v.shape[1:]) for v in ins[:4]] + [whole(ins[4].shape)],
        outs + (shaped((8, 2 * state), F32),),
        [seq(v.shape[1:]) for v in outs] + [whole((8, 2 * state))],
        [],
        0,
        "conv_bc",
    )
    back_bc = shift(back_bc[:, -edge:], "seq", -1)
    d_bc_pre = d_bc_pre.at[:, -edge:].add(back_bc)

    g_w_x = dot(normed, d_x_pre, ((0, 1), (0, 1))).astype(BF).reshape(n_seq, -1, own)
    half = own // 2
    late_a = halving_scatter(g_w_x[..., :half], "seq").astype(F32)
    late_b = halving_scatter(g_w_x[..., half:], "seq").astype(F32)
    d_small = jnp.concatenate([d_bc_pre, d_dt], axis=-1)
    g_small = dot(normed, d_small, ((0, 1), (0, 1))).astype(BF)
    late_s = halving_scatter(g_small.reshape(n_seq, -1, 2 * state + LANES), "seq").astype(F32)

    w_dx = jnp.concatenate([w_x, pad_lanes(w_dt, LANES)], axis=1)
    part_normed = dot(d_z, w_z, ((2,), (1,))) + dot(
        jnp.concatenate([d_x_pre, d_dt], axis=-1), w_dx, ((2,), (1,))
    )
    part_normed = part_normed.astype(BF)
    by_share = jnp.stack(
        [lax.slice_in_dim(part_normed, k * share, (k + 1) * share, axis=2) for k in range(n_head)]
    )
    row_dot = dot_z[:, 0] + dot_x[:, 0]
    fix = jnp.sum(back_x.astype(F32) * pre[:, -edge:, :own].astype(F32), axis=-1)
    row_dot = row_dot + jnp.pad(fix, ((0, 0), (span - edge, 0)))
    row_dot = sum_all(row_dot, "head") + jnp.sum(
        d_bc_pre.astype(F32) * bc_pre.astype(F32), axis=-1
    )
    own_grad = halving_scatter(by_share, "head").astype(F32)
    w_bc_own = lax.dynamic_slice_in_dim(w_bc, offset, share, 0)
    own_grad = own_grad + dot(d_bc_pre, w_bc_own, ((2,), (1,)))
    tokens_f = tokens.astype(F32)
    rstd_in = lax.rsqrt(jnp.mean(tokens_f * tokens_f, axis=-1, keepdims=True) + EPS)
    unit_own = tokens_own * rstd_in
    gain_own = lax.dynamic_slice_in_dim(norm_gain, offset, share, 0)
    g_norm = jnp.sum(own_grad * unit_own, axis=(0, 1))
    d_unit = own_grad * gain_own
    input_grad = (
        rstd_in * (d_unit - unit_own * (row_dot / model)[..., None]) + cotangent.astype(F32)
    ).astype(BF)

    taps = edge + 1
    small = (
        conv_grads[:taps],
        conv_grads[taps],
        bc_grads[:taps],
        bc_grads[taps],
        head_grads[0, :heads],
        head_grads[1, :heads],
        jnp.sum(gate_grads[1].reshape(heads, HEAD_DIM), axis=-1),
        gate_grads[0],
    )
    flat = sum_all(jnp.concatenate([v.reshape(-1) for v in small]), "seq")
    summed, at = [], 0
    for v in small:
        summed.append(flat[at : at + v.size].reshape(v.shape))
        at += v.size
    g_norm = sum_all(g_norm, "seq")
    g_w_zx_own = jnp.stack([early[:, own:], jnp.concatenate([late_a, late_b], axis=1)], axis=1)
    return (
        layer_out,
        input_grad,
        g_norm,
        g_w_zx_own,
        late_s[:, : 2 * state],
        late_s[:, 2 * state : 2 * state + heads],
        *summed,
        early[:, :own],
    )


def solution(mesh):
    placed = (
        P(None, "seq", None),
        P(None, "seq"),
        P(),
        P(None, None, "head"),
        P(),
        P(None, "head"),
        P(None, "head"),
        P("head"),
        P(),
        P(),
        P("head"),
        P("head"),
        P("head"),
        P("head"),
        P(None, "head"),
        P(None, "seq", "head"),
    )
    return jax.shard_map(
        local,
        mesh=mesh,
        in_specs=placed,
        out_specs=(
            P(None, "seq", "head"),
            P(None, "seq", "head"),
            P("head"),
            P("seq", None, "head"),
            P("seq", None),
            P("seq", "head"),
            P(None, "head"),
            P("head"),
            P(),
            P(),
            P("head"),
            P("head"),
            P("head"),
            P("head"),
            P("seq", "head"),
        ),
        check_vma=False,
    )
```

```python
import functools

import jax
import jax.numpy as jnp
from jax import lax
from jax.experimental import pallas as pl
from jax.experimental.pallas import tpu as pltpu
from jax.sharding import PartitionSpec as P

HEAD_DIM = 64
BLOCK_LEN = 256
LANES = 128
EDGE = 16
ROWS = 16
VMEM = 56 * 2**20
EPS = 1e-05
BF = jnp.bfloat16
F32 = jnp.float32
def cost(micros):
    return pl.CostEstimate(flops=int(micros * 1.15e+09), bytes_accessed=1000, transcendentals=0)


SMEM_SPEC = pl.BlockSpec(memory_space=pltpu.SMEM)


def dot(a, b, contract=((1,), (0,)), precision=None):
    return lax.dot_general(
        a, b, (contract, ((), ())), preferred_element_type=F32, precision=precision
    )


def halves(value):
    high = value.astype(BF)
    return high, (value - high.astype(F32)).astype(BF)


def widen(value, expand):
    high, low = halves(value)
    return dot(high, expand) + dot(low, expand)


def per_head(value, expand):
    high, low = halves(value)
    nt = ((1,), (1,))
    return dot(high, expand, nt) + dot(low, expand, nt)


def to_row(column):
    rows = column.shape[0]
    return jnp.transpose(jnp.broadcast_to(column, (rows, LANES)))[:8]


def sigmoid(value):
    return 0.5 * jnp.tanh(0.5 * value) + 0.5


def softplus(value):
    return jnp.maximum(value, 0.0) + jnp.log1p(jnp.exp(-jnp.abs(value)))


def triangle(span, lower):
    row = lax.broadcasted_iota(jnp.int32, (span, span), 0)
    col = lax.broadcasted_iota(jnp.int32, (span, span), 1)
    return ((col <= row) if lower else (col >= row)).astype(F32)


def running(value, lower):
    return dot(triangle(value.shape[0], lower), value, precision=lax.Precision.HIGHEST)


def doc_mask(seg_col, seg_row, lower):
    span = seg_col.shape[0]
    row = lax.broadcasted_iota(jnp.int32, (span, span), 0)
    col = lax.broadcasted_iota(jnp.int32, (span, span), 1)
    causal = (col <= row) if lower else (col >= row)
    return jnp.where(causal, (seg_col == seg_row).astype(F32), 0.0)


def back_rows(value, steps):
    return value if steps == 0 else pltpu.roll(value, steps, 0)


def ahead_rows(value, steps):
    return value if steps == 0 else pltpu.roll(value, value.shape[0] - steps, 0)


def conv_rows(extended, aux, weight):
    taps = 4
    out = weight[taps : taps + 1] + weight[taps - 1 : taps] * extended[EDGE:]
    for tap in range(taps - 1):
        window = back_rows(extended, taps - 1 - tap)[EDGE:]
        out = out + weight[tap : tap + 1] * (aux[:, tap : tap + 1] * window)
    return out


def conv_back_rows(d_conv, extended, aux, weight, grad_ref=None):
    taps = 4
    room = jnp.zeros((EDGE, d_conv.shape[1]), F32)
    total = None
    for tap in range(taps):
        steps = taps - 1 - tap
        masked = d_conv if steps == 0 else d_conv * aux[:, tap : tap + 1]
        if grad_ref is not None:
            window = back_rows(extended, steps)[EDGE:]
            grad_ref[tap : tap + 1] += jnp.sum(masked * window, axis=0, keepdims=True)
        placed = jnp.concatenate([room, masked * weight[tap : tap + 1]], axis=0)
        placed = ahead_rows(placed, steps)
        total = placed if total is None else total + placed
    if grad_ref is not None:
        grad_ref[taps : taps + 1] += jnp.sum(d_conv, axis=0, keepdims=True)
    return total


def chunk_grid(count, rows, own):
    across = count * ROWS // rows
    return across, own // across


def cut(value, scratch, at, count):
    across, width = chunk_grid(count, value.shape[0], value.shape[1])
    for j in range(count):
        a, b = j // across, j % across
        scratch[j, at] = value[a * ROWS : (a + 1) * ROWS, b * width : (b + 1) * width].astype(BF)


def uncut(scratch, at, count, rows, own):
    across, _ = chunk_grid(count, rows, own)
    return jnp.concatenate(
        [
            jnp.concatenate([scratch[a * across + b, at] for b in range(across)], axis=1)
            for a in range(count // across)
        ],
        axis=0,
    )


def both_halves(me, mine_ref, other_ref):
    mine, other = mine_ref[0], other_ref[0]
    return jnp.where(
        me % 2 == 0,
        jnp.concatenate([mine, other], axis=0),
        jnp.concatenate([other, mine], axis=0),
    )


def front_kernel(
    state, me_ref, tok_ref, halo_ref, gain_ref, w_ref, w_small_ref, seg_ref, conv_x_ref,
    conv_bc_ref, head_ref, expand_ref, normed_ref, pre_x_ref, pre_bc_ref, halo_x_ref, halo_bc_ref,
    x_ref, bc_ref, xs_ref, dt_ref, cum_ref, aux_ref, keep_ref, send_ref
):
    s = pl.program_id(0)
    seqs = pl.num_programs(0)
    odd = me_ref[0] % 2
    half = state // 2
    own = xs_ref.shape[-1]
    wide = 2 * state
    span = tok_ref.shape[1]

    def norm(value):
        value = value.astype(F32)
        rstd = lax.rsqrt(jnp.mean(value * value, axis=-1, keepdims=True) + EPS)
        return (value * rstd * gain_ref[...]).astype(BF), rstd

    normed, rstd = norm(tok_ref[0])
    normed_ref[0] = normed
    room = jnp.zeros((EDGE - halo_ref.shape[1], halo_ref.shape[2]), F32)
    ahead = jnp.concatenate([room, norm(halo_ref[0])[0].astype(F32)], axis=0).astype(BF)
    rows = jnp.concatenate([ahead, normed], axis=0)
    pre_x = dot(rows, w_ref[0]).astype(BF)
    small = dot(rows, w_small_ref[...])
    pre_bc = small[:, :wide].astype(BF)
    dt_raw = small[EDGE:, wide:]

    seg = jnp.transpose(jnp.broadcast_to(seg_ref[0, 0:1], (LANES, LANES + span)))[LANES - EDGE :]
    here = seg[EDGE:]
    lane = lax.broadcasted_iota(jnp.int32, here.shape, 1)
    columns = [(back_rows(seg, 3 - tap)[EDGE:] == here).astype(F32) for tap in range(3)]
    columns.append((here == here[-1:]).astype(F32))
    columns.append((here == seg[EDGE - 1 : EDGE]).astype(F32))
    columns.append(here)
    columns.append(jnp.broadcast_to(rstd, here.shape))
    aux = jnp.zeros(here.shape, F32)
    for at, column in enumerate(columns):
        aux = jnp.where(lane == at, column, aux)
    aux_ref[0] = aux

    dt_ref[0] = dt_raw
    pre_x_ref[0] = pre_x[EDGE:]
    halo_x_ref[0] = pre_x[:EDGE]
    pre_bc_ref[0] = pre_bc[EDGE:]
    halo_bc_ref[0] = pre_bc[:EDGE]
    conv = conv_rows(pre_bc.astype(F32), aux, conv_bc_ref[...])
    bc = (conv * sigmoid(conv)).astype(BF)
    bc_ref[0] = bc
    conv = conv_rows(pre_x.astype(F32), aux, conv_x_ref[...])
    x = (conv * sigmoid(conv)).astype(BF)
    x_ref[0] = x
    x_float = x.astype(F32)
    step = softplus(dt_raw + head_ref[0:1])
    cum = running(-head_ref[1:2] * step, True)
    cum_ref[0] = cum
    expand = expand_ref[...]
    xs_ref[0] = (x_float * widen(step, expand)).astype(BF)
    last = cum[-1:]
    tail_step = jnp.exp(last - cum) * aux[:, 3:4] * step
    loaded = (x_float * widen(tail_step, expand)).astype(BF)
    own_state = dot(bc[:, :state], loaded, ((0,), (0,)))
    low, high = own_state[:half], own_state[half:]
    at = pl.ds(pl.multiple_of(s * half, half), half)
    keep_ref[at] = jnp.where(odd == 0, low, high).astype(BF)
    send_ref[at] = jnp.where(odd == 0, high, low).astype(BF)

    decay = jnp.broadcast_to(jnp.exp(last) * aux[-1:, 4:5], (8, LANES))
    decay_wide = widen(decay, expand)[:1]
    high = decay_wide.astype(BF).astype(F32)
    places = lax.broadcasted_iota(jnp.int32, (ROWS, 1), 0)
    extra = jnp.where(places == s, high, 0.0) + jnp.where(
        places == s + seqs, decay_wide - high, 0.0
    )
    end = pl.ds(seqs * half, ROWS)

    @pl.when(s == 0)
    def _():
        keep_ref[end] = extra.astype(BF)

    @pl.when(s > 0)
    def _():
        keep_ref[end] = (keep_ref[end].astype(F32) + extra).astype(BF)

    @pl.when(s == seqs - 1)
    def _():
        send_ref[end] = keep_ref[end]


def pair_kernel(seqs, groups, half, me_ref, mine_ref, other_ref, *rest):
    outs, decay_ref, scratch = rest[:groups], rest[groups], rest[groups + 1]
    odd, place = me_ref[0] % 2, me_ref[0] // 2
    end = seqs * half
    packed = [ref[end : end + ROWS].astype(F32) for ref in (mine_ref, other_ref)]
    mine, other = [p[:seqs] + p[seqs : 2 * seqs] for p in packed]
    first = jnp.where(odd == 0, mine, other)
    second = jnp.where(odd == 0, other, mine)
    decay_ref[0:seqs] = first
    decay_ref[8 : 8 + seqs] = second
    both = first * second
    high = both.astype(BF).astype(F32)
    room = jnp.zeros((ROWS - 2 * seqs, both.shape[1]), F32)
    extra = jnp.concatenate([high, both - high, room], axis=0)
    width = scratch.shape[3]
    across, _ = chunk_grid(groups, half, both.shape[1])
    for j in range(groups):
        b = j % across
        scratch[j, seqs] = extra[:, b * width : (b + 1) * width].astype(BF)
    for s in range(seqs):
        rows = slice(s * half, (s + 1) * half)
        mine, other = mine_ref[rows].astype(F32), other_ref[rows].astype(F32)
        early = jnp.where(odd == 0, mine, other)
        late = jnp.where(odd == 0, other, mine)
        cut(second[s : s + 1] * early + late, scratch, s, groups)
    for m in range(groups):
        outs[m][...] = scratch[place ^ m]


def pair_back_kernel(seqs, groups, half, me_ref, mine_ref, other_ref, decay_ref, *rest):
    outs, scratch = rest[:groups], rest[groups]
    odd, place = me_ref[0] % 2, me_ref[0] // 2
    for s in range(seqs):
        rows = slice(s * half, (s + 1) * half)
        mine, other = mine_ref[rows].astype(F32), other_ref[rows].astype(F32)
        early = jnp.where(odd == 0, mine, other)
        late = jnp.where(odd == 0, other, mine)
        cut(decay_ref[s : s + 1] * late + early, scratch, s, groups)
    for m in range(groups):
        outs[m][...] = scratch[place ^ m]


def scan_kernel(seqs, groups, me_ref, *rest):
    ins, outs = rest[:groups], rest[groups : 2 * groups]
    decay_ref, scratch = rest[2 * groups], rest[2 * groups + 1]
    place = me_ref[0] // 2
    for m in range(groups):
        scratch[place ^ m] = ins[m][...]
    for s in range(seqs):
        entry = jnp.zeros(scratch.shape[2:], F32)
        for k in range(groups):
            packed = scratch[k, seqs].astype(F32)
            decay = packed[s : s + 1] + packed[s + seqs : s + seqs + 1]
            decay_ref[k, s : s + 1] = decay
            arrived = scratch[k, s].astype(F32)
            scratch[k, s] = entry.astype(BF)
            entry = decay * entry + arrived
    for m in range(groups):
        outs[m][...] = scratch[place ^ m, :seqs]


def scan_back_kernel(seqs, groups, me_ref, decay_ref, *rest):
    ins, outs, scratch = rest[:groups], rest[groups : 2 * groups], rest[2 * groups]
    place = me_ref[0] // 2
    for m in range(groups):
        scratch[place ^ m] = ins[m][...]
    for s in range(seqs):
        leave = jnp.zeros(scratch.shape[2:], F32)
        for k in reversed(range(groups)):
            arrived = scratch[k, s].astype(F32)
            scratch[k, s] = leave.astype(BF)
            leave = decay_ref[k, s : s + 1] * leave + arrived
    for m in range(groups):
        outs[m][...] = scratch[place ^ m]


def unpair_kernel(seqs, groups, half, forward, me_ref, mine_ref, other_ref, decay_ref, *rest):
    ins, (own_ref, send_ref, scratch) = rest[:groups], rest[groups:]
    odd, place = me_ref[0] % 2, me_ref[0] // 2
    own = own_ref.shape[-1]
    for m in range(groups):
        scratch[place ^ m] = ins[m][...]
    is_first = (odd == 0) if forward else (odd == 1)
    for s in range(seqs):
        rows = slice(s * half, (s + 1) * half)
        entry = uncut(scratch, s, groups, half, own).astype(F32)
        mine, other = mine_ref[rows].astype(F32), other_ref[rows].astype(F32)
        first = jnp.where(is_first, mine, other)
        at = s if forward else 8 + s
        later = decay_ref[at : at + 1] * entry + first
        own_ref[s] = jnp.where(is_first, entry, later).astype(BF)
        send_ref[s] = jnp.where(is_first, later, entry).astype(BF)


def inner_kernel(state, bc_ref, xs_ref, cum_ref, aux_ref, seg_ref, out_ref):
    own = xs_ref.shape[-1]
    b_ssm, c_ssm = bc_ref[0, :, :state], bc_ref[0, :, state:]
    cum = cum_ref[0]
    cum_t = jnp.transpose(cum)
    mask = doc_mask(aux_ref[0, :, 5:6], seg_ref[0, 0:1, LANES:], True)
    scores = dot(c_ssm, b_ssm, ((1,), (1,))) * mask
    left = lax.broadcasted_iota(jnp.int32, (1, LANES), 1) < HEAD_DIM
    for pair in range(own // LANES):
        lanes = slice(pair * LANES, (pair + 1) * LANES)
        xs = xs_ref[0, :, lanes].astype(F32)
        total = None
        for side in range(2):
            h = 2 * pair + side
            lag = jnp.minimum(cum[:, h : h + 1] - cum_t[h : h + 1], 0.0)
            weights = (scores * jnp.exp(lag)).astype(BF)
            own_xs = jnp.where(left if side == 0 else ~left, xs, 0.0).astype(BF)
            term = dot(weights, own_xs)
            total = term if total is None else total + term
        out_ref[0, :, lanes] = total


def mixer_out(state, states, x_ref, bc_ref, inner_ref, gate_ref, cum_ref, aux_ref, rows_ref, expand_ref):
    c_ssm = bc_ref[0, :, state:]
    x_float = x_ref[0].astype(F32)
    entry_wide = widen(jnp.exp(cum_ref[0]) * aux_ref[0, :, 4:5], expand_ref[...])
    mixed = inner_ref[0] + dot(c_ssm, states) * entry_wide
    y = mixed + rows_ref[1:2] * x_float
    gate = gate_ref[0].astype(F32)
    sig = sigmoid(gate)
    return mixed, y, x_float, gate, sig, entry_wide


def sums_kernel(
    state, me_ref, x_ref, bc_ref, inner_ref, gate_ref, e_ref, cum_ref, aux_ref, mine_ref,
    other_ref, rows_ref, expand_ref, out_ref
):
    states = both_halves(me_ref[0], mine_ref, other_ref)
    _, y, _, gate, sig, _ = mixer_out(
        state, states, x_ref, bc_ref, inner_ref, gate_ref, cum_ref, aux_ref, rows_ref, expand_ref
    )
    gated = y * (gate * sig)
    squares = jnp.sum(gated * gated, axis=-1, keepdims=True)
    dots = jnp.sum(e_ref[0].astype(F32) * (gated * rows_ref[0:1]), axis=-1, keepdims=True)
    place = lax.broadcasted_iota(jnp.int32, (8, 1), 0)
    out_ref[0] = jnp.where(place == 0, to_row(squares), jnp.where(place == 1, to_row(dots), 0.0))


def gate_back_kernel(
    state, inner_total, me_ref, x_ref, bc_ref, inner_ref, gate_ref, e_ref, cum_ref, aux_ref,
    mine_ref, other_ref, rows_ref, expand_ref, sums_ref, scaled_ref, dz_ref, dy_ref, mixed_ref,
    dc_ref, dot_ref, grad_ref, keep_ref, send_ref
):
    s = pl.program_id(0)
    odd = me_ref[0] % 2
    half = state // 2
    expand = expand_ref[...]
    states = both_halves(me_ref[0], mine_ref, other_ref)
    mixed, y, x_float, gate, sig, entry_wide = mixer_out(
        state, states, x_ref, bc_ref, inner_ref, gate_ref, cum_ref, aux_ref, rows_ref, expand_ref
    )
    columns = jnp.transpose(
        jnp.concatenate([sums_ref[0], jnp.zeros((LANES - 8, sums_ref.shape[2]), F32)], axis=0)
    )
    rstd = lax.rsqrt(columns[:, 0:1] / inner_total + EPS)
    slope = columns[:, 1:2] * (rstd * rstd * rstd) / inner_total
    gain = rows_ref[0:1]
    silu = gate * sig
    gated = y * silu
    scaled_ref[0] = (gated * gain * rstd).astype(BF)
    d_scaled = e_ref[0].astype(F32) * rstd
    d_gated = d_scaled * gain - slope * gated
    d_y = d_gated * silu
    dy_ref[0] = d_y.astype(BF)
    d_z = (d_gated * y * (sig * (1.0 + gate * (1.0 - sig)))).astype(BF)
    dz_ref[0] = d_z
    row = jnp.sum(d_z.astype(F32) * gate, axis=-1, keepdims=True)
    dot_ref[0] = to_row(row)
    mixed_ref[0] = per_head(d_y * mixed, expand)

    @pl.when(s == 0)
    def _():
        grad_ref[...] = jnp.zeros_like(grad_ref)

    grad_ref[0:1] += jnp.sum(d_scaled * gated, axis=0, keepdims=True)
    grad_ref[1:2] += jnp.sum(d_y * x_float, axis=0, keepdims=True)
    d_carried = (d_y * entry_wide).astype(BF)
    dc_ref[0] = dot(d_carried, states, ((1,), (1,)))
    grad = dot(bc_ref[0, :, state:], d_carried, ((0,), (0,)))
    low, high = grad[:half], grad[half:]
    at = pl.ds(pl.multiple_of(s * half, half), half)
    keep_ref[at] = jnp.where(odd == 0, low, high).astype(BF)
    send_ref[at] = jnp.where(odd == 0, high, low).astype(BF)


def inner_back_kernel(
    state, x_ref, bc_ref, xs_ref, dy_ref, dc_ref, cum_ref, dt_ref, aux_ref, seg_ref, rows_ref,
    head_ref, expand_ref, dx_ref, dstep_ref, dbc_ref
):
    own = xs_ref.shape[-1]
    b_ssm, c_ssm = bc_ref[0, :, :state], bc_ref[0, :, state:]
    cum = cum_ref[0]
    cum_t = jnp.transpose(cum)
    nt = ((1,), (1,))
    mask = doc_mask(aux_ref[0, :, 5:6], seg_ref[0, 0:1, LANES:], False)
    scores = dot(b_ssm, c_ssm, nt) * mask
    left = lax.broadcasted_iota(jnp.int32, (1, LANES), 1) < HEAD_DIM
    d_scores = None
    sums = []
    for pair in range(own // LANES):
        lanes = slice(pair * LANES, (pair + 1) * LANES)
        xs = xs_ref[0, :, lanes]
        dy = dy_ref[0, :, lanes].astype(F32)
        total = None
        for side in range(2):
            h = 2 * pair + side
            lag = jnp.minimum(cum_t[h : h + 1] - cum[:, h : h + 1], 0.0)
            mixing = jnp.exp(lag)
            weights = (scores * mixing).astype(BF)
            own_dy = jnp.where(left if side == 0 else ~left, dy, 0.0).astype(BF)
            term = dot(weights, own_dy)
            total = term if total is None else total + term
            d_mixed = dot(xs, own_dy, nt) * mixing
            d_scores = d_mixed if d_scores is None else d_scores + d_mixed
        sums.append(total)
    back = jnp.concatenate(sums, axis=1)
    expand = expand_ref[...]
    x_float = x_ref[0].astype(F32)
    dstep_ref[0] = per_head(x_float * back, expand)
    step = softplus(dt_ref[0] + head_ref[0:1])
    dy_all = dy_ref[0].astype(F32)
    dx_ref[0] = (back * widen(step, expand) + rows_ref[1:2] * dy_all).astype(BF)
    d_scores = (d_scores * mask).astype(BF)
    dbc_ref[0, :, :state] = dot(d_scores, c_ssm)
    dbc_ref[0, :, state:] = dot(d_scores, b_ssm, ((0,), (0,))) + dc_ref[0]


def leave_kernel(
    state, me_ref, x_ref, bc_ref, pre_ref, halo_ref, pre_bc_ref, halo_bc_ref, dx_ref, dstep_ref,
    dbc_ref, mixed_ref, cum_ref, dt_ref, aux_ref, dot_z_ref, mine_ref, other_ref, end_mine_ref,
    end_other_ref, conv_ref, conv_bc_ref, head_ref, expand_ref, dpre_ref, back_ref, back_bc_ref,
    dbc_out_ref, ddt_ref, dot_ref, grad_ref, small_ref
):
    me = me_ref[0]
    own = dx_ref.shape[-1]
    expand = expand_ref[...]
    states = both_halves(me, mine_ref, other_ref)
    ends = both_halves(me, end_mine_ref, end_other_ref)
    b_ssm = bc_ref[0, :, :state]
    x_float = x_ref[0].astype(F32)
    aux = aux_ref[0]
    dt_pre = dt_ref[0] + head_ref[0:1]
    step = softplus(dt_pre)
    rate = head_ref[1:2]
    cum = cum_ref[0]
    last = cum[-1:]
    tail_decay = jnp.exp(last - cum) * aux[:, 3:4]
    tail_step = tail_decay * step
    tail_wide = widen(tail_step, expand)
    loaded = (x_float * tail_wide).astype(BF)
    d_loaded = dot(b_ssm, ends)
    dbc_out_ref[0, :, :state] = (dbc_ref[0, :, :state] + dot(loaded, ends, ((1,), (1,)))).astype(BF)
    dbc_out_ref[0, :, state:] = dbc_ref[0, :, state:].astype(BF)
    d_bc = dbc_out_ref[0, :EDGE].astype(F32)
    extended = jnp.concatenate([halo_bc_ref[0], pre_bc_ref[0, :EDGE]], axis=0).astype(F32)
    weight = conv_bc_ref[...]
    conv = conv_rows(extended, aux[:EDGE], weight)
    sig = sigmoid(conv)
    d_conv = d_bc * (sig * (1.0 + conv * (1.0 - sig)))
    back_bc_ref[0] = conv_back_rows(d_conv, extended, aux[:EDGE], weight)[:EDGE].astype(BF)
    d_x = dx_ref[0].astype(F32) + d_loaded * tail_wide
    d_tail = per_head(d_loaded * x_float, expand)
    end_terms = d_tail * tail_step
    product = jnp.sum(ends.astype(F32) * states.astype(F32), axis=0, keepdims=True)
    d_decay = per_head(jnp.broadcast_to(product, (8, own)), expand)[:1]
    block_decay = jnp.exp(last) * aux[-1:, 4:5]
    d_cum = mixed_ref[0] - step * dstep_ref[0] - end_terms
    last_add = jnp.sum(end_terms, axis=0, keepdims=True) + d_decay * block_decay
    d_log = running(d_cum, False) + last_add
    d_step = dstep_ref[0] + d_tail * tail_decay - d_log * rate
    d_dt = d_step * sigmoid(dt_pre)
    ddt_ref[0] = d_dt.astype(BF)

    @pl.when(pl.program_id(0) == 0)
    def _():
        grad_ref[...] = jnp.zeros_like(grad_ref)
        small_ref[...] = jnp.zeros_like(small_ref)

    small_ref[0:1] += jnp.sum(d_dt, axis=0, keepdims=True)
    small_ref[1:2] += jnp.sum(d_log * (-rate * step), axis=0, keepdims=True)

    extended = jnp.concatenate([halo_ref[0], pre_ref[0]], axis=0).astype(F32)
    weight = conv_ref[...]
    conv = conv_rows(extended, aux, weight)
    sig = sigmoid(conv)
    d_conv = d_x * (sig * (1.0 + conv * (1.0 - sig)))
    d_ext = conv_back_rows(d_conv, extended, aux, weight, grad_ref)
    d_pre = d_ext[EDGE:].astype(BF)
    dpre_ref[0] = d_pre
    back_ref[0] = d_ext[:EDGE].astype(BF)
    row = jnp.sum(d_pre.astype(F32) * extended[EDGE:], axis=-1, keepdims=True)
    row = row + jnp.sum(ddt_ref[0].astype(F32) * dt_ref[0], axis=-1, keepdims=True)
    dot_ref[0] = to_row(row) + dot_z_ref[0]


def conv_bc_kernel(d_ref, pre_ref, halo_ref, aux_ref, conv_ref, dpre_ref, dot_ref, grad_ref):
    span = pre_ref.shape[1]
    extended = jnp.concatenate([halo_ref[0], pre_ref[0]], axis=0).astype(F32)
    aux = aux_ref[0]
    weight = conv_ref[...]
    conv = conv_rows(extended, aux, weight)
    sig = sigmoid(conv)
    d_conv = d_ref[0, :span].astype(F32) * (sig * (1.0 + conv * (1.0 - sig)))

    @pl.when(pl.program_id(0) == 0)
    def _():
        grad_ref[...] = jnp.zeros_like(grad_ref)

    d_pre = conv_back_rows(d_conv, extended, aux, weight, grad_ref)[EDGE:]
    ahead = d_ref[0, span : span + EDGE].astype(F32)
    d_pre = jnp.concatenate([d_pre[: span - EDGE], d_pre[span - EDGE :] + ahead], axis=0)
    d_pre = d_pre.astype(BF)
    dpre_ref[0] = d_pre
    row = jnp.sum(d_pre.astype(F32) * extended[EDGE:], axis=-1, keepdims=True)
    packed = d_ref[0, span + EDGE :].astype(F32)
    dot_ref[0] = to_row(row) + (packed[0:1] + packed[1:2])


def gram_chunk_kernel(me_ref, a_ref, b_ref, *outs):
    product = dot(a_ref[...], b_ref[...], ((0,), (0,))).astype(BF)
    width = product.shape[1] // len(outs)
    for at, out_ref in enumerate(outs):
        out_ref[0] = product[:, at * width : (at + 1) * width]


def share_kernel(terms, with_sum, me_ref, *refs):
    out_ref = refs[2 * terms + with_sum]
    nt = ((1,), (1,))
    total = None
    for t in range(terms):
        rhs = refs[2 * t + 1]
        rhs = rhs[0] if len(rhs.shape) == 3 else rhs[...]
        term = dot(refs[2 * t][...], rhs, nt)
        total = term if total is None else total + term
    out_ref[0] = total.astype(BF)
    if with_sum:
        sum_ref = refs[-1]

        @pl.when(pl.program_id(1) == 0)
        def _():
            sum_ref[...] = jnp.zeros_like(sum_ref)

        normed = refs[2 * terms][...].astype(F32)
        sum_ref[0, 0:1] += jnp.sum(total * normed, axis=0, keepdims=True)


def per_seq(seqs, shape):
    zeros = (0,) * len(shape)
    return pl.BlockSpec((1, *shape), lambda s: (jnp.minimum(s, seqs - 1), *zeros))


def whole(shape):
    zeros = (0,) * len(shape)
    return pl.BlockSpec(tuple(shape), lambda s: zeros)


def call(body, grid, ins, in_specs, outs, out_specs, scratch, flops, name, aliases={}):
    return pl.pallas_call(
        body,
        grid=(grid,),
        in_specs=in_specs,
        out_specs=out_specs,
        out_shape=outs,
        scratch_shapes=scratch,
        name=name,
        input_output_aliases=aliases,
        compiler_params=pltpu.CompilerParams(vmem_limit_bytes=VMEM),
        cost_estimate=cost(flops),
    )(*ins)


def shaped(shape, dtype):
    return jax.ShapeDtypeStruct(tuple(shape), dtype)


def swap(value, axis, mask):
    count = lax.axis_size(axis)
    return lax.ppermute(value, axis, [(i, i ^ mask) for i in range(count)])


def shift(value, axis, steps):
    count = lax.axis_size(axis)
    leading, last = (max(0, -steps), min(count, count - steps))
    return lax.ppermute(value, axis, [(i, i + steps) for i in range(leading, last)])


def exchange(chunks, masks):
    return [swap(c, "seq", mask) if mask else c for c, mask in zip(chunks, masks)]


def after(value, *others):
    return lax.optimization_barrier((value, *others))[0]


def fold_step(sides, axis, mask):
    odd, even = sides
    arrived = swap(odd, axis, mask)
    if even.shape[0] == 1:
        return (even + arrived)[0]
    return even[1::2] + arrived[1::2], even[0::2] + arrived[0::2]


def fold(sides, axis, mask=1):
    while isinstance(sides, tuple):
        sides = fold_step(sides, axis, mask)
        mask *= 2
    return sides


def pair_sides(full):
    odd = lax.axis_index("seq") % 2
    chunks = full.reshape(lax.axis_size("seq") // 2, 2, -1, full.shape[-1])
    return tuple(lax.dynamic_index_in_dim(chunks, at, 1, False) for at in (1 - odd, odd))


def pair_sum(sides):
    return sides[1] + swap(sides[0], "seq", 1)


def spread_sum(total):
    count = lax.axis_size("seq")
    return lax.psum_scatter(
        total.reshape(-1, total.shape[-1]),
        "seq",
        scatter_dimension=0,
        tiled=True,
        axis_index_groups=[[2 * z + x for z in range(count // 2)] for x in range(2)],
    )


def row_sides(full, axis):
    count = lax.axis_size(axis)
    me = lax.axis_index(axis)
    chunks = full.reshape(count, -1, full.shape[-1])

    def stacked(masks):
        return jnp.stack([lax.dynamic_index_in_dim(chunks, me ^ m, 0, False) for m in masks])

    return stacked(range(1, count, 2)), stacked(range(0, count, 2))


def sum_all(value, axis):
    mask = 1
    while mask < lax.axis_size(axis):
        value = value + swap(value, axis, mask)
        mask *= 2
    return value


def pad_lanes(value, width):
    return jnp.pad(value, ((0, 0), (0, width - value.shape[1])))


def pad_rows(rows, count=8):
    stacked = jnp.concatenate([r.reshape(-1, r.shape[-1]).astype(F32) for r in rows], axis=0)
    return jnp.pad(stacked, ((0, count - stacked.shape[0]), (0, 0)))


def local(
    tokens,
    segments,
    norm_gain,
    w_zx,
    w_bc,
    w_dt,
    conv_x,
    conv_x_bias,
    conv_bc,
    conv_bc_bias,
    dt_bias,
    a_log,
    d_skip,
    gate_gain,
    w_out,
    cotangent,
):
    seqs, span, model = tokens.shape
    rows = seqs * span
    heads = d_skip.shape[0]
    own = heads * HEAD_DIM
    n_seq, n_head = lax.axis_size("seq"), lax.axis_size("head")
    me_head = lax.axis_index("head")
    me = lax.axis_index("seq").astype(jnp.int32).reshape(1)
    head_at = me_head.astype(jnp.int32).reshape(1)
    inner_total = own * n_head
    state = w_bc.shape[1] // 2
    half = state // 2
    wide = 2 * state
    share = model // n_head
    offset = me_head * share
    edge = conv_x.shape[0] - 1
    groups = n_seq // 2
    masks = [2 * m for m in range(groups)]
    _, width = chunk_grid(groups, half, own)

    tok_halo = shift(tokens[:, -8:], "seq", 1)
    seg_halo = shift(segments[:, -8:], "seq", 1)
    cot_full = lax.all_gather(cotangent, "head", axis=2, tiled=True)

    w_in = lax.optimization_barrier(jnp.transpose(w_zx, (1, 0, 2)))
    w_dt = pad_lanes(w_dt, LANES)
    w_small = jnp.concatenate([w_bc, w_dt], axis=1)
    seg_rows = jnp.concatenate([jnp.pad(seg_halo, ((0, 0), (LANES - 8, 0))), segments], axis=1)
    seg_rows = jnp.broadcast_to(seg_rows.astype(F32)[:, None], (seqs, 8, LANES + span))
    conv_x_w = pad_rows([conv_x, conv_x_bias])
    conv_bc_w = pad_rows([conv_bc, conv_bc_bias])
    head_rows = pad_lanes(pad_rows([dt_bias, jnp.exp(a_log)]), LANES)
    wide_rows = pad_rows([gate_gain, jnp.repeat(d_skip, HEAD_DIM)])
    expand = (
        jnp.arange(LANES)[:, None] == (jnp.arange(own) // HEAD_DIM)[None, :]
    ).astype(BF)

    seq = functools.partial(per_seq, seqs)

    def seq_of(values):
        return [seq(v.shape[1:]) for v in values]

    def whole_of(values):
        return [whole(v.shape) for v in values]

    w_x_spec = pl.BlockSpec((1, model, own), lambda s: (1, 0, 0))
    ins = (
        me, tokens, tok_halo, norm_gain.reshape(1, model), w_in, w_small, seg_rows, conv_x_w,
        conv_bc_w, head_rows, expand,
    )
    per = (
        shaped((seqs, span, model), BF),
        shaped((seqs, span, own), BF),
        shaped((seqs, span, wide), BF),
        shaped((seqs, EDGE, own), BF),
        shaped((seqs, EDGE, wide), BF),
        shaped((seqs, span, own), BF),
        shaped((seqs, span, wide), BF),
        shaped((seqs, span, own), BF),
        shaped((seqs, span, LANES), F32),
        shaped((seqs, span, LANES), F32),
        shaped((seqs, span, LANES), F32),
    )
    packed = (shaped((seqs * half + ROWS, own), BF),) * 2
    normed, pre_x, pre_bc, halo_x, halo_bc, x_ssm, bc_ssm, xs, dt_raw, cum, aux, keep, send = call(
        functools.partial(front_kernel, state),
        seqs,
        ins,
        [SMEM_SPEC, *seq_of(ins[1:3]), whole(ins[3].shape), w_x_spec, whole(w_small.shape)]
        + seq_of(ins[6:7])
        + whole_of(ins[7:]),
        per + packed,
        seq_of(per) + whole_of(packed),
        [],
        30,
        "front",
    )

    def small_call(body, ins, outs, blocks, name):
        return call(
            body,
            1,
            ins,
            [SMEM_SPEC] + whole_of(ins[1:]),
            outs,
            whole_of(outs),
            [pltpu.VMEM((groups, blocks, ROWS, width), BF)],
            3,
            name,
        )

    piece = shaped((seqs, ROWS, width), BF)
    halves_out = (shaped((seqs, half, own), BF),) * 2
    other = swap(send, "seq", 1)
    *parts, pair_decay = small_call(
        functools.partial(pair_kernel, seqs, groups, half),
        (me, keep, other),
        (shaped((seqs + 1, ROWS, width), BF),) * groups + (shaped((16, own), F32),),
        seqs + 1,
        "pair",
    )
    *entries, decays = small_call(
        functools.partial(scan_kernel, seqs, groups),
        (me, *exchange(parts, masks)),
        (piece,) * groups + (shaped((groups, 8, width), F32),),
        seqs + 1,
        "scan",
    )
    state_mine, state_send = small_call(
        functools.partial(unpair_kernel, seqs, groups, half, True),
        (me, keep, other, pair_decay, *exchange(entries, masks)),
        halves_out,
        seqs,
        "unpair",
    )
    state_other = swap(state_send, "seq", 1)

    gate = dot(normed, w_in[0], ((2,), (0,))).astype(BF)
    e_raw = dot(cot_full, w_out, ((2,), (0,))).astype(BF)
    ins = (bc_ssm, xs, cum, aux, seg_rows)
    (inner,) = call(
        functools.partial(inner_kernel, state),
        seqs,
        ins,
        seq_of(ins),
        (shaped((seqs, span, own), F32),),
        [seq((span, own))],
        [],
        10.3,
        "inner",
    )

    mixer = (me, x_ssm, bc_ssm, inner, gate, e_raw, cum, aux, state_mine, state_other, wide_rows, expand)
    mixer_specs = [SMEM_SPEC] + seq_of(mixer[1:10]) + whole_of(mixer[10:])
    (sums,) = call(
        functools.partial(sums_kernel, state),
        seqs,
        mixer,
        mixer_specs,
        (shaped((seqs, 8, span), F32),),
        [seq((8, span))],
        [],
        12,
        "sums",
    )
    sums = sum_all(sums, "head")

    per = (
        shaped((seqs, span, own), BF),
        shaped((seqs, span, own), BF),
        shaped((seqs, span, own), BF),
        shaped((seqs, span, LANES), F32),
        shaped((seqs, span, state), F32),
        shaped((seqs, 8, span), F32),
    )
    fixed = (shaped((8, own), F32),) + (shaped((seqs * half, own), BF),) * 2
    scaled, d_z, d_y, mixed, d_c, dot_z, gate_grads, keep, send = call(
        functools.partial(gate_back_kernel, state, inner_total),
        seqs,
        (*mixer, sums),
        mixer_specs + [seq((8, span))],
        per + fixed,
        seq_of(per) + whole_of(fixed),
        [],
        21,
        "gate_back",
    )

    other = swap(send, "seq", 1)

    ins = (x_ssm, bc_ssm, xs, d_y, d_c, cum, dt_raw, aux, seg_rows, wide_rows, head_rows, expand)
    per = (
        shaped((seqs, span, own), BF),
        shaped((seqs, span, LANES), F32),
        shaped((seqs, span, wide), F32),
    )
    d_x, d_step, d_bc = call(
        functools.partial(inner_back_kernel, state),
        seqs,
        ins,
        seq_of(ins[:9]) + whole_of(ins[9:]),
        per,
        seq_of(per),
        [],
        18.6,
        "inner_back",
    )

    normed_rows = normed.reshape(rows, model)

    def chunk_sides(left, values, pieces, natural=False):
        tile = model // n_seq
        block = values.shape[1] // pieces
        if tile % LANES:
            full = dot(left, values, ((0,), (0,))).astype(BF)
            cuts = [full[:, at * block : (at + 1) * block] for at in range(pieces)]
            if natural:
                return [pair_sides(c) for c in cuts]
            return [row_sides(c, "seq") for c in cuts]
        sides = []
        for parity in (1, 0):
            if sides:
                values = after(values, sides[0][0])
            sides.append(
                pl.pallas_call(
                    gram_chunk_kernel,
                    grid_spec=pltpu.PrefetchScalarGridSpec(
                        num_scalar_prefetch=1,
                        grid=(groups,),
                        in_specs=[
                            pl.BlockSpec(
                                (rows, tile), lambda i, me_ref: (
                                    0,
                                    2 * i + ((parity + me_ref[0]) % 2)
                                    if natural
                                    else (2 * i + parity) ^ me_ref[0],
                                ),
                            ),
                            pl.BlockSpec(values.shape, lambda i, me_ref: (0, 0)),
                        ],
                        out_specs=[
                            pl.BlockSpec((1, tile, block), lambda i, me_ref: (i, 0, 0))
                        ] * pieces,
                    ),
                    out_shape=[shaped((groups, tile, block), BF)] * pieces,
                    name="gram_chunks",
                    compiler_params=pltpu.CompilerParams(vmem_limit_bytes=VMEM),
                    cost_estimate=pl.CostEstimate(
                        flops=rows * model * values.shape[1],
                        bytes_accessed=rows * (model + 2 * values.shape[1])
                        + model * values.shape[1],
                        transcendentals=0,
                    ),
                )(me, left, values)
            )
        return list(zip(*sides))

    def share_sum(terms, parity, summed):
        pairs = n_head // 2
        tall = rows
        def at(i, head_ref):
            return (2 * i + parity) ^ head_ref[0]

        ins, specs = [], []
        for lhs, rhs, first in terms:
            ins += [lhs, rhs]
            specs.append(pl.BlockSpec((tall, lhs.shape[1]), lambda i, s, head_ref: (s, 0)))
            if rhs.ndim == 3:
                specs.append(
                    pl.BlockSpec(
                        (1, share, rhs.shape[2]),
                        lambda i, s, head_ref, first=first: (first, at(i, head_ref), 0),
                    )
                )
            else:
                specs.append(
                    pl.BlockSpec(
                        (share, rhs.shape[1]), lambda i, s, head_ref: (at(i, head_ref), 0)
                    )
                )
        out_specs = [pl.BlockSpec((1, tall, share), lambda i, s, head_ref: (i, s, 0))]
        outs = [shaped((pairs, rows, share), BF)]
        if summed:
            ins.append(normed_rows)
            specs.append(
                pl.BlockSpec((tall, share), lambda i, s, head_ref: (s, at(i, head_ref)))
            )
            out_specs.append(pl.BlockSpec((1, 8, share), lambda i, s, head_ref: (i, 0, 0)))
            outs.append(shaped((pairs, 8, share), F32))
        depth = sum(t[0].shape[1] for t in terms)
        got = pl.pallas_call(
            functools.partial(share_kernel, len(terms), summed),
            grid_spec=pltpu.PrefetchScalarGridSpec(
                num_scalar_prefetch=1,
                grid=(pairs, rows // tall),
                in_specs=specs,
                out_specs=out_specs,
            ),
            out_shape=outs,
            name="shares",
            compiler_params=pltpu.CompilerParams(vmem_limit_bytes=VMEM),
            cost_estimate=cost(rows * model * depth / 5e8),
        )(head_at, *ins)
        return got if summed else got[0]

    scaled_rows, d_z_rows = scaled.reshape(rows, own), d_z.reshape(rows, own)
    parts = small_call(
        functools.partial(pair_back_kernel, seqs, groups, half),
        (me, after(keep, d_x), other, pair_decay),
        (piece,) * groups,
        seqs,
        "pair_back",
    )
    arrived = exchange(parts, masks)
    (out_grad,) = chunk_sides(cot_full.reshape(rows, model), after(scaled_rows, parts[0]), 1, True)
    out_total = pair_sum(out_grad)
    leaves = small_call(
        functools.partial(scan_back_kernel, seqs, groups),
        (me, after(decays, out_grad[1]), *arrived),
        (piece,) * groups,
        seqs,
        "scan_back",
    )
    arrived = exchange(leaves, masks)
    (gate_grad,) = chunk_sides(normed_rows, after(d_z_rows, leaves[0]), 1, True)
    end_mine, end_send = small_call(
        functools.partial(unpair_kernel, seqs, groups, half, False),
        (me, after(keep, gate_grad[1]), other, pair_decay, *arrived),
        halves_out,
        seqs,
        "unpair_back",
    )
    end_other = swap(end_send, "seq", 1)
    gate_total = pair_sum((after(gate_grad[0], end_other), gate_grad[1]))
    out_odd = share_sum([(after(scaled_rows, end_mine), w_out, 0)], 1, False)
    out_even = share_sum([(after(scaled_rows, out_odd), w_out, 0)], 0, False)

    ins = (
        me, after(x_ssm, out_even, out_total), bc_ssm, pre_x, halo_x, pre_bc, halo_bc, d_x, d_step, d_bc, mixed, cum,
        dt_raw, aux, dot_z, state_mine, state_other, end_mine, end_other, conv_x_w, conv_bc_w,
        head_rows, expand,
    )
    per = (
        shaped((seqs, span, own), BF),
        shaped((seqs, EDGE, own), BF),
        shaped((seqs, EDGE, wide), BF),
        shaped((seqs, span, wide), BF),
        shaped((seqs, span, LANES), BF),
        shaped((seqs, 8, span), F32),
    )
    fixed = (shaped((8, own), F32), shaped((8, LANES), F32))
    d_x_pre, back_x, back_bc, d_bc, d_dt, row_dot, conv_grads, head_grads = call(
        functools.partial(leave_kernel, state),
        seqs,
        ins,
        [SMEM_SPEC] + seq_of(ins[1:19]) + whole_of(ins[19:]),
        per + fixed,
        seq_of(per) + whole_of(fixed),
        [],
        28,
        "leave",
    )
    back = shift(jnp.concatenate([back_x, back_bc], axis=2)[:, -edge:], "seq", -1)
    back_x, back_bc = back[..., :own], back[..., own:]
    fix = jnp.sum(back_x.astype(F32) * pre_x[:, -edge:].astype(F32), axis=-1)
    row_dot = row_dot[:, 0] + jnp.pad(fix, ((0, 0), (span - edge, 0)))
    dot_high = row_dot.astype(BF)
    dot_low = (row_dot - dot_high.astype(F32)).astype(BF)
    dots = jnp.pad(jnp.stack([dot_high, dot_low], axis=1), ((0, 0), (0, EDGE - 2), (0, 0)))
    back_bc = jnp.pad(back_bc, ((0, 0), (EDGE - edge, 0), (0, 0)))
    d_bc = jnp.concatenate([d_bc, back_bc, dots], axis=1)
    d_bc = d_bc + swap(d_bc, "head", 1)
    d_x_pre = after(d_x_pre, d_bc, gate_total).at[:, -edge:].add(back_x)
    d_x_rows = d_x_pre.reshape(rows, own)
    d_dt_rows = d_dt.reshape(rows, LANES)
    (late_sides,) = chunk_sides(normed_rows, d_x_rows, 1, True)

    core, middle = me_head % 2, seqs // 2
    part = lax.dynamic_slice_in_dim(d_bc, core * middle, middle, 0)
    mask = 2
    while mask < n_head:
        part = part + swap(part, "head", mask)
        mask *= 2
    part = after(part, late_sides[1])
    part_other = swap(part, "head", 1)
    d_bc_all = jnp.where(
        core == 0,
        jnp.concatenate([part, part_other], axis=0),
        jnp.concatenate([part_other, part], axis=0),
    )
    ins = (d_bc_all, pre_bc, halo_bc, aux, conv_bc_w)
    per = (shaped((seqs, span, wide), BF), shaped((seqs, 8, span), F32))
    d_bc_pre, row_dot, bc_grads = call(
        conv_bc_kernel,
        seqs,
        ins,
        seq_of(ins[:4]) + whole_of(ins[4:]),
        per + (shaped((8, wide), F32),),
        seq_of(per) + [whole((8, wide))],
        [],
        6.3,
        "conv_bc",
    )
    d_small = jnp.concatenate([d_bc_pre.reshape(rows, wide), d_dt_rows], axis=-1)
    (small_sides,) = chunk_sides(normed_rows, d_small, 1)
    out_next = fold_step((out_odd, after(out_even, d_bc_pre)), "head", 1)
    terms = [(after(d_z_rows, small_sides[1], *out_next), w_in, 0), (d_x_rows, w_in, 1)]
    terms.append((d_dt_rows, w_dt, 0))
    grad_odd, norm_odd = share_sum(terms, 1, True)
    late_total = pair_sum((late_sides[0], after(late_sides[1], grad_odd)))
    terms[0] = (after(d_z_rows, late_total), w_in, 0)
    grad_even, norm_even = share_sum(terms, 0, True)
    grad_next = fold_step((grad_odd, grad_even), "head", 1)
    small_next = fold_step((small_sides[0], after(small_sides[1], *grad_next)), "seq", 1)
    out_next = out_next[0], after(out_next[1], *small_next)
    own_sum = fold(out_next, "head", 2).reshape(seqs, span, share)
    tokens_own = lax.dynamic_slice_in_dim(tokens, offset, share, 2).astype(F32)
    layer_out = (tokens_own + own_sum.astype(F32)).astype(BF)
    own_grad = fold(grad_next, "head", 2).reshape(seqs, span, share).astype(F32)
    late_s = fold(small_next, "seq", 2).astype(F32)
    out_grad_own = spread_sum(out_total).astype(F32)
    gate_grad_own = spread_sum(gate_total).astype(F32)
    late_a = spread_sum(late_total).astype(F32)

    row_dot = row_dot[:, 0]
    w_bc_own = lax.dynamic_slice_in_dim(w_bc, offset, share, 0)
    bc_term = dot(d_bc_pre, w_bc_own, ((2,), (1,)))
    rstd_in = aux[:, :, 6:7]
    unit_own = tokens_own * rstd_in
    gain_own = lax.dynamic_slice_in_dim(norm_gain, offset, share, 0)
    d_unit = (own_grad + bc_term) * gain_own
    input_grad = (
        rstd_in * (d_unit - unit_own * (row_dot / model)[..., None]) + cotangent.astype(F32)
    ).astype(BF)

    taps = edge + 1
    norm_part = jnp.concatenate([norm_even[:, 0], norm_odd[:, 0]], axis=0)
    norm_part = norm_part.at[0].add(gain_own * jnp.sum(bc_term * unit_own, axis=(0, 1)))
    small = (
        norm_part,
        conv_grads[:taps],
        conv_grads[taps],
        bc_grads[:taps],
        bc_grads[taps],
        head_grads[0, :heads],
        head_grads[1, :heads],
        jnp.sum(gate_grads[1].reshape(heads, HEAD_DIM), axis=-1),
        gate_grads[0],
    )
    flat = sum_all(jnp.concatenate([v.reshape(-1) for v in small]), "seq")
    summed, at = [], 0
    for v in small:
        summed.append(flat[at : at + v.size].reshape(v.shape))
        at += v.size
    norm_part = summed.pop(0)
    g_norm = fold((norm_part[n_head // 2 :], norm_part[: n_head // 2]), "head") / gain_own
    g_w_zx_own = jnp.stack([gate_grad_own, late_a], axis=1)
    return (
        layer_out,
        input_grad,
        g_norm,
        g_w_zx_own,
        late_s[:, :wide],
        late_s[:, wide : wide + heads],
        *summed,
        out_grad_own,
    )


def solution(mesh):
    placed = (
        P(None, "seq", None),
        P(None, "seq"),
        P(),
        P(None, None, "head"),
        P(),
        P(None, "head"),
        P(None, "head"),
        P("head"),
        P(),
        P(),
        P("head"),
        P("head"),
        P("head"),
        P("head"),
        P(None, "head"),
        P(None, "seq", "head"),
    )
    return jax.shard_map(
        local,
        mesh=mesh,
        in_specs=placed,
        out_specs=(
            P(None, "seq", "head"),
            P(None, "seq", "head"),
            P("head"),
            P("seq", None, "head"),
            P("seq", None),
            P("seq", "head"),
            P(None, "head"),
            P("head"),
            P(),
            P(),
            P("head"),
            P("head"),
            P("head"),
            P("head"),
            P("seq", "head"),
        ),
        check_vma=False,
    )
```

```python
import functools

import jax
import jax.numpy as jnp
from jax import lax
from jax.experimental import pallas as pl
from jax.experimental.pallas import tpu as pltpu
from jax.sharding import PartitionSpec as P

HEAD_DIM = 64
BLOCK_LEN = 256
LANES = 128
EDGE = 16
ROWS = 16
VMEM = 56 * 2**20
EPS = 1e-05
BF = jnp.bfloat16
F32 = jnp.float32
def cost(micros):
    return pl.CostEstimate(flops=int(micros * 1.15e+09), bytes_accessed=1000, transcendentals=0)


SMEM_SPEC = pl.BlockSpec(memory_space=pltpu.SMEM)


def dot(a, b, contract=((1,), (0,)), precision=None):
    return lax.dot_general(
        a, b, (contract, ((), ())), preferred_element_type=F32, precision=precision
    )


def halves(value):
    high = value.astype(BF)
    return high, (value - high.astype(F32)).astype(BF)


def widen(value, expand):
    high, low = halves(value)
    return dot(high, expand) + dot(low, expand)


def per_head(value, expand):
    lane = lax.broadcasted_iota(jnp.int32, (1, LANES), 1)
    left = lane < HEAD_DIM
    total = None
    for pair in range(value.shape[1] // LANES):
        both = value[:, pair * LANES : (pair + 1) * LANES]
        low = jnp.sum(jnp.where(left, both, 0.0), axis=1, keepdims=True)
        high = jnp.sum(jnp.where(left, 0.0, both), axis=1, keepdims=True)
        placed = jnp.where(lane == 2 * pair, low, jnp.where(lane == 2 * pair + 1, high, 0.0))
        total = placed if total is None else total + placed
    return total


def to_row(column):
    rows = column.shape[0]
    return jnp.transpose(jnp.broadcast_to(column, (rows, LANES)))[:8]


def sigmoid(value):
    return 0.5 * jnp.tanh(0.5 * value) + 0.5


def softplus(value):
    return jnp.maximum(value, 0.0) + jnp.log1p(jnp.exp(-jnp.abs(value)))


def triangle(span, lower):
    row = lax.broadcasted_iota(jnp.int32, (span, span), 0)
    col = lax.broadcasted_iota(jnp.int32, (span, span), 1)
    return ((col <= row) if lower else (col >= row)).astype(F32)


def running(value, lower):
    width = value.shape[1]
    high, low = halves(value)
    lowest = (value - high.astype(F32) - low.astype(F32)).astype(BF)
    parts = jnp.concatenate([high, low, lowest], axis=1)
    sums = dot(triangle(value.shape[0], lower).astype(BF), parts)
    return sums[:, :width] + sums[:, width : 2 * width] + sums[:, 2 * width :]


def doc_mask(seg_col, seg_row, lower):
    span = seg_col.shape[0]
    row = lax.broadcasted_iota(jnp.int32, (span, span), 0)
    col = lax.broadcasted_iota(jnp.int32, (span, span), 1)
    causal = (col <= row) if lower else (col >= row)
    return jnp.where(causal, (seg_col == seg_row).astype(F32), 0.0)


def back_rows(value, steps):
    return value if steps == 0 else pltpu.roll(value, steps, 0)


def ahead_rows(value, steps):
    return value if steps == 0 else pltpu.roll(value, value.shape[0] - steps, 0)


def conv_rows(extended, aux, weight):
    taps = 4
    out = weight[taps : taps + 1] + weight[taps - 1 : taps] * extended[EDGE:]
    for tap in range(taps - 1):
        window = back_rows(extended, taps - 1 - tap)[EDGE:]
        out = out + weight[tap : tap + 1] * (aux[:, tap : tap + 1] * window)
    return out


def conv_back_rows(d_conv, extended, aux, weight, grad_ref=None):
    taps = 4
    room = jnp.zeros((EDGE, d_conv.shape[1]), F32)
    total = None
    for tap in range(taps):
        steps = taps - 1 - tap
        masked = d_conv if steps == 0 else d_conv * aux[:, tap : tap + 1]
        if grad_ref is not None:
            window = back_rows(extended, steps)[EDGE:]
            grad_ref[tap : tap + 1] += jnp.sum(masked * window, axis=0, keepdims=True)
        placed = jnp.concatenate([room, masked * weight[tap : tap + 1]], axis=0)
        placed = ahead_rows(placed, steps)
        total = placed if total is None else total + placed
    if grad_ref is not None:
        grad_ref[taps : taps + 1] += jnp.sum(d_conv, axis=0, keepdims=True)
    return total


def chunk_grid(count, rows, own):
    across = count * ROWS // rows
    return across, own // across


def cut(value, scratch, at, count):
    across, width = chunk_grid(count, value.shape[0], value.shape[1])
    for j in range(count):
        a, b = j // across, j % across
        scratch[j, at] = value[a * ROWS : (a + 1) * ROWS, b * width : (b + 1) * width].astype(BF)


def uncut(scratch, at, count, rows, own):
    across, _ = chunk_grid(count, rows, own)
    return jnp.concatenate(
        [
            jnp.concatenate([scratch[a * across + b, at] for b in range(across)], axis=1)
            for a in range(count // across)
        ],
        axis=0,
    )


def both_halves(me, mine_ref, other_ref):
    mine, other = mine_ref[0], other_ref[0]
    return jnp.where(
        me % 2 == 0,
        jnp.concatenate([mine, other], axis=0),
        jnp.concatenate([other, mine], axis=0),
    )


def front_kernel(
    state, me_ref, tok_ref, halo_ref, gain_ref, w_ref, w_small_ref, seg_ref, conv_x_ref,
    conv_bc_ref, head_ref, expand_ref, normed_ref, pre_x_ref, pre_bc_ref, halo_x_ref, halo_bc_ref,
    x_ref, bc_ref, xs_ref, dt_ref, cum_ref, aux_ref, keep_ref, send_ref
):
    s = pl.program_id(0)
    seqs = pl.num_programs(0)
    odd = me_ref[0] % 2
    half = state // 2
    own = xs_ref.shape[-1]
    wide = 2 * state
    span = tok_ref.shape[1]

    def norm(value):
        value = value.astype(F32)
        rstd = lax.rsqrt(jnp.mean(value * value, axis=-1, keepdims=True) + EPS)
        return (value * rstd * gain_ref[...]).astype(BF), rstd

    normed, rstd = norm(tok_ref[0])
    normed_ref[0] = normed
    room = jnp.zeros((EDGE - halo_ref.shape[1], halo_ref.shape[2]), F32)
    ahead = jnp.concatenate([room, norm(halo_ref[0])[0].astype(F32)], axis=0).astype(BF)
    rows = jnp.concatenate([ahead, normed], axis=0)
    pre_x = dot(rows, w_ref[0]).astype(BF)
    small = dot(rows, w_small_ref[...])
    pre_bc = small[:, :wide].astype(BF)
    dt_raw = small[EDGE:, wide:]

    seg = jnp.transpose(jnp.broadcast_to(seg_ref[0, 0:1], (LANES, LANES + span)))[LANES - EDGE :]
    here = seg[EDGE:]
    lane = lax.broadcasted_iota(jnp.int32, here.shape, 1)
    columns = [(back_rows(seg, 3 - tap)[EDGE:] == here).astype(F32) for tap in range(3)]
    columns.append((here == here[-1:]).astype(F32))
    columns.append((here == seg[EDGE - 1 : EDGE]).astype(F32))
    columns.append(here)
    columns.append(jnp.broadcast_to(rstd, here.shape))
    aux = jnp.zeros(here.shape, F32)
    for at, column in enumerate(columns):
        aux = jnp.where(lane == at, column, aux)
    aux_ref[0] = aux

    dt_ref[0] = dt_raw
    pre_x_ref[0] = pre_x[EDGE:]
    halo_x_ref[0] = pre_x[:EDGE]
    pre_bc_ref[0] = pre_bc[EDGE:]
    halo_bc_ref[0] = pre_bc[:EDGE]
    conv = conv_rows(pre_bc.astype(F32), aux, conv_bc_ref[...])
    bc = (conv * sigmoid(conv)).astype(BF)
    bc_ref[0] = bc
    conv = conv_rows(pre_x.astype(F32), aux, conv_x_ref[...])
    x = (conv * sigmoid(conv)).astype(BF)
    x_ref[0] = x
    x_float = x.astype(F32)
    step = softplus(dt_raw + head_ref[0:1])
    cum = running(-head_ref[1:2] * step, True)
    cum_ref[0] = cum
    expand = expand_ref[...]
    xs_ref[0] = (x_float * widen(step, expand)).astype(BF)
    last = cum[-1:]
    tail_step = jnp.exp(last - cum) * aux[:, 3:4] * step
    loaded = (x_float * widen(tail_step, expand)).astype(BF)
    own_state = dot(bc[:, :state], loaded, ((0,), (0,)))
    low, high = own_state[:half], own_state[half:]
    at = pl.ds(pl.multiple_of(s * half, half), half)
    keep_ref[at] = jnp.where(odd == 0, low, high).astype(BF)
    send_ref[at] = jnp.where(odd == 0, high, low).astype(BF)

    decay = jnp.broadcast_to(jnp.exp(last) * aux[-1:, 4:5], (8, LANES))
    decay_wide = widen(decay, expand)[:1]
    high = decay_wide.astype(BF).astype(F32)
    places = lax.broadcasted_iota(jnp.int32, (ROWS, 1), 0)
    extra = jnp.where(places == s, high, 0.0) + jnp.where(
        places == s + seqs, decay_wide - high, 0.0
    )
    end = pl.ds(seqs * half, ROWS)

    @pl.when(s == 0)
    def _():
        keep_ref[end] = extra.astype(BF)

    @pl.when(s > 0)
    def _():
        keep_ref[end] = (keep_ref[end].astype(F32) + extra).astype(BF)

    @pl.when(s == seqs - 1)
    def _():
        send_ref[end] = keep_ref[end]


def pair_kernel(seqs, groups, half, me_ref, mine_ref, other_ref, *rest):
    outs, decay_ref, scratch = rest[:groups], rest[groups], rest[groups + 1]
    odd, place = me_ref[0] % 2, me_ref[0] // 2
    end = seqs * half
    packed = [ref[end : end + ROWS].astype(F32) for ref in (mine_ref, other_ref)]
    mine, other = [p[:seqs] + p[seqs : 2 * seqs] for p in packed]
    first = jnp.where(odd == 0, mine, other)
    second = jnp.where(odd == 0, other, mine)
    decay_ref[0:seqs] = first
    decay_ref[8 : 8 + seqs] = second
    both = first * second
    high = both.astype(BF).astype(F32)
    room = jnp.zeros((ROWS - 2 * seqs, both.shape[1]), F32)
    extra = jnp.concatenate([high, both - high, room], axis=0)
    width = scratch.shape[3]
    across, _ = chunk_grid(groups, half, both.shape[1])
    for j in range(groups):
        b = j % across
        scratch[j, seqs] = extra[:, b * width : (b + 1) * width].astype(BF)
    for s in range(seqs):
        rows = slice(s * half, (s + 1) * half)
        mine, other = mine_ref[rows].astype(F32), other_ref[rows].astype(F32)
        early = jnp.where(odd == 0, mine, other)
        late = jnp.where(odd == 0, other, mine)
        cut(second[s : s + 1] * early + late, scratch, s, groups)
    for m in range(groups):
        outs[m][...] = scratch[place ^ m]


def pair_back_kernel(seqs, groups, half, me_ref, mine_ref, other_ref, decay_ref, *rest):
    outs, scratch = rest[:groups], rest[groups]
    odd, place = me_ref[0] % 2, me_ref[0] // 2
    for s in range(seqs):
        rows = slice(s * half, (s + 1) * half)
        mine, other = mine_ref[rows].astype(F32), other_ref[rows].astype(F32)
        early = jnp.where(odd == 0, mine, other)
        late = jnp.where(odd == 0, other, mine)
        cut(decay_ref[s : s + 1] * late + early, scratch, s, groups)
    for m in range(groups):
        outs[m][...] = scratch[place ^ m]


def scan_kernel(seqs, groups, me_ref, *rest):
    ins, outs = rest[:groups], rest[groups : 2 * groups]
    decay_ref, scratch = rest[2 * groups], rest[2 * groups + 1]
    place = me_ref[0] // 2
    for m in range(groups):
        scratch[place ^ m] = ins[m][...]
    for s in range(seqs):
        entry = jnp.zeros(scratch.shape[2:], F32)
        for k in range(groups):
            packed = scratch[k, seqs].astype(F32)
            decay = packed[s : s + 1] + packed[s + seqs : s + seqs + 1]
            decay_ref[k, s : s + 1] = decay
            arrived = scratch[k, s].astype(F32)
            scratch[k, s] = entry.astype(BF)
            entry = decay * entry + arrived
    for m in range(groups):
        outs[m][...] = scratch[place ^ m, :seqs]


def scan_back_kernel(seqs, groups, me_ref, decay_ref, *rest):
    ins, outs, scratch = rest[:groups], rest[groups : 2 * groups], rest[2 * groups]
    place = me_ref[0] // 2
    for m in range(groups):
        scratch[place ^ m] = ins[m][...]
    for s in range(seqs):
        leave = jnp.zeros(scratch.shape[2:], F32)
        for k in reversed(range(groups)):
            arrived = scratch[k, s].astype(F32)
            scratch[k, s] = leave.astype(BF)
            leave = decay_ref[k, s : s + 1] * leave + arrived
    for m in range(groups):
        outs[m][...] = scratch[place ^ m]


def unpair_kernel(seqs, groups, half, forward, me_ref, mine_ref, other_ref, decay_ref, *rest):
    ins, (own_ref, send_ref, scratch) = rest[:groups], rest[groups:]
    odd, place = me_ref[0] % 2, me_ref[0] // 2
    own = own_ref.shape[-1]
    for m in range(groups):
        scratch[place ^ m] = ins[m][...]
    is_first = (odd == 0) if forward else (odd == 1)
    for s in range(seqs):
        rows = slice(s * half, (s + 1) * half)
        entry = uncut(scratch, s, groups, half, own).astype(F32)
        mine, other = mine_ref[rows].astype(F32), other_ref[rows].astype(F32)
        first = jnp.where(is_first, mine, other)
        at = s if forward else 8 + s
        later = decay_ref[at : at + 1] * entry + first
        own_ref[s] = jnp.where(is_first, entry, later).astype(BF)
        send_ref[s] = jnp.where(is_first, later, entry).astype(BF)


def inner_kernel(state, bc_ref, xs_ref, cum_ref, aux_ref, seg_ref, out_ref):
    own = xs_ref.shape[-1]
    b_ssm, c_ssm = bc_ref[0, :, :state], bc_ref[0, :, state:]
    cum = cum_ref[0]
    cum_t = jnp.transpose(cum)
    mask = doc_mask(aux_ref[0, :, 5:6], seg_ref[0, 0:1, LANES:], True)
    scores = dot(c_ssm, b_ssm, ((1,), (1,))) * mask
    left = lax.broadcasted_iota(jnp.int32, (1, LANES), 1) < HEAD_DIM
    for pair in range(own // LANES):
        lanes = slice(pair * LANES, (pair + 1) * LANES)
        xs = xs_ref[0, :, lanes].astype(F32)
        total = None
        for side in range(2):
            h = 2 * pair + side
            lag = jnp.minimum(cum[:, h : h + 1] - cum_t[h : h + 1], 0.0)
            weights = (scores * jnp.exp(lag)).astype(BF)
            own_xs = jnp.where(left if side == 0 else ~left, xs, 0.0).astype(BF)
            term = dot(weights, own_xs)
            total = term if total is None else total + term
        out_ref[0, :, lanes] = total


def mixer_out(state, states, x_ref, bc_ref, inner_ref, gate_ref, cum_ref, aux_ref, rows_ref, expand_ref):
    c_ssm = bc_ref[0, :, state:]
    x_float = x_ref[0].astype(F32)
    entry_wide = widen(jnp.exp(cum_ref[0]) * aux_ref[0, :, 4:5], expand_ref[...])
    mixed = inner_ref[0] + dot(c_ssm, states) * entry_wide
    y = mixed + rows_ref[1:2] * x_float
    gate = gate_ref[0].astype(F32)
    sig = sigmoid(gate)
    return mixed, y, x_float, gate, sig, entry_wide


def sums_kernel(
    state, me_ref, x_ref, bc_ref, inner_ref, gate_ref, e_ref, cum_ref, aux_ref, mine_ref,
    other_ref, rows_ref, expand_ref, out_ref
):
    states = both_halves(me_ref[0], mine_ref, other_ref)
    _, y, _, gate, sig, _ = mixer_out(
        state, states, x_ref, bc_ref, inner_ref, gate_ref, cum_ref, aux_ref, rows_ref, expand_ref
    )
    gated = y * (gate * sig)
    squares = jnp.sum(gated * gated, axis=-1, keepdims=True)
    dots = jnp.sum(e_ref[0].astype(F32) * (gated * rows_ref[0:1]), axis=-1, keepdims=True)
    place = lax.broadcasted_iota(jnp.int32, (8, 1), 0)
    out_ref[0] = jnp.where(place == 0, to_row(squares), jnp.where(place == 1, to_row(dots), 0.0))


def gate_back_kernel(
    state, inner_total, me_ref, x_ref, bc_ref, inner_ref, gate_ref, e_ref, cum_ref, aux_ref,
    mine_ref, other_ref, rows_ref, expand_ref, sums_ref, scaled_ref, dz_ref, dy_ref, mixed_ref,
    dc_ref, dot_ref, grad_ref, keep_ref, send_ref
):
    s = pl.program_id(0)
    odd = me_ref[0] % 2
    half = state // 2
    expand = expand_ref[...]
    states = both_halves(me_ref[0], mine_ref, other_ref)
    mixed, y, x_float, gate, sig, entry_wide = mixer_out(
        state, states, x_ref, bc_ref, inner_ref, gate_ref, cum_ref, aux_ref, rows_ref, expand_ref
    )
    columns = jnp.transpose(
        jnp.concatenate([sums_ref[0], jnp.zeros((LANES - 8, sums_ref.shape[2]), F32)], axis=0)
    )
    rstd = lax.rsqrt(columns[:, 0:1] / inner_total + EPS)
    slope = columns[:, 1:2] * (rstd * rstd * rstd) / inner_total
    gain = rows_ref[0:1]
    silu = gate * sig
    gated = y * silu
    scaled_ref[0] = (gated * gain * rstd).astype(BF)
    d_scaled = e_ref[0].astype(F32) * rstd
    d_gated = d_scaled * gain - slope * gated
    d_y = d_gated * silu
    dy_ref[0] = d_y.astype(BF)
    d_z = (d_gated * y * (sig * (1.0 + gate * (1.0 - sig)))).astype(BF)
    dz_ref[0] = d_z
    row = jnp.sum(d_z.astype(F32) * gate, axis=-1, keepdims=True)
    dot_ref[0] = to_row(row)
    mixed_ref[0] = per_head(d_y * mixed, expand)

    @pl.when(s == 0)
    def _():
        grad_ref[...] = jnp.zeros_like(grad_ref)

    grad_ref[5:6] += jnp.sum(d_scaled * gated, axis=0, keepdims=True)
    grad_ref[6:7] += jnp.sum(d_y * x_float, axis=0, keepdims=True)
    d_carried = (d_y * entry_wide).astype(BF)
    dc_ref[0] = dot(d_carried, states, ((1,), (1,)))
    grad = dot(bc_ref[0, :, state:], d_carried, ((0,), (0,)))
    low, high = grad[:half], grad[half:]
    at = pl.ds(pl.multiple_of(s * half, half), half)
    keep_ref[at] = jnp.where(odd == 0, low, high).astype(BF)
    send_ref[at] = jnp.where(odd == 0, high, low).astype(BF)


def inner_back_kernel(
    state, x_ref, bc_ref, xs_ref, dy_ref, dc_ref, cum_ref, dt_ref, aux_ref, seg_ref, rows_ref,
    head_ref, expand_ref, dx_ref, dstep_ref, dbc_ref
):
    own = xs_ref.shape[-1]
    b_ssm, c_ssm = bc_ref[0, :, :state], bc_ref[0, :, state:]
    cum = cum_ref[0]
    cum_t = jnp.transpose(cum)
    nt = ((1,), (1,))
    mask = doc_mask(aux_ref[0, :, 5:6], seg_ref[0, 0:1, LANES:], False)
    scores = dot(b_ssm, c_ssm, nt) * mask
    left = lax.broadcasted_iota(jnp.int32, (1, LANES), 1) < HEAD_DIM
    d_scores = None
    sums = []
    for pair in range(own // LANES):
        lanes = slice(pair * LANES, (pair + 1) * LANES)
        xs = xs_ref[0, :, lanes]
        dy = dy_ref[0, :, lanes].astype(F32)
        total = None
        for side in range(2):
            h = 2 * pair + side
            lag = jnp.minimum(cum_t[h : h + 1] - cum[:, h : h + 1], 0.0)
            mixing = jnp.exp(lag)
            weights = (scores * mixing).astype(BF)
            own_dy = jnp.where(left if side == 0 else ~left, dy, 0.0).astype(BF)
            term = dot(weights, own_dy)
            total = term if total is None else total + term
            d_mixed = dot(xs, own_dy, nt) * mixing
            d_scores = d_mixed if d_scores is None else d_scores + d_mixed
        sums.append(total)
    back = jnp.concatenate(sums, axis=1)
    expand = expand_ref[...]
    x_float = x_ref[0].astype(F32)
    dstep_ref[0] = per_head(x_float * back, expand)
    step = softplus(dt_ref[0] + head_ref[0:1])
    dy_all = dy_ref[0].astype(F32)
    dx_ref[0] = (back * widen(step, expand) + rows_ref[1:2] * dy_all).astype(BF)
    d_scores = (d_scores * mask).astype(BF)
    dbc_ref[0, :, :state] = dot(d_scores, c_ssm)
    dbc_ref[0, :, state:] = dot(d_scores, b_ssm, ((0,), (0,))) + dc_ref[0]


def leave_kernel(
    state, me_ref, x_ref, bc_ref, pre_ref, halo_ref, pre_bc_ref, halo_bc_ref, dx_ref, dstep_ref,
    dbc_ref, mixed_ref, cum_ref, dt_ref, aux_ref, dot_z_ref, mine_ref, other_ref, end_mine_ref,
    end_other_ref, conv_ref, conv_bc_ref, head_ref, expand_ref, dpre_ref, back_ref, back_bc_ref,
    dbc_out_ref, ddt_ref, dot_ref, grad_ref, small_ref
):
    me = me_ref[0]
    own = dx_ref.shape[-1]
    expand = expand_ref[...]
    states = both_halves(me, mine_ref, other_ref)
    ends = both_halves(me, end_mine_ref, end_other_ref)
    b_ssm = bc_ref[0, :, :state]
    x_float = x_ref[0].astype(F32)
    aux = aux_ref[0]
    dt_pre = dt_ref[0] + head_ref[0:1]
    step = softplus(dt_pre)
    rate = head_ref[1:2]
    cum = cum_ref[0]
    last = cum[-1:]
    tail_decay = jnp.exp(last - cum) * aux[:, 3:4]
    tail_step = tail_decay * step
    tail_wide = widen(tail_step, expand)
    loaded = (x_float * tail_wide).astype(BF)
    d_loaded = dot(b_ssm, ends)
    dbc_out_ref[0, :, :state] = (dbc_ref[0, :, :state] + dot(loaded, ends, ((1,), (1,)))).astype(BF)
    dbc_out_ref[0, :, state:] = dbc_ref[0, :, state:].astype(BF)
    d_bc = dbc_out_ref[0, :EDGE].astype(F32)
    extended = jnp.concatenate([halo_bc_ref[0], pre_bc_ref[0, :EDGE]], axis=0).astype(F32)
    weight = conv_bc_ref[...]
    conv = conv_rows(extended, aux[:EDGE], weight)
    sig = sigmoid(conv)
    d_conv = d_bc * (sig * (1.0 + conv * (1.0 - sig)))
    back_bc_ref[0] = conv_back_rows(d_conv, extended, aux[:EDGE], weight)[:EDGE].astype(BF)
    d_x = dx_ref[0].astype(F32) + d_loaded * tail_wide
    d_tail = per_head(d_loaded * x_float, expand)
    end_terms = d_tail * tail_step
    product = jnp.sum(ends.astype(F32) * states.astype(F32), axis=0, keepdims=True)
    d_decay = per_head(jnp.broadcast_to(product, (8, own)), expand)[:1]
    block_decay = jnp.exp(last) * aux[-1:, 4:5]
    d_cum = mixed_ref[0] - step * dstep_ref[0] - end_terms
    last_add = jnp.sum(end_terms, axis=0, keepdims=True) + d_decay * block_decay
    d_log = running(d_cum, False) + last_add
    d_step = dstep_ref[0] + d_tail * tail_decay - d_log * rate
    d_dt = d_step * sigmoid(dt_pre)
    ddt_ref[0] = d_dt.astype(BF)

    @pl.when(pl.program_id(0) == 0)
    def _():
        grad_ref[...] = jnp.zeros_like(grad_ref)
        small_ref[...] = jnp.zeros_like(small_ref)

    small_ref[0:1] += jnp.sum(d_dt, axis=0, keepdims=True)
    small_ref[1:2] += jnp.sum(d_log * (-rate * step), axis=0, keepdims=True)

    extended = jnp.concatenate([halo_ref[0], pre_ref[0]], axis=0).astype(F32)
    weight = conv_ref[...]
    conv = conv_rows(extended, aux, weight)
    sig = sigmoid(conv)
    d_conv = d_x * (sig * (1.0 + conv * (1.0 - sig)))
    d_ext = conv_back_rows(d_conv, extended, aux, weight, grad_ref)
    d_pre = d_ext[EDGE:].astype(BF)
    dpre_ref[0] = d_pre
    back_ref[0] = d_ext[:EDGE].astype(BF)
    row = jnp.sum(d_pre.astype(F32) * extended[EDGE:], axis=-1, keepdims=True)
    row = row + jnp.sum(ddt_ref[0].astype(F32) * dt_ref[0], axis=-1, keepdims=True)
    dot_ref[0] = to_row(row) + dot_z_ref[0]


def conv_bc_kernel(
    d_ref, pre_ref, halo_ref, aux_ref, ddt_ref, conv_ref, dpre_ref, dot_ref, grad_ref
):
    span = pre_ref.shape[1]
    extended = jnp.concatenate([halo_ref[0], pre_ref[0]], axis=0).astype(F32)
    aux = aux_ref[0]
    weight = conv_ref[...]
    conv = conv_rows(extended, aux, weight)
    sig = sigmoid(conv)
    d_conv = d_ref[0, :span].astype(F32) * (sig * (1.0 + conv * (1.0 - sig)))

    @pl.when(pl.program_id(0) == 0)
    def _():
        grad_ref[...] = jnp.zeros_like(grad_ref)

    d_pre = conv_back_rows(d_conv, extended, aux, weight, grad_ref)[EDGE:]
    ahead = d_ref[0, span : span + EDGE].astype(F32)
    d_pre = jnp.concatenate([d_pre[: span - EDGE], d_pre[span - EDGE :] + ahead], axis=0)
    d_pre = d_pre.astype(BF)
    dpre_ref[0, :, : d_pre.shape[1]] = d_pre
    dpre_ref[0, :, d_pre.shape[1] :] = ddt_ref[0]
    row = jnp.sum(d_pre.astype(F32) * extended[EDGE:], axis=-1, keepdims=True)
    packed = d_ref[0, span + EDGE :].astype(F32)
    dot_ref[0] = to_row(row) + (packed[0:1] + packed[1:2])


def gram_kernel(a_ref, b_ref, out_ref):
    out_ref[...] = dot(a_ref[...], b_ref[...], ((0,), (0,))).astype(BF)


def gram_pair_kernel(me_ref, a_ref, b_ref, odd_ref, even_ref):
    product = dot(a_ref[...], b_ref[...], ((0,), (0,))).astype(BF)
    tile = product.shape[0] // 2
    low, high = product[:tile], product[tile:]
    same = me_ref[0] % 2 == 0
    odd_ref[0] = jnp.where(same, high, low)
    even_ref[0] = jnp.where(same, low, high)


def share_kernel(terms, with_sum, me_ref, *refs):
    odd_ref, even_ref = refs[2 * terms + with_sum : 2 * terms + with_sum + 2]
    nt = ((1,), (1,))
    total = None
    for t in range(terms):
        rhs = refs[2 * t + 1]
        rhs = rhs[0] if len(rhs.shape) == 3 else rhs[...]
        term = dot(refs[2 * t][...], rhs, nt)
        total = term if total is None else total + term
    total_low = total.astype(BF)

    @pl.when(pl.program_id(0) < pl.num_programs(0) // 2)
    def _():
        odd_ref[0] = total_low

    @pl.when(pl.program_id(0) >= pl.num_programs(0) // 2)
    def _():
        even_ref[0] = total_low

    if with_sum:
        sum_ref = refs[-1]

        @pl.when(pl.program_id(1) == 0)
        def _():
            sum_ref[...] = jnp.zeros_like(sum_ref)

        normed = refs[2 * terms][...].astype(F32)
        sum_ref[0, 0:1] += jnp.sum(total * normed, axis=0, keepdims=True)


def per_seq(seqs, shape):
    zeros = (0,) * len(shape)
    return pl.BlockSpec((1, *shape), lambda s: (jnp.minimum(s, seqs - 1), *zeros))


def whole(shape):
    zeros = (0,) * len(shape)
    return pl.BlockSpec(tuple(shape), lambda s: zeros)


def call(body, grid, ins, in_specs, outs, out_specs, scratch, flops, name, aliases={}):
    return pl.pallas_call(
        body,
        grid=(grid,),
        in_specs=in_specs,
        out_specs=out_specs,
        out_shape=outs,
        scratch_shapes=scratch,
        name=name,
        input_output_aliases=aliases,
        compiler_params=pltpu.CompilerParams(vmem_limit_bytes=VMEM),
        cost_estimate=cost(flops),
    )(*ins)


def shaped(shape, dtype):
    return jax.ShapeDtypeStruct(tuple(shape), dtype)


def swap(value, axis, mask):
    count = lax.axis_size(axis)
    return lax.ppermute(value, axis, [(i, i ^ mask) for i in range(count)])


def shift(value, axis, steps):
    count = lax.axis_size(axis)
    leading, last = (max(0, -steps), min(count, count - steps))
    return lax.ppermute(value, axis, [(i, i + steps) for i in range(leading, last)])


def exchange(chunks, masks):
    return [swap(c, "seq", mask) if mask else c for c, mask in zip(chunks, masks)]


def after(value, *others):
    return lax.optimization_barrier((value, *others))[0]


def fold_step(sides, axis, mask):
    odd, even = sides
    arrived = swap(odd, axis, mask)
    if even.shape[0] == 1:
        return (even + arrived)[0]
    return even[1::2] + arrived[1::2], even[0::2] + arrived[0::2]


def fold(sides, axis, mask=1):
    while isinstance(sides, tuple):
        sides = fold_step(sides, axis, mask)
        mask *= 2
    return sides


def core_sum(odd, even):
    return even + swap(odd, "head", 1)


def pair_sides(full):
    odd = lax.axis_index("seq") % 2
    chunks = full.reshape(lax.axis_size("seq") // 2, 2, -1, full.shape[-1])
    return tuple(lax.dynamic_index_in_dim(chunks, at, 1, False) for at in (1 - odd, odd))


def pair_sum(sides):
    return sides[1] + swap(sides[0], "seq", 1)


def spread_sum(total):
    count = lax.axis_size("seq")
    return lax.psum_scatter(
        total.reshape(-1, total.shape[-1]),
        "seq",
        scatter_dimension=0,
        tiled=True,
        axis_index_groups=[[2 * z + x for z in range(count // 2)] for x in range(2)],
    )


def row_sides(full, axis):
    count = lax.axis_size(axis)
    me = lax.axis_index(axis)
    chunks = full.reshape(count, -1, full.shape[-1])

    def stacked(masks):
        return jnp.stack([lax.dynamic_index_in_dim(chunks, me ^ m, 0, False) for m in masks])

    return stacked(range(1, count, 2)), stacked(range(0, count, 2))


def sum_all(value, axis):
    mask = 1
    while mask < lax.axis_size(axis):
        value = value + swap(value, axis, mask)
        mask *= 2
    return value


def pad_lanes(value, width):
    return jnp.pad(value, ((0, 0), (0, width - value.shape[1])))


def pad_rows(rows, count=8):
    stacked = jnp.concatenate([r.reshape(-1, r.shape[-1]).astype(F32) for r in rows], axis=0)
    return jnp.pad(stacked, ((0, count - stacked.shape[0]), (0, 0)))


def local(
    tokens,
    segments,
    norm_gain,
    w_zx,
    w_bc,
    w_dt,
    conv_x,
    conv_x_bias,
    conv_bc,
    conv_bc_bias,
    dt_bias,
    a_log,
    d_skip,
    gate_gain,
    w_out,
    cotangent,
):
    seqs, span, model = tokens.shape
    rows = seqs * span
    heads = d_skip.shape[0]
    own = heads * HEAD_DIM
    n_seq, n_head = lax.axis_size("seq"), lax.axis_size("head")
    me_head = lax.axis_index("head")
    me = lax.axis_index("seq").astype(jnp.int32).reshape(1)
    head_at = me_head.astype(jnp.int32).reshape(1)
    inner_total = own * n_head
    state = w_bc.shape[1] // 2
    half = state // 2
    wide = 2 * state
    share = model // n_head
    offset = me_head * share
    edge = conv_x.shape[0] - 1
    groups = n_seq // 2
    masks = [2 * m for m in range(groups)]
    _, width = chunk_grid(groups, half, own)

    seg_lanes = jnp.broadcast_to(segments[:, -8:, None].astype(BF), (seqs, 8, LANES))
    halo = shift(jnp.concatenate([tokens[:, -8:], seg_lanes], axis=2), "seq", 1)
    tok_halo, seg_halo = halo[..., :model], halo[..., model]
    cot_full = lax.all_gather(cotangent, "head", axis=2, tiled=True)

    w_in = lax.optimization_barrier(jnp.transpose(w_zx, (1, 0, 2)))
    w_dt = pad_lanes(w_dt, LANES)
    w_small = jnp.concatenate([w_bc, w_dt], axis=1)
    seg_rows = [jnp.pad(seg_halo.astype(F32), ((0, 0), (LANES - 8, 0))), segments.astype(F32)]
    seg_rows = jnp.concatenate(seg_rows, axis=1)
    seg_rows = jnp.broadcast_to(seg_rows[:, None], (seqs, 8, LANES + span))
    conv_x_w = pad_rows([conv_x, conv_x_bias])
    conv_bc_w = pad_rows([conv_bc, conv_bc_bias])
    head_rows = pad_lanes(pad_rows([dt_bias, jnp.exp(a_log)]), LANES)
    wide_rows = pad_rows([gate_gain, jnp.repeat(d_skip, HEAD_DIM)])
    expand = (
        jnp.arange(LANES)[:, None] == (jnp.arange(own) // HEAD_DIM)[None, :]
    ).astype(BF)

    seq = functools.partial(per_seq, seqs)

    def seq_of(values):
        return [seq(v.shape[1:]) for v in values]

    def whole_of(values):
        return [whole(v.shape) for v in values]

    w_x_spec = pl.BlockSpec((1, model, own), lambda s: (1, 0, 0))
    ins = (
        me, tokens, tok_halo, norm_gain.reshape(1, model), w_in, w_small, seg_rows, conv_x_w,
        conv_bc_w, head_rows, expand,
    )
    per = (
        shaped((seqs, span, model), BF),
        shaped((seqs, span, own), BF),
        shaped((seqs, span, wide), BF),
        shaped((seqs, EDGE, own), BF),
        shaped((seqs, EDGE, wide), BF),
        shaped((seqs, span, own), BF),
        shaped((seqs, span, wide), BF),
        shaped((seqs, span, own), BF),
        shaped((seqs, span, LANES), F32),
        shaped((seqs, span, LANES), F32),
        shaped((seqs, span, LANES), F32),
    )
    packed = (shaped((seqs * half + ROWS, own), BF),) * 2
    normed, pre_x, pre_bc, halo_x, halo_bc, x_ssm, bc_ssm, xs, dt_raw, cum, aux, keep, send = call(
        functools.partial(front_kernel, state),
        seqs,
        ins,
        [SMEM_SPEC, *seq_of(ins[1:3]), whole(ins[3].shape), w_x_spec, whole(w_small.shape)]
        + seq_of(ins[6:7])
        + whole_of(ins[7:]),
        per + packed,
        seq_of(per) + whole_of(packed),
        [],
        30,
        "front",
    )

    def small_call(body, ins, outs, blocks, name):
        return call(
            body,
            1,
            ins,
            [SMEM_SPEC] + whole_of(ins[1:]),
            outs,
            whole_of(outs),
            [pltpu.VMEM((groups, blocks, ROWS, width), BF)],
            3,
            name,
        )

    piece = shaped((seqs, ROWS, width), BF)
    halves_out = (shaped((seqs, half, own), BF),) * 2
    other = swap(send, "seq", 1)
    *parts, pair_decay = small_call(
        functools.partial(pair_kernel, seqs, groups, half),
        (me, keep, other),
        (shaped((seqs + 1, ROWS, width), BF),) * groups + (shaped((16, own), F32),),
        seqs + 1,
        "pair",
    )
    *entries, decays = small_call(
        functools.partial(scan_kernel, seqs, groups),
        (me, *exchange(parts, masks)),
        (piece,) * groups + (shaped((groups, 8, width), F32),),
        seqs + 1,
        "scan",
    )
    state_mine, state_send = small_call(
        functools.partial(unpair_kernel, seqs, groups, half, True),
        (me, keep, other, pair_decay, *exchange(entries, masks)),
        halves_out,
        seqs,
        "unpair",
    )
    state_other = swap(state_send, "seq", 1)

    gate = dot(normed, w_in[0], ((2,), (0,))).astype(BF)
    e_raw = dot(cot_full, w_out, ((2,), (0,))).astype(BF)
    ins = (bc_ssm, xs, cum, aux, seg_rows)
    (inner,) = call(
        functools.partial(inner_kernel, state),
        seqs,
        ins,
        seq_of(ins),
        (shaped((seqs, span, own), F32),),
        [seq((span, own))],
        [],
        10.3,
        "inner",
    )

    mixer = (me, x_ssm, bc_ssm, inner, gate, e_raw, cum, aux, state_mine, state_other, wide_rows, expand)
    mixer_specs = [SMEM_SPEC] + seq_of(mixer[1:10]) + whole_of(mixer[10:])
    (sums,) = call(
        functools.partial(sums_kernel, state),
        seqs,
        mixer,
        mixer_specs,
        (shaped((seqs, 8, span), F32),),
        [seq((8, span))],
        [],
        12,
        "sums",
    )
    sums = sum_all(sums, "head")

    per = (
        shaped((seqs, span, own), BF),
        shaped((seqs, span, own), BF),
        shaped((seqs, span, own), BF),
        shaped((seqs, span, LANES), F32),
        shaped((seqs, span, state), F32),
        shaped((seqs, 8, span), F32),
    )
    fixed = (shaped((8, own), F32),) + (shaped((seqs * half, own), BF),) * 2
    scaled, d_z, d_y, mixed, d_c, dot_z, gate_grads, keep, send = call(
        functools.partial(gate_back_kernel, state, inner_total),
        seqs,
        (*mixer, sums),
        mixer_specs + [seq((8, span))],
        per + fixed,
        seq_of(per) + whole_of(fixed),
        [],
        21,
        "gate_back",
    )

    other = swap(send, "seq", 1)

    normed_rows = normed.reshape(rows, model)

    def gram(left, values):
        tile = 4 * LANES
        return call(
            gram_kernel,
            model // tile,
            (left, values),
            [pl.BlockSpec((rows, tile), lambda i: (0, i)), whole(values.shape)],
            (shaped((model, values.shape[1]), BF),),
            [pl.BlockSpec((tile, values.shape[1]), lambda i: (i, 0))],
            [],
            10.8,
            "gram",
        )[0]

    def chunk_pair(left, values, natural):
        tile = model // n_seq
        if tile % LANES:
            full = dot(left, values, ((0,), (0,))).astype(BF)
            return pair_sides(full) if natural else row_sides(full, "seq")
        block = (tile, values.shape[1])

        def at(i, me_ref):
            return i if natural else i ^ (me_ref[0] // 2)

        return tuple(
            pl.pallas_call(
                gram_pair_kernel,
                grid_spec=pltpu.PrefetchScalarGridSpec(
                    num_scalar_prefetch=1,
                    grid=(groups,),
                    in_specs=[
                        pl.BlockSpec((rows, 2 * tile), lambda i, me_ref: (0, at(i, me_ref))),
                        pl.BlockSpec(values.shape, lambda i, me_ref: (0, 0)),
                    ],
                    out_specs=[pl.BlockSpec((1, *block), lambda i, me_ref: (i, 0, 0))] * 2,
                ),
                out_shape=[shaped((groups, *block), BF)] * 2,
                name="gram_pair",
                compiler_params=pltpu.CompilerParams(vmem_limit_bytes=VMEM),
                cost_estimate=cost(rows * model * values.shape[1] / 3e8),
            )(me, left, values)
        )

    def share_sum(terms, parity, summed):
        pairs = n_head // 2
        quads = pairs // 2
        tall = rows
        def at(i, head_ref):
            core = 1 - i // quads
            return (4 * (i % quads) + 2 * parity + core) ^ head_ref[0]

        ins, specs = [], []
        for lhs, rhs, first in terms:
            ins += [lhs, rhs]
            specs.append(pl.BlockSpec((tall, lhs.shape[1]), lambda i, s, head_ref: (s, 0)))
            if rhs.ndim == 3:
                specs.append(
                    pl.BlockSpec(
                        (1, share, rhs.shape[2]),
                        lambda i, s, head_ref, first=first: (first, at(i, head_ref), 0),
                    )
                )
            else:
                specs.append(
                    pl.BlockSpec(
                        (share, rhs.shape[1]), lambda i, s, head_ref: (at(i, head_ref), 0)
                    )
                )
        out_specs = [
            pl.BlockSpec(
                (1, tall, share), lambda i, s, head_ref: (jnp.minimum(i, quads - 1), s, 0)
            ),
            pl.BlockSpec(
                (1, tall, share), lambda i, s, head_ref: (jnp.maximum(i - quads, 0), s, 0)
            ),
        ]
        outs = [shaped((quads, rows, share), BF)] * 2
        if summed:
            ins.append(normed_rows)
            specs.append(
                pl.BlockSpec((tall, share), lambda i, s, head_ref: (s, at(i, head_ref)))
            )
            out_specs.append(pl.BlockSpec((1, 8, share), lambda i, s, head_ref: (i, 0, 0)))
            outs.append(shaped((pairs, 8, share), F32))
        depth = sum(t[0].shape[1] for t in terms)
        got = pl.pallas_call(
            functools.partial(share_kernel, len(terms), summed),
            grid_spec=pltpu.PrefetchScalarGridSpec(
                num_scalar_prefetch=1,
                grid=(pairs, rows // tall),
                in_specs=specs,
                out_specs=out_specs,
            ),
            out_shape=outs,
            name="shares",
            compiler_params=pltpu.CompilerParams(vmem_limit_bytes=VMEM),
            cost_estimate=cost(rows * model * depth / 5e8),
        )(head_at, *ins)
        return (got[:2], got[2]) if summed else got

    scaled_rows, d_z_rows = scaled.reshape(rows, own), d_z.reshape(rows, own)
    out_grad = chunk_pair(cot_full.reshape(rows, model), scaled_rows, True)
    out_far = share_sum([(after(scaled_rows, out_grad[1]), w_out, 0)], 1, False)
    parts = small_call(
        functools.partial(pair_back_kernel, seqs, groups, half),
        (me, after(keep, out_far[1]), other, pair_decay),
        (piece,) * groups,
        seqs,
        "pair_back",
    )
    arrived = exchange(parts, masks)
    ins = (
        x_ssm, bc_ssm, xs, after(d_y, parts[0]), d_c, cum, dt_raw, aux, seg_rows, wide_rows, head_rows, expand,
    )
    per = (
        shaped((seqs, span, own), BF),
        shaped((seqs, span, LANES), F32),
        shaped((seqs, span, wide), F32),
    )
    d_x, d_step, d_bc = call(
        functools.partial(inner_back_kernel, state),
        seqs,
        ins,
        seq_of(ins[:9]) + whole_of(ins[9:]),
        per,
        seq_of(per),
        [],
        18.6,
        "inner_back",
    )

    leaves = small_call(
        functools.partial(scan_back_kernel, seqs, groups),
        (me, after(decays, d_x), *arrived),
        (piece,) * groups,
        seqs,
        "scan_back",
    )
    arrived = exchange(leaves, masks)
    gate_grad = gram(normed_rows, after(d_z_rows, leaves[0]))
    end_mine, end_send = small_call(
        functools.partial(unpair_kernel, seqs, groups, half, False),
        (me, after(keep, gate_grad), other, pair_decay, *arrived),
        halves_out,
        seqs,
        "unpair_back",
    )
    end_other = swap(end_send, "seq", 1)
    gate_total = spread_sum(gate_grad).reshape(2, -1, own)
    gate_total = spread_sum(gate_grad).reshape(2, -1, own)
    out_odd = share_sum([(after(scaled_rows, end_mine), w_out, 0)], 1, False)
    out_even = share_sum([(after(scaled_rows, out_odd), w_out, 0)], 0, False)

    out_total = pair_sum((out_grad[0], after(out_grad[1], end_mine)))
    ins = (
        me, after(x_ssm, out_total), bc_ssm, pre_x, halo_x, pre_bc, halo_bc, d_x, d_step, d_bc, mixed, cum,
        dt_raw, aux, dot_z, state_mine, state_other, end_mine, end_other, conv_x_w, conv_bc_w,
        head_rows, expand,
    )
    per = (
        shaped((seqs, span, own), BF),
        shaped((seqs, EDGE, own), BF),
        shaped((seqs, EDGE, wide), BF),
        shaped((seqs, span, wide), BF),
        shaped((seqs, span, LANES), BF),
        shaped((seqs, 8, span), F32),
    )
    fixed = (shaped((8, own), F32), shaped((8, LANES), F32))
    d_x_pre, back_x, back_bc, d_bc, d_dt, row_dot, conv_grads, head_grads = call(
        functools.partial(leave_kernel, state),
        seqs,
        ins,
        [SMEM_SPEC] + seq_of(ins[1:19]) + whole_of(ins[19:]),
        per + fixed,
        seq_of(per) + whole_of(fixed),
        [],
        28,
        "leave",
    )
    out_near = share_sum([(after(scaled_rows, d_x_pre), w_out, 0)], 0, False)
    out_far = core_sum(out_far[0], after(out_far[1], out_near[1]))
    back = shift(jnp.concatenate([back_x, back_bc], axis=2)[:, -edge:], "seq", -1)
    back = after(back, out_near[1])
    back_x, back_bc = back[..., :own], back[..., own:]
    fix = jnp.sum(back_x.astype(F32) * pre_x[:, -edge:].astype(F32), axis=-1)
    row_dot = row_dot[:, 0] + jnp.pad(fix, ((0, 0), (span - edge, 0)))
    dot_high = row_dot.astype(BF)
    dot_low = (row_dot - dot_high.astype(F32)).astype(BF)
    dots = jnp.pad(jnp.stack([dot_high, dot_low], axis=1), ((0, 0), (0, EDGE - 2), (0, 0)))
    back_bc = jnp.pad(back_bc, ((0, 0), (EDGE - edge, 0), (0, 0)))
    d_bc = jnp.concatenate([d_bc, back_bc, dots], axis=1)
    d_bc = d_bc + swap(d_bc, "head", 1)
    d_x_pre = after(d_x_pre, d_bc, out_far).at[:, -edge:].add(back_x)
    d_x_rows = d_x_pre.reshape(rows, own)
    d_dt_rows = d_dt.reshape(rows, LANES)
    late_sides = chunk_pair(normed_rows, d_x_rows, True)

    core, middle = me_head % 2, seqs // 2
    part = lax.dynamic_slice_in_dim(d_bc, core * middle, middle, 0)
    mask = 2
    while mask < n_head:
        part = part + swap(part, "head", mask)
        mask *= 2
    part = after(part, late_sides[1])
    part_other = swap(part, "head", 1)
    d_bc_all = jnp.where(
        core == 0,
        jnp.concatenate([part, part_other], axis=0),
        jnp.concatenate([part_other, part], axis=0),
    )
    ins = (d_bc_all, pre_bc, halo_bc, aux, d_dt, conv_bc_w)
    per = (shaped((seqs, span, wide + LANES), BF), shaped((seqs, 8, span), F32))
    d_small, row_dot, bc_grads = call(
        conv_bc_kernel,
        seqs,
        ins,
        seq_of(ins[:5]) + whole_of(ins[5:]),
        per + (shaped((8, wide), F32),),
        seq_of(per) + [whole((8, wide))],
        [],
        6.3,
        "conv_bc",
    )
    small_sides = chunk_pair(normed_rows, d_small.reshape(rows, -1), False)
    out_near = core_sum(out_near[0], after(out_near[1], d_small))
    terms = [(after(d_z_rows, small_sides[1], out_near), w_in, 0), (d_x_rows, w_in, 1)]
    terms.append((d_dt_rows, w_dt, 0))
    grad_far, norm_far = share_sum(terms, 1, True)
    late_total = pair_sum((late_sides[0], after(late_sides[1], grad_far[1])))
    grad_far = core_sum(grad_far[0], after(grad_far[1], late_total))
    own_sum = fold((out_far, after(out_near, grad_far)), "head", 2)
    own_sum = own_sum.reshape(seqs, span, share)
    terms[0] = (after(d_z_rows, grad_far), w_in, 0)
    grad_near, norm_near = share_sum(terms, 0, True)
    grad_near = core_sum(grad_near[0], after(grad_near[1], own_sum))
    small_next = fold_step((small_sides[0], after(small_sides[1], grad_near)), "seq", 1)
    tokens_own = lax.dynamic_slice_in_dim(tokens, offset, share, 2).astype(F32)
    layer_out = (tokens_own + own_sum.astype(F32)).astype(BF)
    own_grad = fold((grad_far, grad_near), "head", 2).reshape(seqs, span, share).astype(F32)
    late_s = fold(small_next, "seq", 2).astype(F32)
    out_grad_own = spread_sum(out_total).astype(F32)
    x_at = lax.axis_index("seq") % 2
    gate_own = lax.dynamic_index_in_dim(gate_total, x_at, 0, False)
    gate_sent = lax.dynamic_index_in_dim(gate_total, 1 - x_at, 0, False)
    gate_grad_own = (gate_own + swap(gate_sent, "seq", 1)).astype(F32)
    late_a = spread_sum(late_total).astype(F32)

    row_dot = row_dot[:, 0]
    w_bc_own = pad_lanes(lax.dynamic_slice_in_dim(w_bc, offset, share, 0), wide + LANES)
    bc_term = dot(d_small, w_bc_own, ((2,), (1,)))
    rstd_in = aux[:, :, 6:7]
    unit_own = tokens_own * rstd_in
    gain_own = lax.dynamic_slice_in_dim(norm_gain, offset, share, 0)
    d_unit = (own_grad + bc_term) * gain_own
    input_grad = (
        rstd_in * (d_unit - unit_own * (row_dot / model)[..., None]) + cotangent.astype(F32)
    ).astype(BF)

    taps = edge + 1
    quads = n_head // 4
    norm_odd, norm_even = [
        jnp.stack([norm_near[at, 0], norm_far[at, 0]], axis=1).reshape(-1, share)
        for at in (slice(0, quads), slice(quads, 2 * quads))
    ]
    norm_even = norm_even.at[0].add(gain_own * jnp.sum(bc_term * unit_own, axis=(0, 1)))
    narrow = jnp.concatenate([norm_odd, norm_even, jnp.zeros((8 - 4 * quads, share), F32)], axis=0)
    narrow = jnp.concatenate([bc_grads, head_grads, narrow], axis=1)
    wide_sums = conv_grads + gate_grads
    lanes = max(own, narrow.shape[1])
    sums = sum_all(
        jnp.concatenate([pad_lanes(wide_sums, lanes), pad_lanes(narrow, lanes)], axis=0), "seq"
    )
    norm_sums = sums[8 : 8 + 4 * quads, wide + LANES : wide + LANES + share]
    g_norm = fold((norm_sums[: 2 * quads], norm_sums[2 * quads :]), "head") / gain_own
    summed = (
        sums[:taps, :own],
        sums[taps, :own],
        sums[8 : 8 + taps, :wide],
        sums[8 + taps, :wide],
        sums[8, wide : wide + heads],
        sums[9, wide : wide + heads],
        jnp.sum(sums[6, :own].reshape(heads, HEAD_DIM), axis=-1),
        sums[5, :own],
    )
    g_w_zx_own = jnp.stack([gate_grad_own, late_a], axis=1)
    return (
        layer_out,
        input_grad,
        g_norm,
        g_w_zx_own,
        late_s[:, :wide],
        late_s[:, wide : wide + heads],
        *summed,
        out_grad_own,
    )


def solution(mesh):
    placed = (
        P(None, "seq", None),
        P(None, "seq"),
        P(),
        P(None, None, "head"),
        P(),
        P(None, "head"),
        P(None, "head"),
        P("head"),
        P(),
        P(),
        P("head"),
        P("head"),
        P("head"),
        P("head"),
        P(None, "head"),
        P(None, "seq", "head"),
    )
    return jax.shard_map(
        local,
        mesh=mesh,
        in_specs=placed,
        out_specs=(
            P(None, "seq", "head"),
            P(None, "seq", "head"),
            P("head"),
            P("seq", None, "head"),
            P("seq", None),
            P("seq", "head"),
            P(None, "head"),
            P("head"),
            P(),
            P(),
            P("head"),
            P("head"),
            P("head"),
            P("head"),
            P("seq", "head"),
        ),
        check_vma=False,
    )
```

```python
import functools

import jax
import jax.numpy as jnp
from jax import lax
from jax.experimental import pallas as pl
from jax.experimental.pallas import tpu as pltpu
from jax.sharding import PartitionSpec as P

HEAD_DIM = 64
BLOCK_LEN = 256
LANES = 128
EDGE = 16
ROWS = 16
VMEM = 56 * 2**20
EPS = 1e-05
BF = jnp.bfloat16
F32 = jnp.float32
def cost(micros):
    return pl.CostEstimate(flops=int(micros * 1.15e+09), bytes_accessed=1000, transcendentals=0)


SMEM_SPEC = pl.BlockSpec(memory_space=pltpu.SMEM)


def dot(a, b, contract=((1,), (0,)), precision=None):
    return lax.dot_general(
        a, b, (contract, ((), ())), preferred_element_type=F32, precision=precision
    )


def halves(value):
    high = value.astype(BF)
    return high, (value - high.astype(F32)).astype(BF)


def widen(value, expand):
    high, low = halves(value)
    return dot(high, expand) + dot(low, expand)


def per_head(value, expand):
    lane = lax.broadcasted_iota(jnp.int32, (1, LANES), 1)
    left = lane < HEAD_DIM
    total = None
    for pair in range(value.shape[1] // LANES):
        both = value[:, pair * LANES : (pair + 1) * LANES]
        low = jnp.sum(jnp.where(left, both, 0.0), axis=1, keepdims=True)
        high = jnp.sum(jnp.where(left, 0.0, both), axis=1, keepdims=True)
        placed = jnp.where(lane == 2 * pair, low, jnp.where(lane == 2 * pair + 1, high, 0.0))
        total = placed if total is None else total + placed
    return total


def to_row(column):
    rows = column.shape[0]
    return jnp.transpose(jnp.broadcast_to(column, (rows, LANES)))[:8]


def sigmoid(value):
    return 0.5 * jnp.tanh(0.5 * value) + 0.5


def softplus(value):
    return jnp.maximum(value, 0.0) + jnp.log1p(jnp.exp(-jnp.abs(value)))


def triangle(span, lower):
    row = lax.broadcasted_iota(jnp.int32, (span, span), 0)
    col = lax.broadcasted_iota(jnp.int32, (span, span), 1)
    return ((col <= row) if lower else (col >= row)).astype(F32)


def running(value, lower):
    width = value.shape[1]
    high, low = halves(value)
    lowest = (value - high.astype(F32) - low.astype(F32)).astype(BF)
    parts = jnp.concatenate([high, low, lowest], axis=1)
    sums = dot(triangle(value.shape[0], lower).astype(BF), parts)
    return sums[:, :width] + sums[:, width : 2 * width] + sums[:, 2 * width :]


def doc_mask(seg_col, seg_row, lower):
    span = seg_col.shape[0]
    row = lax.broadcasted_iota(jnp.int32, (span, span), 0)
    col = lax.broadcasted_iota(jnp.int32, (span, span), 1)
    causal = (col <= row) if lower else (col >= row)
    return jnp.where(causal, (seg_col == seg_row).astype(F32), 0.0)


def back_rows(value, steps):
    return value if steps == 0 else pltpu.roll(value, steps, 0)


def ahead_rows(value, steps):
    return value if steps == 0 else pltpu.roll(value, value.shape[0] - steps, 0)


def conv_rows(extended, aux, weight):
    taps = 4
    out = weight[taps : taps + 1] + weight[taps - 1 : taps] * extended[EDGE:]
    for tap in range(taps - 1):
        window = back_rows(extended, taps - 1 - tap)[EDGE:]
        out = out + weight[tap : tap + 1] * (aux[:, tap : tap + 1] * window)
    return out


def conv_back_rows(d_conv, extended, aux, weight, grad_ref=None):
    taps = 4
    room = jnp.zeros((EDGE, d_conv.shape[1]), F32)
    total = None
    for tap in range(taps):
        steps = taps - 1 - tap
        masked = d_conv if steps == 0 else d_conv * aux[:, tap : tap + 1]
        if grad_ref is not None:
            window = back_rows(extended, steps)[EDGE:]
            grad_ref[tap : tap + 1] += jnp.sum(masked * window, axis=0, keepdims=True)
        placed = jnp.concatenate([room, masked * weight[tap : tap + 1]], axis=0)
        placed = ahead_rows(placed, steps)
        total = placed if total is None else total + placed
    if grad_ref is not None:
        grad_ref[taps : taps + 1] += jnp.sum(d_conv, axis=0, keepdims=True)
    return total


def chunk_grid(count, rows, own):
    across = count * ROWS // rows
    return across, own // across


def cut(value, scratch, at, count):
    across, width = chunk_grid(count, value.shape[0], value.shape[1])
    for j in range(count):
        a, b = j // across, j % across
        scratch[j, at] = value[a * ROWS : (a + 1) * ROWS, b * width : (b + 1) * width].astype(BF)


def uncut(scratch, at, count, rows, own):
    across, _ = chunk_grid(count, rows, own)
    return jnp.concatenate(
        [
            jnp.concatenate([scratch[a * across + b, at] for b in range(across)], axis=1)
            for a in range(count // across)
        ],
        axis=0,
    )


def both_halves(me, mine_ref, other_ref):
    mine, other = mine_ref[0], other_ref[0]
    return jnp.where(
        me % 2 == 0,
        jnp.concatenate([mine, other], axis=0),
        jnp.concatenate([other, mine], axis=0),
    )


def front_kernel(
    state, me_ref, tok_ref, halo_ref, gain_ref, w_ref, w_small_ref, seg_ref, conv_x_ref,
    conv_bc_ref, head_ref, expand_ref, normed_ref, pre_x_ref, pre_bc_ref, halo_x_ref, halo_bc_ref,
    x_ref, bc_ref, xs_ref, dt_ref, cum_ref, aux_ref, keep_ref, send_ref
):
    s = pl.program_id(0)
    seqs = pl.num_programs(0)
    odd = me_ref[0] % 2
    half = state // 2
    own = xs_ref.shape[-1]
    wide = 2 * state
    span = tok_ref.shape[1]

    def norm(value):
        value = value.astype(F32)
        rstd = lax.rsqrt(jnp.mean(value * value, axis=-1, keepdims=True) + EPS)
        return (value * rstd * gain_ref[...]).astype(BF), rstd

    normed, rstd = norm(tok_ref[0])
    normed_ref[0] = normed
    room = jnp.zeros((EDGE - halo_ref.shape[1], halo_ref.shape[2]), F32)
    ahead = jnp.concatenate([room, norm(halo_ref[0])[0].astype(F32)], axis=0).astype(BF)
    rows = jnp.concatenate([ahead, normed], axis=0)
    pre_x = dot(rows, w_ref[0]).astype(BF)
    small = dot(rows, w_small_ref[...])
    pre_bc = small[:, :wide].astype(BF)
    dt_raw = small[EDGE:, wide:]

    seg = jnp.transpose(jnp.broadcast_to(seg_ref[0, 0:1], (LANES, LANES + span)))[LANES - EDGE :]
    here = seg[EDGE:]
    lane = lax.broadcasted_iota(jnp.int32, here.shape, 1)
    columns = [(back_rows(seg, 3 - tap)[EDGE:] == here).astype(F32) for tap in range(3)]
    columns.append((here == here[-1:]).astype(F32))
    columns.append((here == seg[EDGE - 1 : EDGE]).astype(F32))
    columns.append(here)
    columns.append(jnp.broadcast_to(rstd, here.shape))
    aux = jnp.zeros(here.shape, F32)
    for at, column in enumerate(columns):
        aux = jnp.where(lane == at, column, aux)
    aux_ref[0] = aux

    dt_ref[0] = dt_raw
    pre_x_ref[0] = pre_x[EDGE:]
    halo_x_ref[0] = pre_x[:EDGE]
    pre_bc_ref[0] = pre_bc[EDGE:]
    halo_bc_ref[0] = pre_bc[:EDGE]
    conv = conv_rows(pre_bc.astype(F32), aux, conv_bc_ref[...])
    bc = (conv * sigmoid(conv)).astype(BF)
    bc_ref[0] = bc
    conv = conv_rows(pre_x.astype(F32), aux, conv_x_ref[...])
    x = (conv * sigmoid(conv)).astype(BF)
    x_ref[0] = x
    x_float = x.astype(F32)
    step = softplus(dt_raw + head_ref[0:1])
    cum = running(-head_ref[1:2] * step, True)
    cum_ref[0] = cum
    expand = expand_ref[...]
    xs_ref[0] = (x_float * widen(step, expand)).astype(BF)
    last = cum[-1:]
    tail_step = jnp.exp(last - cum) * aux[:, 3:4] * step
    loaded = (x_float * widen(tail_step, expand)).astype(BF)
    own_state = dot(bc[:, :state], loaded, ((0,), (0,)))
    low, high = own_state[:half], own_state[half:]
    at = pl.ds(pl.multiple_of(s * half, half), half)
    keep_ref[at] = jnp.where(odd == 0, low, high).astype(BF)
    send_ref[at] = jnp.where(odd == 0, high, low).astype(BF)

    decay = jnp.broadcast_to(jnp.exp(last) * aux[-1:, 4:5], (8, LANES))
    decay_wide = widen(decay, expand)[:1]
    high = decay_wide.astype(BF).astype(F32)
    places = lax.broadcasted_iota(jnp.int32, (ROWS, 1), 0)
    extra = jnp.where(places == s, high, 0.0) + jnp.where(
        places == s + seqs, decay_wide - high, 0.0
    )
    end = pl.ds(seqs * half, ROWS)

    @pl.when(s == 0)
    def _():
        keep_ref[end] = extra.astype(BF)

    @pl.when(s > 0)
    def _():
        keep_ref[end] = (keep_ref[end].astype(F32) + extra).astype(BF)

    @pl.when(s == seqs - 1)
    def _():
        send_ref[end] = keep_ref[end]


def pair_kernel(seqs, groups, half, me_ref, mine_ref, other_ref, *rest):
    outs, decay_ref, scratch = rest[:groups], rest[groups], rest[groups + 1]
    odd, place = me_ref[0] % 2, me_ref[0] // 2
    end = seqs * half
    packed = [ref[end : end + ROWS].astype(F32) for ref in (mine_ref, other_ref)]
    mine, other = [p[:seqs] + p[seqs : 2 * seqs] for p in packed]
    first = jnp.where(odd == 0, mine, other)
    second = jnp.where(odd == 0, other, mine)
    decay_ref[0:seqs] = first
    decay_ref[8 : 8 + seqs] = second
    both = first * second
    high = both.astype(BF).astype(F32)
    room = jnp.zeros((ROWS - 2 * seqs, both.shape[1]), F32)
    extra = jnp.concatenate([high, both - high, room], axis=0)
    width = scratch.shape[3]
    across, _ = chunk_grid(groups, half, both.shape[1])
    for j in range(groups):
        b = j % across
        scratch[j, seqs] = extra[:, b * width : (b + 1) * width].astype(BF)
    for s in range(seqs):
        rows = slice(s * half, (s + 1) * half)
        mine, other = mine_ref[rows].astype(F32), other_ref[rows].astype(F32)
        early = jnp.where(odd == 0, mine, other)
        late = jnp.where(odd == 0, other, mine)
        cut(second[s : s + 1] * early + late, scratch, s, groups)
    for m in range(groups):
        outs[m][...] = scratch[place ^ m]


def pair_back_kernel(seqs, groups, half, me_ref, mine_ref, other_ref, decay_ref, *rest):
    outs, scratch = rest[:groups], rest[groups]
    odd, place = me_ref[0] % 2, me_ref[0] // 2
    for s in range(seqs):
        rows = slice(s * half, (s + 1) * half)
        mine, other = mine_ref[rows].astype(F32), other_ref[rows].astype(F32)
        early = jnp.where(odd == 0, mine, other)
        late = jnp.where(odd == 0, other, mine)
        cut(decay_ref[s : s + 1] * late + early, scratch, s, groups)
    for m in range(groups):
        outs[m][...] = scratch[place ^ m]


def scan_kernel(seqs, groups, me_ref, *rest):
    ins, outs = rest[:groups], rest[groups : 2 * groups]
    decay_ref, scratch = rest[2 * groups], rest[2 * groups + 1]
    place = me_ref[0] // 2
    for m in range(groups):
        scratch[place ^ m] = ins[m][...]
    for s in range(seqs):
        entry = jnp.zeros(scratch.shape[2:], F32)
        for k in range(groups):
            packed = scratch[k, seqs].astype(F32)
            decay = packed[s : s + 1] + packed[s + seqs : s + seqs + 1]
            decay_ref[k, s : s + 1] = decay
            arrived = scratch[k, s].astype(F32)
            scratch[k, s] = entry.astype(BF)
            entry = decay * entry + arrived
    for m in range(groups):
        outs[m][...] = scratch[place ^ m, :seqs]


def scan_back_kernel(seqs, groups, me_ref, decay_ref, *rest):
    ins, outs, scratch = rest[:groups], rest[groups : 2 * groups], rest[2 * groups]
    place = me_ref[0] // 2
    for m in range(groups):
        scratch[place ^ m] = ins[m][...]
    for s in range(seqs):
        leave = jnp.zeros(scratch.shape[2:], F32)
        for k in reversed(range(groups)):
            arrived = scratch[k, s].astype(F32)
            scratch[k, s] = leave.astype(BF)
            leave = decay_ref[k, s : s + 1] * leave + arrived
    for m in range(groups):
        outs[m][...] = scratch[place ^ m]


def unpair_kernel(seqs, groups, half, forward, me_ref, mine_ref, other_ref, decay_ref, *rest):
    ins, (own_ref, send_ref, scratch) = rest[:groups], rest[groups:]
    odd, place = me_ref[0] % 2, me_ref[0] // 2
    own = own_ref.shape[-1]
    for m in range(groups):
        scratch[place ^ m] = ins[m][...]
    is_first = (odd == 0) if forward else (odd == 1)
    for s in range(seqs):
        rows = slice(s * half, (s + 1) * half)
        entry = uncut(scratch, s, groups, half, own).astype(F32)
        mine, other = mine_ref[rows].astype(F32), other_ref[rows].astype(F32)
        first = jnp.where(is_first, mine, other)
        at = s if forward else 8 + s
        later = decay_ref[at : at + 1] * entry + first
        own_ref[s] = jnp.where(is_first, entry, later).astype(BF)
        send_ref[s] = jnp.where(is_first, later, entry).astype(BF)


def inner_kernel(state, bc_ref, xs_ref, cum_ref, aux_ref, seg_ref, out_ref):
    own = xs_ref.shape[-1]
    b_ssm, c_ssm = bc_ref[0, :, :state], bc_ref[0, :, state:]
    cum = cum_ref[0]
    cum_t = jnp.transpose(cum)
    mask = doc_mask(aux_ref[0, :, 5:6], seg_ref[0, 0:1, LANES:], True)
    scores = dot(c_ssm, b_ssm, ((1,), (1,))) * mask
    left = lax.broadcasted_iota(jnp.int32, (1, LANES), 1) < HEAD_DIM
    for pair in range(own // LANES):
        lanes = slice(pair * LANES, (pair + 1) * LANES)
        xs = xs_ref[0, :, lanes].astype(F32)
        total = None
        for side in range(2):
            h = 2 * pair + side
            lag = jnp.minimum(cum[:, h : h + 1] - cum_t[h : h + 1], 0.0)
            weights = (scores * jnp.exp(lag)).astype(BF)
            own_xs = jnp.where(left if side == 0 else ~left, xs, 0.0).astype(BF)
            term = dot(weights, own_xs)
            total = term if total is None else total + term
        out_ref[0, :, lanes] = total


def mixer_out(state, states, x_ref, bc_ref, inner_ref, gate_ref, cum_ref, aux_ref, rows_ref, expand_ref):
    c_ssm = bc_ref[0, :, state:]
    x_float = x_ref[0].astype(F32)
    entry_wide = widen(jnp.exp(cum_ref[0]) * aux_ref[0, :, 4:5], expand_ref[...])
    mixed = inner_ref[0] + dot(c_ssm, states) * entry_wide
    y = mixed + rows_ref[1:2] * x_float
    gate = gate_ref[0].astype(F32)
    sig = sigmoid(gate)
    return mixed, y, x_float, gate, sig, entry_wide


def sums_kernel(
    state, me_ref, x_ref, bc_ref, inner_ref, gate_ref, e_ref, cum_ref, aux_ref, mine_ref,
    other_ref, rows_ref, expand_ref, out_ref
):
    states = both_halves(me_ref[0], mine_ref, other_ref)
    _, y, _, gate, sig, _ = mixer_out(
        state, states, x_ref, bc_ref, inner_ref, gate_ref, cum_ref, aux_ref, rows_ref, expand_ref
    )
    gated = y * (gate * sig)
    squares = jnp.sum(gated * gated, axis=-1, keepdims=True)
    dots = jnp.sum(e_ref[0].astype(F32) * (gated * rows_ref[0:1]), axis=-1, keepdims=True)
    place = lax.broadcasted_iota(jnp.int32, (8, 1), 0)
    out_ref[0] = jnp.where(place == 0, to_row(squares), jnp.where(place == 1, to_row(dots), 0.0))


def gate_back_kernel(
    state, inner_total, me_ref, x_ref, bc_ref, inner_ref, gate_ref, e_ref, cum_ref, aux_ref,
    mine_ref, other_ref, rows_ref, expand_ref, sums_ref, scaled_ref, dz_ref, dy_ref, mixed_ref,
    dc_ref, dot_ref, grad_ref, keep_ref, send_ref
):
    s = pl.program_id(0)
    odd = me_ref[0] % 2
    half = state // 2
    expand = expand_ref[...]
    states = both_halves(me_ref[0], mine_ref, other_ref)
    mixed, y, x_float, gate, sig, entry_wide = mixer_out(
        state, states, x_ref, bc_ref, inner_ref, gate_ref, cum_ref, aux_ref, rows_ref, expand_ref
    )
    columns = jnp.transpose(
        jnp.concatenate([sums_ref[0], jnp.zeros((LANES - 8, sums_ref.shape[2]), F32)], axis=0)
    )
    rstd = lax.rsqrt(columns[:, 0:1] / inner_total + EPS)
    slope = columns[:, 1:2] * (rstd * rstd * rstd) / inner_total
    gain = rows_ref[0:1]
    silu = gate * sig
    gated = y * silu
    scaled_ref[0] = (gated * gain * rstd).astype(BF)
    d_scaled = e_ref[0].astype(F32) * rstd
    d_gated = d_scaled * gain - slope * gated
    d_y = d_gated * silu
    dy_ref[0] = d_y.astype(BF)
    d_z = (d_gated * y * (sig * (1.0 + gate * (1.0 - sig)))).astype(BF)
    dz_ref[0] = d_z
    row = jnp.sum(d_z.astype(F32) * gate, axis=-1, keepdims=True)
    dot_ref[0] = to_row(row)
    mixed_ref[0] = per_head(d_y * mixed, expand)

    @pl.when(s == 0)
    def _():
        grad_ref[...] = jnp.zeros_like(grad_ref)

    grad_ref[5:6] += jnp.sum(d_scaled * gated, axis=0, keepdims=True)
    grad_ref[6:7] += jnp.sum(d_y * x_float, axis=0, keepdims=True)
    d_carried = (d_y * entry_wide).astype(BF)
    dc_ref[0] = dot(d_carried, states, ((1,), (1,)))
    grad = dot(bc_ref[0, :, state:], d_carried, ((0,), (0,)))
    low, high = grad[:half], grad[half:]
    at = pl.ds(pl.multiple_of(s * half, half), half)
    keep_ref[at] = jnp.where(odd == 0, low, high).astype(BF)
    send_ref[at] = jnp.where(odd == 0, high, low).astype(BF)


def inner_back_kernel(
    state, x_ref, bc_ref, xs_ref, dy_ref, dc_ref, cum_ref, dt_ref, aux_ref, seg_ref, rows_ref,
    head_ref, expand_ref, dx_ref, dstep_ref, dbc_ref
):
    own = xs_ref.shape[-1]
    b_ssm, c_ssm = bc_ref[0, :, :state], bc_ref[0, :, state:]
    cum = cum_ref[0]
    cum_t = jnp.transpose(cum)
    nt = ((1,), (1,))
    mask = doc_mask(aux_ref[0, :, 5:6], seg_ref[0, 0:1, LANES:], False)
    scores = dot(b_ssm, c_ssm, nt) * mask
    left = lax.broadcasted_iota(jnp.int32, (1, LANES), 1) < HEAD_DIM
    d_scores = None
    sums = []
    for pair in range(own // LANES):
        lanes = slice(pair * LANES, (pair + 1) * LANES)
        xs = xs_ref[0, :, lanes]
        dy = dy_ref[0, :, lanes].astype(F32)
        total = None
        for side in range(2):
            h = 2 * pair + side
            lag = jnp.minimum(cum_t[h : h + 1] - cum[:, h : h + 1], 0.0)
            mixing = jnp.exp(lag)
            weights = (scores * mixing).astype(BF)
            own_dy = jnp.where(left if side == 0 else ~left, dy, 0.0).astype(BF)
            term = dot(weights, own_dy)
            total = term if total is None else total + term
            d_mixed = dot(xs, own_dy, nt) * mixing
            d_scores = d_mixed if d_scores is None else d_scores + d_mixed
        sums.append(total)
    back = jnp.concatenate(sums, axis=1)
    expand = expand_ref[...]
    x_float = x_ref[0].astype(F32)
    dstep_ref[0] = per_head(x_float * back, expand)
    step = softplus(dt_ref[0] + head_ref[0:1])
    dy_all = dy_ref[0].astype(F32)
    dx_ref[0] = (back * widen(step, expand) + rows_ref[1:2] * dy_all).astype(BF)
    d_scores = (d_scores * mask).astype(BF)
    dbc_ref[0, :, :state] = dot(d_scores, c_ssm)
    dbc_ref[0, :, state:] = dot(d_scores, b_ssm, ((0,), (0,))) + dc_ref[0]


def leave_kernel(
    state, me_ref, x_ref, bc_ref, pre_ref, halo_ref, pre_bc_ref, halo_bc_ref, dx_ref, dstep_ref,
    dbc_ref, mixed_ref, cum_ref, dt_ref, aux_ref, dot_z_ref, mine_ref, other_ref, end_mine_ref,
    end_other_ref, conv_ref, conv_bc_ref, head_ref, expand_ref, dpre_ref, back_ref, back_bc_ref,
    dbc_out_ref, ddt_ref, dot_ref, grad_ref, small_ref
):
    me = me_ref[0]
    own = dx_ref.shape[-1]
    expand = expand_ref[...]
    states = both_halves(me, mine_ref, other_ref)
    ends = both_halves(me, end_mine_ref, end_other_ref)
    b_ssm = bc_ref[0, :, :state]
    x_float = x_ref[0].astype(F32)
    aux = aux_ref[0]
    dt_pre = dt_ref[0] + head_ref[0:1]
    step = softplus(dt_pre)
    rate = head_ref[1:2]
    cum = cum_ref[0]
    last = cum[-1:]
    tail_decay = jnp.exp(last - cum) * aux[:, 3:4]
    tail_step = tail_decay * step
    tail_wide = widen(tail_step, expand)
    loaded = (x_float * tail_wide).astype(BF)
    d_loaded = dot(b_ssm, ends)
    dbc_out_ref[0, :, :state] = (dbc_ref[0, :, :state] + dot(loaded, ends, ((1,), (1,)))).astype(BF)
    dbc_out_ref[0, :, state:] = dbc_ref[0, :, state:].astype(BF)
    d_bc = dbc_out_ref[0, :EDGE].astype(F32)
    extended = jnp.concatenate([halo_bc_ref[0], pre_bc_ref[0, :EDGE]], axis=0).astype(F32)
    weight = conv_bc_ref[...]
    conv = conv_rows(extended, aux[:EDGE], weight)
    sig = sigmoid(conv)
    d_conv = d_bc * (sig * (1.0 + conv * (1.0 - sig)))
    back_bc_ref[0] = conv_back_rows(d_conv, extended, aux[:EDGE], weight)[:EDGE].astype(BF)
    d_x = dx_ref[0].astype(F32) + d_loaded * tail_wide
    d_tail = per_head(d_loaded * x_float, expand)
    end_terms = d_tail * tail_step
    product = jnp.sum(ends.astype(F32) * states.astype(F32), axis=0, keepdims=True)
    d_decay = per_head(jnp.broadcast_to(product, (8, own)), expand)[:1]
    block_decay = jnp.exp(last) * aux[-1:, 4:5]
    d_cum = mixed_ref[0] - step * dstep_ref[0] - end_terms
    last_add = jnp.sum(end_terms, axis=0, keepdims=True) + d_decay * block_decay
    d_log = running(d_cum, False) + last_add
    d_step = dstep_ref[0] + d_tail * tail_decay - d_log * rate
    d_dt = d_step * sigmoid(dt_pre)
    ddt_ref[0] = d_dt.astype(BF)

    @pl.when(pl.program_id(0) == 0)
    def _():
        grad_ref[...] = jnp.zeros_like(grad_ref)
        small_ref[...] = jnp.zeros_like(small_ref)

    small_ref[0:1] += jnp.sum(d_dt, axis=0, keepdims=True)
    small_ref[1:2] += jnp.sum(d_log * (-rate * step), axis=0, keepdims=True)

    extended = jnp.concatenate([halo_ref[0], pre_ref[0]], axis=0).astype(F32)
    weight = conv_ref[...]
    conv = conv_rows(extended, aux, weight)
    sig = sigmoid(conv)
    d_conv = d_x * (sig * (1.0 + conv * (1.0 - sig)))
    d_ext = conv_back_rows(d_conv, extended, aux, weight, grad_ref)
    d_pre = d_ext[EDGE:].astype(BF)
    dpre_ref[0] = d_pre
    back_ref[0] = d_ext[:EDGE].astype(BF)
    row = jnp.sum(d_pre.astype(F32) * extended[EDGE:], axis=-1, keepdims=True)
    row = row + jnp.sum(ddt_ref[0].astype(F32) * dt_ref[0], axis=-1, keepdims=True)
    dot_ref[0] = to_row(row) + dot_z_ref[0]


def conv_bc_kernel(
    d_ref, pre_ref, halo_ref, aux_ref, ddt_ref, conv_ref, dpre_ref, dot_ref, grad_ref
):
    span = pre_ref.shape[1]
    extended = jnp.concatenate([halo_ref[0], pre_ref[0]], axis=0).astype(F32)
    aux = aux_ref[0]
    weight = conv_ref[...]
    conv = conv_rows(extended, aux, weight)
    sig = sigmoid(conv)
    d_conv = d_ref[0, :span].astype(F32) * (sig * (1.0 + conv * (1.0 - sig)))

    @pl.when(pl.program_id(0) == 0)
    def _():
        grad_ref[...] = jnp.zeros_like(grad_ref)

    d_pre = conv_back_rows(d_conv, extended, aux, weight, grad_ref)[EDGE:]
    ahead = d_ref[0, span : span + EDGE].astype(F32)
    d_pre = jnp.concatenate([d_pre[: span - EDGE], d_pre[span - EDGE :] + ahead], axis=0)
    d_pre = d_pre.astype(BF)
    dpre_ref[0, :, : d_pre.shape[1]] = d_pre
    dpre_ref[0, :, d_pre.shape[1] :] = ddt_ref[0]
    row = jnp.sum(d_pre.astype(F32) * extended[EDGE:], axis=-1, keepdims=True)
    packed = d_ref[0, span + EDGE :].astype(F32)
    dot_ref[0] = to_row(row) + (packed[0:1] + packed[1:2])


def gram_kernel(a_ref, b_ref, out_ref):
    out_ref[...] = dot(a_ref[...], b_ref[...], ((0,), (0,))).astype(BF)


def gram_pair_kernel(me_ref, a_ref, b_ref, odd_ref, even_ref):
    product = dot(a_ref[...], b_ref[...], ((0,), (0,))).astype(BF)
    tile = product.shape[0] // 2
    low, high = product[:tile], product[tile:]
    same = me_ref[0] % 2 == 0
    odd_ref[0] = jnp.where(same, high, low)
    even_ref[0] = jnp.where(same, low, high)


def share_kernel(terms, with_sum, me_ref, *refs):
    odd_ref, even_ref = refs[2 * terms + with_sum : 2 * terms + with_sum + 2]
    nt = ((1,), (1,))
    total = None
    for t in range(terms):
        rhs = refs[2 * t + 1]
        rhs = rhs[0] if len(rhs.shape) == 3 else rhs[...]
        term = dot(refs[2 * t][...], rhs, nt)
        total = term if total is None else total + term
    total_low = total.astype(BF)

    @pl.when(pl.program_id(0) < pl.num_programs(0) // 2)
    def _():
        odd_ref[0] = total_low

    @pl.when(pl.program_id(0) >= pl.num_programs(0) // 2)
    def _():
        even_ref[0] = total_low

    if with_sum:
        sum_ref = refs[-1]

        @pl.when(pl.program_id(1) == 0)
        def _():
            sum_ref[...] = jnp.zeros_like(sum_ref)

        normed = refs[2 * terms][...].astype(F32)
        sum_ref[0, 0:1] += jnp.sum(total * normed, axis=0, keepdims=True)


def per_seq(seqs, shape):
    zeros = (0,) * len(shape)
    return pl.BlockSpec((1, *shape), lambda s: (jnp.minimum(s, seqs - 1), *zeros))


def whole(shape):
    zeros = (0,) * len(shape)
    return pl.BlockSpec(tuple(shape), lambda s: zeros)


def call(body, grid, ins, in_specs, outs, out_specs, scratch, flops, name, aliases={}):
    return pl.pallas_call(
        body,
        grid=(grid,),
        in_specs=in_specs,
        out_specs=out_specs,
        out_shape=outs,
        scratch_shapes=scratch,
        name=name,
        input_output_aliases=aliases,
        compiler_params=pltpu.CompilerParams(vmem_limit_bytes=VMEM),
        cost_estimate=cost(flops),
    )(*ins)


def shaped(shape, dtype):
    return jax.ShapeDtypeStruct(tuple(shape), dtype)


def swap(value, axis, mask):
    count = lax.axis_size(axis)
    return lax.ppermute(value, axis, [(i, i ^ mask) for i in range(count)])


def shift(value, axis, steps):
    count = lax.axis_size(axis)
    leading, last = (max(0, -steps), min(count, count - steps))
    return lax.ppermute(value, axis, [(i, i + steps) for i in range(leading, last)])


def exchange(chunks, masks):
    return [swap(c, "seq", mask) if mask else c for c, mask in zip(chunks, masks)]


def after(value, *others):
    return lax.optimization_barrier((value, *others))[0]


def fold_step(sides, axis, mask):
    odd, even = sides
    arrived = swap(odd, axis, mask)
    if even.shape[0] == 1:
        return (even + arrived)[0]
    return even[1::2] + arrived[1::2], even[0::2] + arrived[0::2]


def fold(sides, axis, mask=1):
    while isinstance(sides, tuple):
        sides = fold_step(sides, axis, mask)
        mask *= 2
    return sides


def core_sum(odd, even):
    return even + swap(odd, "head", 1)


def pair_sides(full):
    odd = lax.axis_index("seq") % 2
    chunks = full.reshape(lax.axis_size("seq") // 2, 2, -1, full.shape[-1])
    return tuple(lax.dynamic_index_in_dim(chunks, at, 1, False) for at in (1 - odd, odd))


def pair_sum(sides):
    return sides[1] + swap(sides[0], "seq", 1)


def spread_sum(total):
    count = lax.axis_size("seq")
    return lax.psum_scatter(
        total.reshape(-1, total.shape[-1]),
        "seq",
        scatter_dimension=0,
        tiled=True,
        axis_index_groups=[[2 * z + x for z in range(count // 2)] for x in range(2)],
    )


def row_sides(full, axis):
    count = lax.axis_size(axis)
    me = lax.axis_index(axis)
    chunks = full.reshape(count, -1, full.shape[-1])

    def stacked(masks):
        return jnp.stack([lax.dynamic_index_in_dim(chunks, me ^ m, 0, False) for m in masks])

    return stacked(range(1, count, 2)), stacked(range(0, count, 2))


def sum_all(value, axis):
    mask = 1
    while mask < lax.axis_size(axis):
        value = value + swap(value, axis, mask)
        mask *= 2
    return value


def pad_lanes(value, width):
    return jnp.pad(value, ((0, 0), (0, width - value.shape[1])))


def pad_rows(rows, count=8):
    stacked = jnp.concatenate([r.reshape(-1, r.shape[-1]).astype(F32) for r in rows], axis=0)
    return jnp.pad(stacked, ((0, count - stacked.shape[0]), (0, 0)))


def local(
    tokens,
    segments,
    norm_gain,
    w_zx,
    w_bc,
    w_dt,
    conv_x,
    conv_x_bias,
    conv_bc,
    conv_bc_bias,
    dt_bias,
    a_log,
    d_skip,
    gate_gain,
    w_out,
    cotangent,
):
    seqs, span, model = tokens.shape
    rows = seqs * span
    heads = d_skip.shape[0]
    own = heads * HEAD_DIM
    n_seq, n_head = lax.axis_size("seq"), lax.axis_size("head")
    me_head = lax.axis_index("head")
    me = lax.axis_index("seq").astype(jnp.int32).reshape(1)
    head_at = me_head.astype(jnp.int32).reshape(1)
    inner_total = own * n_head
    state = w_bc.shape[1] // 2
    half = state // 2
    wide = 2 * state
    share = model // n_head
    offset = me_head * share
    edge = conv_x.shape[0] - 1
    groups = n_seq // 2
    masks = [2 * m for m in range(groups)]
    _, width = chunk_grid(groups, half, own)

    seg_lanes = jnp.broadcast_to(segments[:, -8:, None].astype(BF), (seqs, 8, LANES))
    cot_full = lax.all_gather(cotangent, "head", axis=2, tiled=True)

    w_in = lax.optimization_barrier(jnp.transpose(w_zx, (1, 0, 2)))
    halo = jnp.concatenate([after(tokens, w_in)[:, -8:], seg_lanes], axis=2)
    halo = shift(halo, "seq", 1)
    tok_halo, seg_halo = halo[..., :model], halo[..., model]
    w_dt = pad_lanes(w_dt, LANES)
    w_small = jnp.concatenate([w_bc, w_dt], axis=1)
    seg_rows = [jnp.pad(seg_halo.astype(F32), ((0, 0), (LANES - 8, 0))), segments.astype(F32)]
    seg_rows = jnp.concatenate(seg_rows, axis=1)
    seg_rows = jnp.broadcast_to(seg_rows[:, None], (seqs, 8, LANES + span))
    conv_x_w = pad_rows([conv_x, conv_x_bias])
    conv_bc_w = pad_rows([conv_bc, conv_bc_bias])
    head_rows = pad_lanes(pad_rows([dt_bias, jnp.exp(a_log)]), LANES)
    wide_rows = pad_rows([gate_gain, jnp.repeat(d_skip, HEAD_DIM)])
    expand = (
        jnp.arange(LANES)[:, None] == (jnp.arange(own) // HEAD_DIM)[None, :]
    ).astype(BF)

    seq = functools.partial(per_seq, seqs)

    def seq_of(values):
        return [seq(v.shape[1:]) for v in values]

    def whole_of(values):
        return [whole(v.shape) for v in values]

    w_x_spec = pl.BlockSpec((1, model, own), lambda s: (1, 0, 0))
    ins = (
        me, tokens, tok_halo, norm_gain.reshape(1, model), w_in, w_small, seg_rows, conv_x_w,
        conv_bc_w, head_rows, expand,
    )
    per = (
        shaped((seqs, span, model), BF),
        shaped((seqs, span, own), BF),
        shaped((seqs, span, wide), BF),
        shaped((seqs, EDGE, own), BF),
        shaped((seqs, EDGE, wide), BF),
        shaped((seqs, span, own), BF),
        shaped((seqs, span, wide), BF),
        shaped((seqs, span, own), BF),
        shaped((seqs, span, LANES), F32),
        shaped((seqs, span, LANES), F32),
        shaped((seqs, span, LANES), F32),
    )
    packed = (shaped((seqs * half + ROWS, own), BF),) * 2
    normed, pre_x, pre_bc, halo_x, halo_bc, x_ssm, bc_ssm, xs, dt_raw, cum, aux, keep, send = call(
        functools.partial(front_kernel, state),
        seqs,
        ins,
        [SMEM_SPEC, *seq_of(ins[1:3]), whole(ins[3].shape), w_x_spec, whole(w_small.shape)]
        + seq_of(ins[6:7])
        + whole_of(ins[7:]),
        per + packed,
        seq_of(per) + whole_of(packed),
        [],
        30,
        "front",
    )

    def small_call(body, ins, outs, blocks, name):
        return call(
            body,
            1,
            ins,
            [SMEM_SPEC] + whole_of(ins[1:]),
            outs,
            whole_of(outs),
            [pltpu.VMEM((groups, blocks, ROWS, width), BF)],
            3,
            name,
        )

    piece = shaped((seqs, ROWS, width), BF)
    halves_out = (shaped((seqs, half, own), BF),) * 2
    other = swap(send, "seq", 1)
    *parts, pair_decay = small_call(
        functools.partial(pair_kernel, seqs, groups, half),
        (me, keep, other),
        (shaped((seqs + 1, ROWS, width), BF),) * groups + (shaped((16, own), F32),),
        seqs + 1,
        "pair",
    )
    *entries, decays = small_call(
        functools.partial(scan_kernel, seqs, groups),
        (me, *exchange(parts, masks)),
        (piece,) * groups + (shaped((groups, 8, width), F32),),
        seqs + 1,
        "scan",
    )
    state_mine, state_send = small_call(
        functools.partial(unpair_kernel, seqs, groups, half, True),
        (me, keep, other, pair_decay, *exchange(entries, masks)),
        halves_out,
        seqs,
        "unpair",
    )
    state_other = swap(state_send, "seq", 1)

    gate = dot(normed, w_in[0], ((2,), (0,))).astype(BF)
    e_raw = dot(cot_full, w_out, ((2,), (0,))).astype(BF)
    ins = (bc_ssm, xs, cum, aux, seg_rows)
    (inner,) = call(
        functools.partial(inner_kernel, state),
        seqs,
        ins,
        seq_of(ins),
        (shaped((seqs, span, own), F32),),
        [seq((span, own))],
        [],
        10.3,
        "inner",
    )

    mixer = (me, x_ssm, bc_ssm, inner, gate, e_raw, cum, aux, state_mine, state_other, wide_rows, expand)
    mixer_specs = [SMEM_SPEC] + seq_of(mixer[1:10]) + whole_of(mixer[10:])
    (sums,) = call(
        functools.partial(sums_kernel, state),
        seqs,
        mixer,
        mixer_specs,
        (shaped((seqs, 8, span), F32),),
        [seq((8, span))],
        [],
        12,
        "sums",
    )
    sums = sum_all(sums, "head")

    per = (
        shaped((seqs, span, own), BF),
        shaped((seqs, span, own), BF),
        shaped((seqs, span, own), BF),
        shaped((seqs, span, LANES), F32),
        shaped((seqs, span, state), F32),
        shaped((seqs, 8, span), F32),
    )
    fixed = (shaped((8, own), F32),) + (shaped((seqs * half, own), BF),) * 2
    scaled, d_z, d_y, mixed, d_c, dot_z, gate_grads, keep, send = call(
        functools.partial(gate_back_kernel, state, inner_total),
        seqs,
        (*mixer, sums),
        mixer_specs + [seq((8, span))],
        per + fixed,
        seq_of(per) + whole_of(fixed),
        [],
        21,
        "gate_back",
    )

    other = swap(send, "seq", 1)

    normed_rows = normed.reshape(rows, model)

    def gram(left, values):
        tile = 4 * LANES
        return call(
            gram_kernel,
            model // tile,
            (left, values),
            [pl.BlockSpec((rows, tile), lambda i: (0, i)), whole(values.shape)],
            (shaped((model, values.shape[1]), BF),),
            [pl.BlockSpec((tile, values.shape[1]), lambda i: (i, 0))],
            [],
            10.8,
            "gram",
        )[0]

    def chunk_pair(left, values, natural):
        tile = model // n_seq
        if tile % LANES:
            full = dot(left, values, ((0,), (0,))).astype(BF)
            return pair_sides(full) if natural else row_sides(full, "seq")
        block = (tile, values.shape[1])

        def at(i, me_ref):
            return i if natural else i ^ (me_ref[0] // 2)

        return tuple(
            pl.pallas_call(
                gram_pair_kernel,
                grid_spec=pltpu.PrefetchScalarGridSpec(
                    num_scalar_prefetch=1,
                    grid=(groups,),
                    in_specs=[
                        pl.BlockSpec((rows, 2 * tile), lambda i, me_ref: (0, at(i, me_ref))),
                        pl.BlockSpec(values.shape, lambda i, me_ref: (0, 0)),
                    ],
                    out_specs=[pl.BlockSpec((1, *block), lambda i, me_ref: (i, 0, 0))] * 2,
                ),
                out_shape=[shaped((groups, *block), BF)] * 2,
                name="gram_pair",
                compiler_params=pltpu.CompilerParams(vmem_limit_bytes=VMEM),
                cost_estimate=cost(rows * model * values.shape[1] / 3e8),
            )(me, left, values)
        )

    def share_sum(terms, parity, summed):
        pairs = n_head // 2
        quads = pairs // 2
        tall = rows
        def at(i, head_ref):
            core = 1 - i // quads
            return (4 * (i % quads) + 2 * parity + core) ^ head_ref[0]

        ins, specs = [], []
        for lhs, rhs, first in terms:
            ins += [lhs, rhs]
            specs.append(pl.BlockSpec((tall, lhs.shape[1]), lambda i, s, head_ref: (s, 0)))
            if rhs.ndim == 3:
                specs.append(
                    pl.BlockSpec(
                        (1, share, rhs.shape[2]),
                        lambda i, s, head_ref, first=first: (first, at(i, head_ref), 0),
                    )
                )
            else:
                specs.append(
                    pl.BlockSpec(
                        (share, rhs.shape[1]), lambda i, s, head_ref: (at(i, head_ref), 0)
                    )
                )
        out_specs = [
            pl.BlockSpec(
                (1, tall, share), lambda i, s, head_ref: (jnp.minimum(i, quads - 1), s, 0)
            ),
            pl.BlockSpec(
                (1, tall, share), lambda i, s, head_ref: (jnp.maximum(i - quads, 0), s, 0)
            ),
        ]
        outs = [shaped((quads, rows, share), BF)] * 2
        if summed:
            ins.append(normed_rows)
            specs.append(
                pl.BlockSpec((tall, share), lambda i, s, head_ref: (s, at(i, head_ref)))
            )
            out_specs.append(pl.BlockSpec((1, 8, share), lambda i, s, head_ref: (i, 0, 0)))
            outs.append(shaped((pairs, 8, share), F32))
        depth = sum(t[0].shape[1] for t in terms)
        got = pl.pallas_call(
            functools.partial(share_kernel, len(terms), summed),
            grid_spec=pltpu.PrefetchScalarGridSpec(
                num_scalar_prefetch=1,
                grid=(pairs, rows // tall),
                in_specs=specs,
                out_specs=out_specs,
            ),
            out_shape=outs,
            name="shares",
            compiler_params=pltpu.CompilerParams(vmem_limit_bytes=VMEM),
            cost_estimate=cost(rows * model * depth / 5e8),
        )(head_at, *ins)
        return (got[:2], got[2]) if summed else got

    scaled_rows, d_z_rows = scaled.reshape(rows, own), d_z.reshape(rows, own)
    out_grad = chunk_pair(cot_full.reshape(rows, model), scaled_rows, True)
    out_far = share_sum([(after(scaled_rows, out_grad[1]), w_out, 0)], 1, False)
    parts = small_call(
        functools.partial(pair_back_kernel, seqs, groups, half),
        (me, after(keep, out_far[1]), other, pair_decay),
        (piece,) * groups,
        seqs,
        "pair_back",
    )
    arrived = exchange(parts, masks)
    ins = (
        x_ssm, bc_ssm, xs, after(d_y, parts[0]), d_c, cum, dt_raw, aux, seg_rows, wide_rows, head_rows, expand,
    )
    per = (
        shaped((seqs, span, own), BF),
        shaped((seqs, span, LANES), F32),
        shaped((seqs, span, wide), F32),
    )
    d_x, d_step, d_bc = call(
        functools.partial(inner_back_kernel, state),
        seqs,
        ins,
        seq_of(ins[:9]) + whole_of(ins[9:]),
        per,
        seq_of(per),
        [],
        18.6,
        "inner_back",
    )

    leaves = small_call(
        functools.partial(scan_back_kernel, seqs, groups),
        (me, after(decays, d_x), *arrived),
        (piece,) * groups,
        seqs,
        "scan_back",
    )
    arrived = exchange(leaves, masks)
    gate_grad = gram(normed_rows, after(d_z_rows, leaves[0]))
    end_mine, end_send = small_call(
        functools.partial(unpair_kernel, seqs, groups, half, False),
        (me, after(keep, gate_grad), other, pair_decay, *arrived),
        halves_out,
        seqs,
        "unpair_back",
    )
    end_other = swap(end_send, "seq", 1)
    gate_total = spread_sum(gate_grad).reshape(2, -1, own)
    gate_total = spread_sum(gate_grad).reshape(2, -1, own)
    out_odd = share_sum([(after(scaled_rows, end_mine), w_out, 0)], 1, False)
    out_even = share_sum([(after(scaled_rows, out_odd), w_out, 0)], 0, False)

    out_total = pair_sum((out_grad[0], after(out_grad[1], end_mine)))
    ins = (
        me, after(x_ssm, out_total), bc_ssm, pre_x, halo_x, pre_bc, halo_bc, d_x, d_step, d_bc, mixed, cum,
        dt_raw, aux, dot_z, state_mine, state_other, end_mine, end_other, conv_x_w, conv_bc_w,
        head_rows, expand,
    )
    per = (
        shaped((seqs, span, own), BF),
        shaped((seqs, EDGE, own), BF),
        shaped((seqs, EDGE, wide), BF),
        shaped((seqs, span, wide), BF),
        shaped((seqs, span, LANES), BF),
        shaped((seqs, 8, span), F32),
    )
    fixed = (shaped((8, own), F32), shaped((8, LANES), F32))
    d_x_pre, back_x, back_bc, d_bc, d_dt, row_dot, conv_grads, head_grads = call(
        functools.partial(leave_kernel, state),
        seqs,
        ins,
        [SMEM_SPEC] + seq_of(ins[1:19]) + whole_of(ins[19:]),
        per + fixed,
        seq_of(per) + whole_of(fixed),
        [],
        28,
        "leave",
    )
    out_near = share_sum([(after(scaled_rows, d_x_pre), w_out, 0)], 0, False)
    out_far = core_sum(out_far[0], after(out_far[1], out_near[1]))
    back = shift(jnp.concatenate([back_x, back_bc], axis=2)[:, -edge:], "seq", -1)
    back = after(back, out_near[1])
    back_x, back_bc = back[..., :own], back[..., own:]
    fix = jnp.sum(back_x.astype(F32) * pre_x[:, -edge:].astype(F32), axis=-1)
    row_dot = row_dot[:, 0] + jnp.pad(fix, ((0, 0), (span - edge, 0)))
    dot_high = row_dot.astype(BF)
    dot_low = (row_dot - dot_high.astype(F32)).astype(BF)
    dots = jnp.pad(jnp.stack([dot_high, dot_low], axis=1), ((0, 0), (0, EDGE - 2), (0, 0)))
    back_bc = jnp.pad(back_bc, ((0, 0), (EDGE - edge, 0), (0, 0)))
    d_bc = jnp.concatenate([d_bc, back_bc, dots], axis=1)
    d_bc = d_bc + swap(d_bc, "head", 1)
    d_x_pre = after(d_x_pre, d_bc, out_far).at[:, -edge:].add(back_x)
    d_x_rows = d_x_pre.reshape(rows, own)
    d_dt_rows = d_dt.reshape(rows, LANES)
    late_sides = chunk_pair(normed_rows, d_x_rows, True)

    core, middle = me_head % 2, seqs // 2
    part = lax.dynamic_slice_in_dim(d_bc, core * middle, middle, 0)
    mask = 2
    while mask < n_head:
        part = part + swap(part, "head", mask)
        mask *= 2
    part = after(part, late_sides[1])
    part_other = swap(part, "head", 1)
    d_bc_all = jnp.where(
        core == 0,
        jnp.concatenate([part, part_other], axis=0),
        jnp.concatenate([part_other, part], axis=0),
    )
    ins = (d_bc_all, pre_bc, halo_bc, aux, d_dt, conv_bc_w)
    per = (shaped((seqs, span, wide + LANES), BF), shaped((seqs, 8, span), F32))
    d_small, row_dot, bc_grads = call(
        conv_bc_kernel,
        seqs,
        ins,
        seq_of(ins[:5]) + whole_of(ins[5:]),
        per + (shaped((8, wide), F32),),
        seq_of(per) + [whole((8, wide))],
        [],
        6.3,
        "conv_bc",
    )
    small_sides = chunk_pair(normed_rows, d_small.reshape(rows, -1), False)
    out_near = core_sum(out_near[0], after(out_near[1], d_small))
    terms = [(after(d_z_rows, small_sides[1], out_near), w_in, 0), (d_x_rows, w_in, 1)]
    terms.append((d_dt_rows, w_dt, 0))
    grad_far, norm_far = share_sum(terms, 1, True)
    own_sum = fold((out_far, after(out_near, grad_far[1])), "head", 2)
    own_sum = own_sum.reshape(seqs, span, share)
    late_total = pair_sum((late_sides[0], after(late_sides[1], own_sum)))
    grad_far = core_sum(grad_far[0], after(grad_far[1], late_total))
    terms[0] = (after(d_z_rows, grad_far), w_in, 0)
    grad_near, norm_near = share_sum(terms, 0, True)
    grad_near = core_sum(grad_near[0], after(grad_near[1], own_sum))
    small_sum = after(small_sides[1], grad_near) + swap(small_sides[0], "seq", 1)
    tokens_own = lax.dynamic_slice_in_dim(tokens, offset, share, 2).astype(F32)
    layer_out = (tokens_own + own_sum.astype(F32)).astype(BF)
    own_grad = fold((grad_far, grad_near), "head", 2).reshape(seqs, span, share).astype(F32)
    late_s = small_sum[0].astype(F32)
    for m in range(1, groups):
        late_s = late_s + swap(small_sum[m], "seq", 2 * m).astype(F32)
    out_grad_own = spread_sum(out_total).astype(F32)
    x_at = lax.axis_index("seq") % 2
    gate_own = lax.dynamic_index_in_dim(gate_total, x_at, 0, False)
    gate_sent = lax.dynamic_index_in_dim(gate_total, 1 - x_at, 0, False)
    gate_grad_own = (gate_own + swap(gate_sent, "seq", 1)).astype(F32)
    late_a = spread_sum(late_total).astype(F32)

    row_dot = row_dot[:, 0]
    w_bc_own = pad_lanes(lax.dynamic_slice_in_dim(w_bc, offset, share, 0), wide + LANES)
    bc_term = dot(d_small, w_bc_own, ((2,), (1,)))
    rstd_in = aux[:, :, 6:7]
    unit_own = tokens_own * rstd_in
    gain_own = lax.dynamic_slice_in_dim(norm_gain, offset, share, 0)
    d_unit = (own_grad + bc_term) * gain_own
    input_grad = (
        rstd_in * (d_unit - unit_own * (row_dot / model)[..., None]) + cotangent.astype(F32)
    ).astype(BF)

    taps = edge + 1
    quads = n_head // 4
    norm_odd, norm_even = [
        jnp.stack([norm_near[at, 0], norm_far[at, 0]], axis=1).reshape(-1, share)
        for at in (slice(0, quads), slice(quads, 2 * quads))
    ]
    norm_even = norm_even.at[0].add(gain_own * jnp.sum(bc_term * unit_own, axis=(0, 1)))
    narrow = jnp.concatenate([norm_odd, norm_even, jnp.zeros((8 - 4 * quads, share), F32)], axis=0)
    narrow = jnp.concatenate([bc_grads, head_grads, narrow], axis=1)
    wide_sums = conv_grads + gate_grads
    lanes = max(own, narrow.shape[1])
    sums = sum_all(
        jnp.concatenate([pad_lanes(wide_sums, lanes), pad_lanes(narrow, lanes)], axis=0), "seq"
    )
    norm_sums = sums[8 : 8 + 4 * quads, wide + LANES : wide + LANES + share]
    g_norm = fold((norm_sums[: 2 * quads], norm_sums[2 * quads :]), "head") / gain_own
    summed = (
        sums[:taps, :own],
        sums[taps, :own],
        sums[8 : 8 + taps, :wide],
        sums[8 + taps, :wide],
        sums[8, wide : wide + heads],
        sums[9, wide : wide + heads],
        jnp.sum(sums[6, :own].reshape(heads, HEAD_DIM), axis=-1),
        sums[5, :own],
    )
    g_w_zx_own = jnp.stack([gate_grad_own, late_a], axis=1)
    return (
        layer_out,
        input_grad,
        g_norm,
        g_w_zx_own,
        late_s[:, :wide],
        late_s[:, wide : wide + heads],
        *summed,
        out_grad_own,
    )


def solution(mesh):
    placed = (
        P(None, "seq", None),
        P(None, "seq"),
        P(),
        P(None, None, "head"),
        P(),
        P(None, "head"),
        P(None, "head"),
        P("head"),
        P(),
        P(),
        P("head"),
        P("head"),
        P("head"),
        P("head"),
        P(None, "head"),
        P(None, "seq", "head"),
    )
    return jax.shard_map(
        local,
        mesh=mesh,
        in_specs=placed,
        out_specs=(
            P(None, "seq", "head"),
            P(None, "seq", "head"),
            P("head"),
            P("seq", None, "head"),
            P("seq", None),
            P("seq", "head"),
            P(None, "head"),
            P("head"),
            P(),
            P(),
            P("head"),
            P("head"),
            P("head"),
            P("head"),
            P("seq", "head"),
        ),
        check_vma=False,
    )
```

```python
import functools

import jax
import jax.numpy as jnp
from jax import lax
from jax.experimental import pallas as pl
from jax.experimental.pallas import tpu as pltpu
from jax.sharding import PartitionSpec as P

HEAD_DIM = 64
BLOCK_LEN = 256
LANES = 128
EDGE = 16
ROWS = 16
VMEM = 56 * 2**20
EPS = 1e-05
BF = jnp.bfloat16
F32 = jnp.float32
def cost(micros):
    return pl.CostEstimate(flops=int(micros * 1.15e+09), bytes_accessed=1000, transcendentals=0)


SMEM_SPEC = pl.BlockSpec(memory_space=pltpu.SMEM)


def dot(a, b, contract=((1,), (0,)), precision=None):
    return lax.dot_general(
        a, b, (contract, ((), ())), preferred_element_type=F32, precision=precision
    )


def halves(value):
    high = value.astype(BF)
    return high, (value - high.astype(F32)).astype(BF)


def widen(value, expand):
    high, low = halves(value)
    return dot(high, expand) + dot(low, expand)


def per_head(value, expand):
    lane = lax.broadcasted_iota(jnp.int32, (1, LANES), 1)
    left = lane < HEAD_DIM
    total = None
    for pair in range(value.shape[1] // LANES):
        both = value[:, pair * LANES : (pair + 1) * LANES]
        low = jnp.sum(jnp.where(left, both, 0.0), axis=1, keepdims=True)
        high = jnp.sum(jnp.where(left, 0.0, both), axis=1, keepdims=True)
        placed = jnp.where(lane == 2 * pair, low, jnp.where(lane == 2 * pair + 1, high, 0.0))
        total = placed if total is None else total + placed
    return total


def to_row(column):
    rows = column.shape[0]
    return jnp.transpose(jnp.broadcast_to(column, (rows, LANES)))[:8]


def sigmoid(value):
    return 0.5 * jnp.tanh(0.5 * value) + 0.5


def softplus(value):
    return jnp.maximum(value, 0.0) + jnp.log1p(jnp.exp(-jnp.abs(value)))


def triangle(span, lower):
    row = lax.broadcasted_iota(jnp.int32, (span, span), 0)
    col = lax.broadcasted_iota(jnp.int32, (span, span), 1)
    return ((col <= row) if lower else (col >= row)).astype(F32)


def running(value, lower):
    width = value.shape[1]
    high, low = halves(value)
    lowest = (value - high.astype(F32) - low.astype(F32)).astype(BF)
    parts = jnp.concatenate([high, low, lowest], axis=1)
    sums = dot(triangle(value.shape[0], lower).astype(BF), parts)
    return sums[:, :width] + sums[:, width : 2 * width] + sums[:, 2 * width :]


def doc_mask(seg_col, seg_row, lower):
    span = seg_col.shape[0]
    row = lax.broadcasted_iota(jnp.int32, (span, span), 0)
    col = lax.broadcasted_iota(jnp.int32, (span, span), 1)
    causal = (col <= row) if lower else (col >= row)
    return jnp.where(causal, (seg_col == seg_row).astype(F32), 0.0)


def back_rows(value, steps):
    return value if steps == 0 else pltpu.roll(value, steps, 0)


def ahead_rows(value, steps):
    return value if steps == 0 else pltpu.roll(value, value.shape[0] - steps, 0)


def conv_rows(extended, aux, weight):
    taps = 4
    out = weight[taps : taps + 1] + weight[taps - 1 : taps] * extended[EDGE:]
    for tap in range(taps - 1):
        window = back_rows(extended, taps - 1 - tap)[EDGE:]
        out = out + weight[tap : tap + 1] * (aux[:, tap : tap + 1] * window)
    return out


def conv_back_rows(d_conv, extended, aux, weight, grad_ref=None):
    taps = 4
    room = jnp.zeros((EDGE, d_conv.shape[1]), F32)
    total = None
    for tap in range(taps):
        steps = taps - 1 - tap
        masked = d_conv if steps == 0 else d_conv * aux[:, tap : tap + 1]
        if grad_ref is not None:
            window = back_rows(extended, steps)[EDGE:]
            grad_ref[tap : tap + 1] += jnp.sum(masked * window, axis=0, keepdims=True)
        placed = jnp.concatenate([room, masked * weight[tap : tap + 1]], axis=0)
        placed = ahead_rows(placed, steps)
        total = placed if total is None else total + placed
    if grad_ref is not None:
        grad_ref[taps : taps + 1] += jnp.sum(d_conv, axis=0, keepdims=True)
    return total


def chunk_grid(count, rows, own):
    across = count * ROWS // rows
    return across, own // across


def cut(value, scratch, at, count):
    across, width = chunk_grid(count, value.shape[0], value.shape[1])
    for j in range(count):
        a, b = j // across, j % across
        scratch[j, at] = value[a * ROWS : (a + 1) * ROWS, b * width : (b + 1) * width].astype(BF)


def uncut(scratch, at, count, rows, own):
    across, _ = chunk_grid(count, rows, own)
    return jnp.concatenate(
        [
            jnp.concatenate([scratch[a * across + b, at] for b in range(across)], axis=1)
            for a in range(count // across)
        ],
        axis=0,
    )


def both_halves(me, mine_ref, other_ref):
    mine, other = mine_ref[0], other_ref[0]
    return jnp.where(
        me % 2 == 0,
        jnp.concatenate([mine, other], axis=0),
        jnp.concatenate([other, mine], axis=0),
    )


def front_kernel(
    state, me_ref, tok_ref, halo_ref, gain_ref, w_ref, w_small_ref, seg_ref, conv_x_ref,
    conv_bc_ref, head_ref, expand_ref, normed_ref, pre_x_ref, pre_bc_ref, halo_x_ref, halo_bc_ref,
    x_ref, bc_ref, dt_ref, cum_ref, aux_ref, keep_ref, send_ref
):
    s = pl.program_id(0)
    seqs = pl.num_programs(0)
    odd = me_ref[0] % 2
    half = state // 2
    wide = 2 * state
    span = tok_ref.shape[1]

    def norm(value):
        value = value.astype(F32)
        rstd = lax.rsqrt(jnp.mean(value * value, axis=-1, keepdims=True) + EPS)
        return (value * rstd * gain_ref[...]).astype(BF), rstd

    normed, rstd = norm(tok_ref[0])
    normed_ref[0] = normed
    room = jnp.zeros((EDGE - halo_ref.shape[1], halo_ref.shape[2]), F32)
    ahead = jnp.concatenate([room, norm(halo_ref[0])[0].astype(F32)], axis=0).astype(BF)
    rows = jnp.concatenate([ahead, normed], axis=0)
    pre_x = dot(rows, w_ref[0]).astype(BF)
    small = dot(rows, w_small_ref[...])
    pre_bc = small[:, :wide].astype(BF)
    dt_raw = small[EDGE:, wide:]

    seg = jnp.transpose(jnp.broadcast_to(seg_ref[0, 0:1], (LANES, LANES + span)))[LANES - EDGE :]
    here = seg[EDGE:]
    lane = lax.broadcasted_iota(jnp.int32, here.shape, 1)
    columns = [(back_rows(seg, 3 - tap)[EDGE:] == here).astype(F32) for tap in range(3)]
    columns.append((here == here[-1:]).astype(F32))
    columns.append((here == seg[EDGE - 1 : EDGE]).astype(F32))
    columns.append(here)
    columns.append(jnp.broadcast_to(rstd, here.shape))
    aux = jnp.zeros(here.shape, F32)
    for at, column in enumerate(columns):
        aux = jnp.where(lane == at, column, aux)
    aux_ref[0] = aux

    dt_ref[0] = dt_raw
    pre_x_ref[0] = pre_x[EDGE:]
    halo_x_ref[0] = pre_x[:EDGE]
    pre_bc_ref[0] = pre_bc[EDGE:]
    halo_bc_ref[0] = pre_bc[:EDGE]
    conv = conv_rows(pre_bc.astype(F32), aux, conv_bc_ref[...])
    bc = (conv * sigmoid(conv)).astype(BF)
    bc_ref[0] = bc
    conv = conv_rows(pre_x.astype(F32), aux, conv_x_ref[...])
    x = (conv * sigmoid(conv)).astype(BF)
    x_ref[0] = x
    x_float = x.astype(F32)
    step = softplus(dt_raw + head_ref[0:1])
    cum = running(-head_ref[1:2] * step, True)
    cum_ref[0] = cum
    expand = expand_ref[...]
    last = cum[-1:]
    tail_step = jnp.exp(last - cum) * aux[:, 3:4] * step
    loaded = (x_float * widen(tail_step, expand)).astype(BF)
    own_state = dot(bc[:, :state], loaded, ((0,), (0,)))
    low, high = own_state[:half], own_state[half:]
    at = pl.ds(pl.multiple_of(s * half, half), half)
    keep_ref[at] = jnp.where(odd == 0, low, high).astype(BF)
    send_ref[at] = jnp.where(odd == 0, high, low).astype(BF)

    decay = jnp.broadcast_to(jnp.exp(last) * aux[-1:, 4:5], (8, LANES))
    decay_wide = widen(decay, expand)[:1]
    high = decay_wide.astype(BF).astype(F32)
    places = lax.broadcasted_iota(jnp.int32, (ROWS, 1), 0)
    extra = jnp.where(places == s, high, 0.0) + jnp.where(
        places == s + seqs, decay_wide - high, 0.0
    )
    end = pl.ds(seqs * half, ROWS)

    @pl.when(s == 0)
    def _():
        keep_ref[end] = extra.astype(BF)

    @pl.when(s > 0)
    def _():
        keep_ref[end] = (keep_ref[end].astype(F32) + extra).astype(BF)

    @pl.when(s == seqs - 1)
    def _():
        send_ref[end] = keep_ref[end]


def pair_kernel(seqs, groups, half, me_ref, mine_ref, other_ref, *rest):
    outs, decay_ref, scratch = rest[:groups], rest[groups], rest[groups + 1]
    odd, place = me_ref[0] % 2, me_ref[0] // 2
    end = seqs * half
    packed = [ref[end : end + ROWS].astype(F32) for ref in (mine_ref, other_ref)]
    mine, other = [p[:seqs] + p[seqs : 2 * seqs] for p in packed]
    first = jnp.where(odd == 0, mine, other)
    second = jnp.where(odd == 0, other, mine)
    decay_ref[0:seqs] = first
    decay_ref[8 : 8 + seqs] = second
    both = first * second
    high = both.astype(BF).astype(F32)
    room = jnp.zeros((ROWS - 2 * seqs, both.shape[1]), F32)
    extra = jnp.concatenate([high, both - high, room], axis=0)
    width = scratch.shape[3]
    across, _ = chunk_grid(groups, half, both.shape[1])
    for j in range(groups):
        b = j % across
        scratch[j, seqs] = extra[:, b * width : (b + 1) * width].astype(BF)
    for s in range(seqs):
        rows = slice(s * half, (s + 1) * half)
        mine, other = mine_ref[rows].astype(F32), other_ref[rows].astype(F32)
        early = jnp.where(odd == 0, mine, other)
        late = jnp.where(odd == 0, other, mine)
        cut(second[s : s + 1] * early + late, scratch, s, groups)
    for m in range(groups):
        outs[m][...] = scratch[place ^ m]


def pair_back_kernel(seqs, groups, half, me_ref, mine_ref, other_ref, decay_ref, *rest):
    outs, scratch = rest[:groups], rest[groups]
    odd, place = me_ref[0] % 2, me_ref[0] // 2
    for s in range(seqs):
        rows = slice(s * half, (s + 1) * half)
        mine, other = mine_ref[rows].astype(F32), other_ref[rows].astype(F32)
        early = jnp.where(odd == 0, mine, other)
        late = jnp.where(odd == 0, other, mine)
        cut(decay_ref[s : s + 1] * late + early, scratch, s, groups)
    for m in range(groups):
        outs[m][...] = scratch[place ^ m]


def scan_kernel(seqs, groups, me_ref, *rest):
    ins, outs = rest[:groups], rest[groups : 2 * groups]
    decay_ref, scratch = rest[2 * groups], rest[2 * groups + 1]
    place = me_ref[0] // 2
    for m in range(groups):
        scratch[place ^ m] = ins[m][...]
    for s in range(seqs):
        entry = jnp.zeros(scratch.shape[2:], F32)
        for k in range(groups):
            packed = scratch[k, seqs].astype(F32)
            decay = packed[s : s + 1] + packed[s + seqs : s + seqs + 1]
            decay_ref[k, s : s + 1] = decay
            arrived = scratch[k, s].astype(F32)
            scratch[k, s] = entry.astype(BF)
            entry = decay * entry + arrived
    for m in range(groups):
        outs[m][...] = scratch[place ^ m, :seqs]


def scan_back_kernel(seqs, groups, me_ref, decay_ref, *rest):
    ins, outs, scratch = rest[:groups], rest[groups : 2 * groups], rest[2 * groups]
    place = me_ref[0] // 2
    for m in range(groups):
        scratch[place ^ m] = ins[m][...]
    for s in range(seqs):
        leave = jnp.zeros(scratch.shape[2:], F32)
        for k in reversed(range(groups)):
            arrived = scratch[k, s].astype(F32)
            scratch[k, s] = leave.astype(BF)
            leave = decay_ref[k, s : s + 1] * leave + arrived
    for m in range(groups):
        outs[m][...] = scratch[place ^ m]


def unpair_kernel(seqs, groups, half, forward, me_ref, mine_ref, other_ref, decay_ref, *rest):
    ins, (own_ref, send_ref, scratch) = rest[:groups], rest[groups:]
    odd, place = me_ref[0] % 2, me_ref[0] // 2
    own = own_ref.shape[-1]
    for m in range(groups):
        scratch[place ^ m] = ins[m][...]
    is_first = (odd == 0) if forward else (odd == 1)
    for s in range(seqs):
        rows = slice(s * half, (s + 1) * half)
        entry = uncut(scratch, s, groups, half, own).astype(F32)
        mine, other = mine_ref[rows].astype(F32), other_ref[rows].astype(F32)
        first = jnp.where(is_first, mine, other)
        at = s if forward else 8 + s
        later = decay_ref[at : at + 1] * entry + first
        own_ref[s] = jnp.where(is_first, entry, later).astype(BF)
        send_ref[s] = jnp.where(is_first, later, entry).astype(BF)


def inner_kernel(
    state, bc_ref, x_ref, cum_ref, dt_ref, aux_ref, seg_ref, head_ref, expand_ref, out_ref, xs_ref
):
    own = xs_ref.shape[-1]
    step = softplus(dt_ref[0] + head_ref[0:1])
    xs_all = (x_ref[0].astype(F32) * widen(step, expand_ref[...])).astype(BF)
    xs_ref[0] = xs_all
    b_ssm, c_ssm = bc_ref[0, :, :state], bc_ref[0, :, state:]
    cum = cum_ref[0]
    cum_t = jnp.transpose(cum)
    mask = doc_mask(aux_ref[0, :, 5:6], seg_ref[0, 0:1, LANES:], True)
    scores = dot(c_ssm, b_ssm, ((1,), (1,))) * mask
    left = lax.broadcasted_iota(jnp.int32, (1, LANES), 1) < HEAD_DIM
    for pair in range(own // LANES):
        lanes = slice(pair * LANES, (pair + 1) * LANES)
        xs = xs_all[:, lanes].astype(F32)
        total = None
        for side in range(2):
            h = 2 * pair + side
            lag = jnp.minimum(cum[:, h : h + 1] - cum_t[h : h + 1], 0.0)
            weights = (scores * jnp.exp(lag)).astype(BF)
            own_xs = jnp.where(left if side == 0 else ~left, xs, 0.0).astype(BF)
            term = dot(weights, own_xs)
            total = term if total is None else total + term
        out_ref[0, :, lanes] = total


def mixer_out(state, states, x_ref, bc_ref, inner_ref, gate_ref, cum_ref, aux_ref, rows_ref, expand_ref):
    c_ssm = bc_ref[0, :, state:]
    x_float = x_ref[0].astype(F32)
    entry_wide = widen(jnp.exp(cum_ref[0]) * aux_ref[0, :, 4:5], expand_ref[...])
    mixed = inner_ref[0] + dot(c_ssm, states) * entry_wide
    y = mixed + rows_ref[1:2] * x_float
    gate = gate_ref[0].astype(F32)
    sig = sigmoid(gate)
    return mixed, y, x_float, gate, sig, entry_wide


def sums_kernel(
    state, me_ref, x_ref, bc_ref, inner_ref, gate_ref, e_ref, cum_ref, aux_ref, mine_ref,
    other_ref, rows_ref, expand_ref, out_ref
):
    states = both_halves(me_ref[0], mine_ref, other_ref)
    _, y, _, gate, sig, _ = mixer_out(
        state, states, x_ref, bc_ref, inner_ref, gate_ref, cum_ref, aux_ref, rows_ref, expand_ref
    )
    gated = y * (gate * sig)
    squares = jnp.sum(gated * gated, axis=-1, keepdims=True)
    dots = jnp.sum(e_ref[0].astype(F32) * (gated * rows_ref[0:1]), axis=-1, keepdims=True)
    place = lax.broadcasted_iota(jnp.int32, (8, 1), 0)
    out_ref[0] = jnp.where(place == 0, to_row(squares), jnp.where(place == 1, to_row(dots), 0.0))


def gate_back_kernel(
    state, inner_total, me_ref, x_ref, bc_ref, inner_ref, gate_ref, e_ref, cum_ref, aux_ref,
    mine_ref, other_ref, rows_ref, expand_ref, sums_ref, scaled_ref, dz_ref, dy_ref, mixed_ref,
    dc_ref, dot_ref, grad_ref, keep_ref, send_ref
):
    s = pl.program_id(0)
    odd = me_ref[0] % 2
    half = state // 2
    expand = expand_ref[...]
    states = both_halves(me_ref[0], mine_ref, other_ref)
    mixed, y, x_float, gate, sig, entry_wide = mixer_out(
        state, states, x_ref, bc_ref, inner_ref, gate_ref, cum_ref, aux_ref, rows_ref, expand_ref
    )
    columns = jnp.transpose(
        jnp.concatenate([sums_ref[0], jnp.zeros((LANES - 8, sums_ref.shape[2]), F32)], axis=0)
    )
    rstd = lax.rsqrt(columns[:, 0:1] / inner_total + EPS)
    slope = columns[:, 1:2] * (rstd * rstd * rstd) / inner_total
    gain = rows_ref[0:1]
    silu = gate * sig
    gated = y * silu
    scaled_ref[0] = (gated * gain * rstd).astype(BF)
    d_scaled = e_ref[0].astype(F32) * rstd
    d_gated = d_scaled * gain - slope * gated
    d_y = d_gated * silu
    dy_ref[0] = d_y.astype(BF)
    d_z = (d_gated * y * (sig * (1.0 + gate * (1.0 - sig)))).astype(BF)
    dz_ref[0] = d_z
    row = jnp.sum(d_z.astype(F32) * gate, axis=-1, keepdims=True)
    dot_ref[0] = to_row(row)
    mixed_ref[0] = per_head(d_y * mixed, expand)

    @pl.when(s == 0)
    def _():
        grad_ref[...] = jnp.zeros_like(grad_ref)

    grad_ref[5:6] += jnp.sum(d_scaled * gated, axis=0, keepdims=True)
    grad_ref[6:7] += jnp.sum(d_y * x_float, axis=0, keepdims=True)
    d_carried = (d_y * entry_wide).astype(BF)
    dc_ref[0] = dot(d_carried, states, ((1,), (1,)))
    grad = dot(bc_ref[0, :, state:], d_carried, ((0,), (0,)))
    low, high = grad[:half], grad[half:]
    at = pl.ds(pl.multiple_of(s * half, half), half)
    keep_ref[at] = jnp.where(odd == 0, low, high).astype(BF)
    send_ref[at] = jnp.where(odd == 0, high, low).astype(BF)


def inner_back_kernel(
    state, x_ref, bc_ref, xs_ref, dy_ref, dc_ref, cum_ref, dt_ref, aux_ref, seg_ref, rows_ref,
    head_ref, expand_ref, dx_ref, dstep_ref, dbc_ref
):
    own = xs_ref.shape[-1]
    b_ssm, c_ssm = bc_ref[0, :, :state], bc_ref[0, :, state:]
    cum = cum_ref[0]
    cum_t = jnp.transpose(cum)
    nt = ((1,), (1,))
    mask = doc_mask(aux_ref[0, :, 5:6], seg_ref[0, 0:1, LANES:], False)
    scores = dot(b_ssm, c_ssm, nt) * mask
    left = lax.broadcasted_iota(jnp.int32, (1, LANES), 1) < HEAD_DIM
    d_scores = None
    sums = []
    for pair in range(own // LANES):
        lanes = slice(pair * LANES, (pair + 1) * LANES)
        xs = xs_ref[0, :, lanes]
        dy = dy_ref[0, :, lanes].astype(F32)
        total = None
        for side in range(2):
            h = 2 * pair + side
            lag = jnp.minimum(cum_t[h : h + 1] - cum[:, h : h + 1], 0.0)
            mixing = jnp.exp(lag)
            weights = (scores * mixing).astype(BF)
            own_dy = jnp.where(left if side == 0 else ~left, dy, 0.0).astype(BF)
            term = dot(weights, own_dy)
            total = term if total is None else total + term
            d_mixed = dot(xs, own_dy, nt) * mixing
            d_scores = d_mixed if d_scores is None else d_scores + d_mixed
        sums.append(total)
    back = jnp.concatenate(sums, axis=1)
    expand = expand_ref[...]
    x_float = x_ref[0].astype(F32)
    dstep_ref[0] = per_head(x_float * back, expand)
    step = softplus(dt_ref[0] + head_ref[0:1])
    dy_all = dy_ref[0].astype(F32)
    dx_ref[0] = (back * widen(step, expand) + rows_ref[1:2] * dy_all).astype(BF)
    d_scores = (d_scores * mask).astype(BF)
    dbc_ref[0, :, :state] = dot(d_scores, c_ssm)
    dbc_ref[0, :, state:] = dot(d_scores, b_ssm, ((0,), (0,))) + dc_ref[0]


def leave_kernel(
    state, me_ref, x_ref, bc_ref, pre_ref, halo_ref, pre_bc_ref, halo_bc_ref, dx_ref, dstep_ref,
    dbc_ref, mixed_ref, cum_ref, dt_ref, aux_ref, dot_z_ref, mine_ref, other_ref, end_mine_ref,
    end_other_ref, conv_ref, conv_bc_ref, head_ref, expand_ref, dpre_ref, back_ref, back_bc_ref,
    dbc_out_ref, ddt_ref, dot_ref, grad_ref, small_ref
):
    me = me_ref[0]
    own = dx_ref.shape[-1]
    expand = expand_ref[...]
    states = both_halves(me, mine_ref, other_ref)
    ends = both_halves(me, end_mine_ref, end_other_ref)
    b_ssm = bc_ref[0, :, :state]
    x_float = x_ref[0].astype(F32)
    aux = aux_ref[0]
    dt_pre = dt_ref[0] + head_ref[0:1]
    step = softplus(dt_pre)
    rate = head_ref[1:2]
    cum = cum_ref[0]
    last = cum[-1:]
    tail_decay = jnp.exp(last - cum) * aux[:, 3:4]
    tail_step = tail_decay * step
    tail_wide = widen(tail_step, expand)
    loaded = (x_float * tail_wide).astype(BF)
    d_loaded = dot(b_ssm, ends)
    dbc_out_ref[0, :, :state] = (dbc_ref[0, :, :state] + dot(loaded, ends, ((1,), (1,)))).astype(BF)
    dbc_out_ref[0, :, state:] = dbc_ref[0, :, state:].astype(BF)
    d_bc = dbc_out_ref[0, :EDGE].astype(F32)
    extended = jnp.concatenate([halo_bc_ref[0], pre_bc_ref[0, :EDGE]], axis=0).astype(F32)
    weight = conv_bc_ref[...]
    conv = conv_rows(extended, aux[:EDGE], weight)
    sig = sigmoid(conv)
    d_conv = d_bc * (sig * (1.0 + conv * (1.0 - sig)))
    back_bc_ref[0] = conv_back_rows(d_conv, extended, aux[:EDGE], weight)[:EDGE].astype(BF)
    d_x = dx_ref[0].astype(F32) + d_loaded * tail_wide
    d_tail = per_head(d_loaded * x_float, expand)
    end_terms = d_tail * tail_step
    product = jnp.sum(ends.astype(F32) * states.astype(F32), axis=0, keepdims=True)
    d_decay = per_head(jnp.broadcast_to(product, (8, own)), expand)[:1]
    block_decay = jnp.exp(last) * aux[-1:, 4:5]
    d_cum = mixed_ref[0] - step * dstep_ref[0] - end_terms
    last_add = jnp.sum(end_terms, axis=0, keepdims=True) + d_decay * block_decay
    d_log = running(d_cum, False) + last_add
    d_step = dstep_ref[0] + d_tail * tail_decay - d_log * rate
    d_dt = d_step * sigmoid(dt_pre)
    ddt_ref[0] = d_dt.astype(BF)

    @pl.when(pl.program_id(0) == 0)
    def _():
        grad_ref[...] = jnp.zeros_like(grad_ref)
        small_ref[...] = jnp.zeros_like(small_ref)

    small_ref[0:1] += jnp.sum(d_dt, axis=0, keepdims=True)
    small_ref[1:2] += jnp.sum(d_log * (-rate * step), axis=0, keepdims=True)

    extended = jnp.concatenate([halo_ref[0], pre_ref[0]], axis=0).astype(F32)
    weight = conv_ref[...]
    conv = conv_rows(extended, aux, weight)
    sig = sigmoid(conv)
    d_conv = d_x * (sig * (1.0 + conv * (1.0 - sig)))
    d_ext = conv_back_rows(d_conv, extended, aux, weight, grad_ref)
    d_pre = d_ext[EDGE:].astype(BF)
    dpre_ref[0] = d_pre
    back_ref[0] = d_ext[:EDGE].astype(BF)
    row = jnp.sum(d_pre.astype(F32) * extended[EDGE:], axis=-1, keepdims=True)
    row = row + jnp.sum(ddt_ref[0].astype(F32) * dt_ref[0], axis=-1, keepdims=True)
    dot_ref[0] = to_row(row) + dot_z_ref[0]


def conv_bc_kernel(
    n_head, head_ref, d_ref, pre_ref, halo_ref, aux_ref, ddt_ref, conv_ref, dpre_ref, cut_ref,
    dot_ref, grad_ref
):
    span = pre_ref.shape[1]
    extended = jnp.concatenate([halo_ref[0], pre_ref[0]], axis=0).astype(F32)
    aux = aux_ref[0]
    weight = conv_ref[...]
    conv = conv_rows(extended, aux, weight)
    sig = sigmoid(conv)
    d_conv = d_ref[0, :span].astype(F32) * (sig * (1.0 + conv * (1.0 - sig)))

    @pl.when(pl.program_id(0) == 0)
    def _():
        grad_ref[...] = jnp.zeros_like(grad_ref)

    d_pre = conv_back_rows(d_conv, extended, aux, weight, grad_ref)[EDGE:]
    ahead = d_ref[0, span : span + EDGE].astype(F32)
    d_pre = jnp.concatenate([d_pre[: span - EDGE], d_pre[span - EDGE :] + ahead], axis=0)
    d_pre = d_pre.astype(BF)
    dpre_ref[0] = d_pre
    part = d_pre.shape[1] // n_head
    steps = ddt_ref[0].astype(F32)[:, : LANES - part]
    columns = d_pre.astype(F32)
    cut_out = None
    for head in range(n_head):
        own = jnp.concatenate([columns[:, head * part : (head + 1) * part], steps], axis=1)
        cut_out = own if cut_out is None else jnp.where(head_ref[0] == head, own, cut_out)
    cut_ref[0] = cut_out.astype(BF)
    row = jnp.sum(d_pre.astype(F32) * extended[EDGE:], axis=-1, keepdims=True)
    packed = d_ref[0, span + EDGE :].astype(F32)
    dot_ref[0] = to_row(row) + (packed[0:1] + packed[1:2])


def gram_kernel(a_ref, b_ref, out_ref):
    out_ref[...] = dot(a_ref[...], b_ref[...], ((0,), (0,))).astype(BF)


def gram_pair_kernel(me_ref, a_ref, b_ref, odd_ref, even_ref):
    product = dot(a_ref[...], b_ref[...], ((0,), (0,))).astype(BF)
    tile = product.shape[0] // 2
    low, high = product[:tile], product[tile:]
    same = me_ref[0] % 2 == 0
    odd_ref[0] = jnp.where(same, high, low)
    even_ref[0] = jnp.where(same, low, high)


def share_kernel(terms, with_sum, me_ref, *refs):
    odd_ref, even_ref = refs[2 * terms + with_sum : 2 * terms + with_sum + 2]
    nt = ((1,), (1,))
    total = None
    for t in range(terms):
        rhs = refs[2 * t + 1]
        rhs = rhs[0] if len(rhs.shape) == 3 else rhs[...]
        term = dot(refs[2 * t][...], rhs, nt)
        total = term if total is None else total + term
    total_low = total.astype(BF)

    @pl.when(pl.program_id(0) < pl.num_programs(0) // 2)
    def _():
        odd_ref[0] = total_low

    @pl.when(pl.program_id(0) >= pl.num_programs(0) // 2)
    def _():
        even_ref[0] = total_low

    if with_sum:
        sum_ref = refs[-1]

        @pl.when(pl.program_id(1) == 0)
        def _():
            sum_ref[...] = jnp.zeros_like(sum_ref)

        normed = refs[2 * terms][...].astype(F32)
        sum_ref[0, 0:1] += jnp.sum(total * normed, axis=0, keepdims=True)


def per_seq(seqs, shape):
    zeros = (0,) * len(shape)
    return pl.BlockSpec((1, *shape), lambda s: (jnp.minimum(s, seqs - 1), *zeros))


def whole(shape):
    zeros = (0,) * len(shape)
    return pl.BlockSpec(tuple(shape), lambda s: zeros)


def call(body, grid, ins, in_specs, outs, out_specs, scratch, flops, name, aliases={}):
    return pl.pallas_call(
        body,
        grid=(grid,),
        in_specs=in_specs,
        out_specs=out_specs,
        out_shape=outs,
        scratch_shapes=scratch,
        name=name,
        input_output_aliases=aliases,
        compiler_params=pltpu.CompilerParams(vmem_limit_bytes=VMEM),
        cost_estimate=cost(flops),
    )(*ins)


def shaped(shape, dtype):
    return jax.ShapeDtypeStruct(tuple(shape), dtype)


def swap(value, axis, mask):
    count = lax.axis_size(axis)
    return lax.ppermute(value, axis, [(i, i ^ mask) for i in range(count)])


def shift(value, axis, steps):
    count = lax.axis_size(axis)
    leading, last = (max(0, -steps), min(count, count - steps))
    return lax.ppermute(value, axis, [(i, i + steps) for i in range(leading, last)])


def exchange(chunks, masks):
    return [swap(c, "seq", mask) if mask else c for c, mask in zip(chunks, masks)]


def after(value, *others):
    return lax.optimization_barrier((value, *others))[0]


def fold_step(sides, axis, mask):
    odd, even = sides
    arrived = swap(odd, axis, mask)
    if even.shape[0] == 1:
        return (even + arrived)[0]
    return even[1::2] + arrived[1::2], even[0::2] + arrived[0::2]


def fold(sides, axis, mask=1):
    while isinstance(sides, tuple):
        sides = fold_step(sides, axis, mask)
        mask *= 2
    return sides


def core_sum(odd, even):
    return even + swap(odd, "head", 1)


def pair_sides(full):
    odd = lax.axis_index("seq") % 2
    chunks = full.reshape(lax.axis_size("seq") // 2, 2, -1, full.shape[-1])
    return tuple(lax.dynamic_index_in_dim(chunks, at, 1, False) for at in (1 - odd, odd))


def pair_sum(sides):
    return sides[1] + swap(sides[0], "seq", 1)


def spread_sum(total):
    count = lax.axis_size("seq")
    return lax.psum_scatter(
        total.reshape(-1, total.shape[-1]),
        "seq",
        scatter_dimension=0,
        tiled=True,
        axis_index_groups=[[2 * z + x for z in range(count // 2)] for x in range(2)],
    )


def row_sides(full, axis):
    count = lax.axis_size(axis)
    me = lax.axis_index(axis)
    chunks = full.reshape(count, -1, full.shape[-1])

    def stacked(masks):
        return jnp.stack([lax.dynamic_index_in_dim(chunks, me ^ m, 0, False) for m in masks])

    return stacked(range(1, count, 2)), stacked(range(0, count, 2))


def sum_all(value, axis):
    mask = 1
    while mask < lax.axis_size(axis):
        value = value + swap(value, axis, mask)
        mask *= 2
    return value


def pad_lanes(value, width):
    return jnp.pad(value, ((0, 0), (0, width - value.shape[1])))


def pad_rows(rows, count=8):
    stacked = jnp.concatenate([r.reshape(-1, r.shape[-1]).astype(F32) for r in rows], axis=0)
    return jnp.pad(stacked, ((0, count - stacked.shape[0]), (0, 0)))


def local(
    tokens,
    segments,
    norm_gain,
    w_zx,
    w_bc,
    w_dt,
    conv_x,
    conv_x_bias,
    conv_bc,
    conv_bc_bias,
    dt_bias,
    a_log,
    d_skip,
    gate_gain,
    w_out,
    cotangent,
):
    seqs, span, model = tokens.shape
    rows = seqs * span
    heads = d_skip.shape[0]
    own = heads * HEAD_DIM
    n_seq, n_head = lax.axis_size("seq"), lax.axis_size("head")
    me_head = lax.axis_index("head")
    me = lax.axis_index("seq").astype(jnp.int32).reshape(1)
    head_at = me_head.astype(jnp.int32).reshape(1)
    inner_total = own * n_head
    state = w_bc.shape[1] // 2
    half = state // 2
    wide = 2 * state
    share = model // n_head
    offset = me_head * share
    edge = conv_x.shape[0] - 1
    groups = n_seq // 2
    masks = [2 * m for m in range(groups)]
    _, width = chunk_grid(groups, half, own)

    seg_lanes = jnp.broadcast_to(segments[:, -8:, None].astype(BF), (seqs, 8, LANES))
    cot_full = lax.all_gather(cotangent, "head", axis=2, tiled=True)

    w_in = lax.optimization_barrier(jnp.transpose(w_zx, (1, 0, 2)))
    halo = jnp.concatenate([after(tokens, w_in)[:, -8:], seg_lanes], axis=2)
    halo = shift(halo, "seq", 1)
    tok_halo, seg_halo = halo[..., :model], halo[..., model]
    w_dt = pad_lanes(w_dt, LANES)
    w_small = jnp.concatenate([w_bc, w_dt], axis=1)
    seg_rows = [jnp.pad(seg_halo.astype(F32), ((0, 0), (LANES - 8, 0))), segments.astype(F32)]
    seg_rows = jnp.concatenate(seg_rows, axis=1)
    seg_rows = jnp.broadcast_to(seg_rows[:, None], (seqs, 8, LANES + span))
    conv_x_w = pad_rows([conv_x, conv_x_bias])
    conv_bc_w = pad_rows([conv_bc, conv_bc_bias])
    head_rows = pad_lanes(pad_rows([dt_bias, jnp.exp(a_log)]), LANES)
    wide_rows = pad_rows([gate_gain, jnp.repeat(d_skip, HEAD_DIM)])
    expand = (
        jnp.arange(LANES)[:, None] == (jnp.arange(own) // HEAD_DIM)[None, :]
    ).astype(BF)

    seq = functools.partial(per_seq, seqs)

    def seq_of(values):
        return [seq(v.shape[1:]) for v in values]

    def whole_of(values):
        return [whole(v.shape) for v in values]

    w_x_spec = pl.BlockSpec((1, model, own), lambda s: (1, 0, 0))
    ins = (
        me, tokens, tok_halo, norm_gain.reshape(1, model), w_in, w_small, seg_rows, conv_x_w,
        conv_bc_w, head_rows, expand,
    )
    per = (
        shaped((seqs, span, model), BF),
        shaped((seqs, span, own), BF),
        shaped((seqs, span, wide), BF),
        shaped((seqs, EDGE, own), BF),
        shaped((seqs, EDGE, wide), BF),
        shaped((seqs, span, own), BF),
        shaped((seqs, span, wide), BF),
        shaped((seqs, span, LANES), F32),
        shaped((seqs, span, LANES), F32),
        shaped((seqs, span, LANES), F32),
    )
    packed = (shaped((seqs * half + ROWS, own), BF),) * 2
    normed, pre_x, pre_bc, halo_x, halo_bc, x_ssm, bc_ssm, dt_raw, cum, aux, keep, send = call(
        functools.partial(front_kernel, state),
        seqs,
        ins,
        [SMEM_SPEC, *seq_of(ins[1:3]), whole(ins[3].shape), w_x_spec, whole(w_small.shape)]
        + seq_of(ins[6:7])
        + whole_of(ins[7:]),
        per + packed,
        seq_of(per) + whole_of(packed),
        [],
        30,
        "front",
    )

    def small_call(body, ins, outs, blocks, name):
        return call(
            body,
            1,
            ins,
            [SMEM_SPEC] + whole_of(ins[1:]),
            outs,
            whole_of(outs),
            [pltpu.VMEM((groups, blocks, ROWS, width), BF)],
            3,
            name,
        )

    piece = shaped((seqs, ROWS, width), BF)
    halves_out = (shaped((seqs, half, own), BF),) * 2
    other = swap(send, "seq", 1)
    *parts, pair_decay = small_call(
        functools.partial(pair_kernel, seqs, groups, half),
        (me, keep, other),
        (shaped((seqs + 1, ROWS, width), BF),) * groups + (shaped((16, own), F32),),
        seqs + 1,
        "pair",
    )
    *entries, decays = small_call(
        functools.partial(scan_kernel, seqs, groups),
        (me, *exchange(parts, masks)),
        (piece,) * groups + (shaped((groups, 8, width), F32),),
        seqs + 1,
        "scan",
    )
    state_mine, state_send = small_call(
        functools.partial(unpair_kernel, seqs, groups, half, True),
        (me, keep, other, pair_decay, *exchange(entries, masks)),
        halves_out,
        seqs,
        "unpair",
    )
    state_other = swap(state_send, "seq", 1)

    gate = dot(normed, w_in[0], ((2,), (0,))).astype(BF)
    e_raw = dot(cot_full, w_out, ((2,), (0,))).astype(BF)
    ins = (bc_ssm, x_ssm, cum, dt_raw, aux, seg_rows, head_rows, expand)
    inner, xs = call(
        functools.partial(inner_kernel, state),
        seqs,
        ins,
        seq_of(ins[:6]) + whole_of(ins[6:]),
        (shaped((seqs, span, own), F32), shaped((seqs, span, own), BF)),
        [seq((span, own))] * 2,
        [],
        12,
        "inner",
    )

    mixer = (me, x_ssm, bc_ssm, inner, gate, e_raw, cum, aux, state_mine, state_other, wide_rows, expand)
    mixer_specs = [SMEM_SPEC] + seq_of(mixer[1:10]) + whole_of(mixer[10:])
    (sums,) = call(
        functools.partial(sums_kernel, state),
        seqs,
        mixer,
        mixer_specs,
        (shaped((seqs, 8, span), F32),),
        [seq((8, span))],
        [],
        12,
        "sums",
    )
    sums = sum_all(sums, "head")

    per = (
        shaped((seqs, span, own), BF),
        shaped((seqs, span, own), BF),
        shaped((seqs, span, own), BF),
        shaped((seqs, span, LANES), F32),
        shaped((seqs, span, state), F32),
        shaped((seqs, 8, span), F32),
    )
    fixed = (shaped((8, own), F32),) + (shaped((seqs * half, own), BF),) * 2
    scaled, d_z, d_y, mixed, d_c, dot_z, gate_grads, keep, send = call(
        functools.partial(gate_back_kernel, state, inner_total),
        seqs,
        (*mixer, sums),
        mixer_specs + [seq((8, span))],
        per + fixed,
        seq_of(per) + whole_of(fixed),
        [],
        21,
        "gate_back",
    )

    other = swap(send, "seq", 1)

    normed_rows = normed.reshape(rows, model)

    def gram(left, values):
        tile = 4 * LANES
        return call(
            gram_kernel,
            model // tile,
            (left, values),
            [pl.BlockSpec((rows, tile), lambda i: (0, i)), whole(values.shape)],
            (shaped((model, values.shape[1]), BF),),
            [pl.BlockSpec((tile, values.shape[1]), lambda i: (i, 0))],
            [],
            10.8,
            "gram",
        )[0]

    def chunk_pair(left, values, natural):
        tile = model // n_seq
        if tile % LANES:
            full = dot(left, values, ((0,), (0,))).astype(BF)
            return pair_sides(full) if natural else row_sides(full, "seq")
        block = (tile, values.shape[1])

        def at(i, me_ref):
            return i if natural else i ^ (me_ref[0] // 2)

        return tuple(
            pl.pallas_call(
                gram_pair_kernel,
                grid_spec=pltpu.PrefetchScalarGridSpec(
                    num_scalar_prefetch=1,
                    grid=(groups,),
                    in_specs=[
                        pl.BlockSpec((rows, 2 * tile), lambda i, me_ref: (0, at(i, me_ref))),
                        pl.BlockSpec(values.shape, lambda i, me_ref: (0, 0)),
                    ],
                    out_specs=[pl.BlockSpec((1, *block), lambda i, me_ref: (i, 0, 0))] * 2,
                ),
                out_shape=[shaped((groups, *block), BF)] * 2,
                name="gram_pair",
                compiler_params=pltpu.CompilerParams(vmem_limit_bytes=VMEM),
                cost_estimate=cost(rows * model * values.shape[1] / 3e8),
            )(me, left, values)
        )

    def share_sum(terms, parity, summed):
        pairs = n_head // 2
        quads = pairs // 2
        tall = rows
        def at(i, head_ref):
            core = 1 - i // quads
            return (4 * (i % quads) + 2 * parity + core) ^ head_ref[0]

        ins, specs = [], []
        for lhs, rhs, first in terms:
            ins += [lhs, rhs]
            specs.append(pl.BlockSpec((tall, lhs.shape[1]), lambda i, s, head_ref: (s, 0)))
            if rhs.ndim == 3:
                specs.append(
                    pl.BlockSpec(
                        (1, share, rhs.shape[2]),
                        lambda i, s, head_ref, first=first: (first, at(i, head_ref), 0),
                    )
                )
            else:
                specs.append(
                    pl.BlockSpec(
                        (share, rhs.shape[1]), lambda i, s, head_ref: (at(i, head_ref), 0)
                    )
                )
        out_specs = [
            pl.BlockSpec(
                (1, tall, share), lambda i, s, head_ref: (jnp.minimum(i, quads - 1), s, 0)
            ),
            pl.BlockSpec(
                (1, tall, share), lambda i, s, head_ref: (jnp.maximum(i - quads, 0), s, 0)
            ),
        ]
        outs = [shaped((quads, rows, share), BF)] * 2
        if summed:
            ins.append(normed_rows)
            specs.append(
                pl.BlockSpec((tall, share), lambda i, s, head_ref: (s, at(i, head_ref)))
            )
            out_specs.append(pl.BlockSpec((1, 8, share), lambda i, s, head_ref: (i, 0, 0)))
            outs.append(shaped((pairs, 8, share), F32))
        depth = sum(t[0].shape[1] for t in terms)
        got = pl.pallas_call(
            functools.partial(share_kernel, len(terms), summed),
            grid_spec=pltpu.PrefetchScalarGridSpec(
                num_scalar_prefetch=1,
                grid=(pairs, rows // tall),
                in_specs=specs,
                out_specs=out_specs,
            ),
            out_shape=outs,
            name="shares",
            compiler_params=pltpu.CompilerParams(vmem_limit_bytes=VMEM),
            cost_estimate=cost(rows * model * depth / 5e8),
        )(head_at, *ins)
        return (got[:2], got[2]) if summed else got

    scaled_rows, d_z_rows = scaled.reshape(rows, own), d_z.reshape(rows, own)
    out_grad = chunk_pair(cot_full.reshape(rows, model), scaled_rows, True)
    out_far = share_sum([(after(scaled_rows, out_grad[1]), w_out, 0)], 1, False)
    parts = small_call(
        functools.partial(pair_back_kernel, seqs, groups, half),
        (me, after(keep, out_far[1]), other, pair_decay),
        (piece,) * groups,
        seqs,
        "pair_back",
    )
    arrived = exchange(parts, masks)
    ins = (
        x_ssm, bc_ssm, xs, after(d_y, parts[0]), d_c, cum, dt_raw, aux, seg_rows, wide_rows, head_rows, expand,
    )
    per = (
        shaped((seqs, span, own), BF),
        shaped((seqs, span, LANES), F32),
        shaped((seqs, span, wide), F32),
    )
    d_x, d_step, d_bc = call(
        functools.partial(inner_back_kernel, state),
        seqs,
        ins,
        seq_of(ins[:9]) + whole_of(ins[9:]),
        per,
        seq_of(per),
        [],
        18.6,
        "inner_back",
    )

    leaves = small_call(
        functools.partial(scan_back_kernel, seqs, groups),
        (me, after(decays, d_x), *arrived),
        (piece,) * groups,
        seqs,
        "scan_back",
    )
    arrived = exchange(leaves, masks)
    gate_grad = gram(normed_rows, after(d_z_rows, leaves[0]))
    end_mine, end_send = small_call(
        functools.partial(unpair_kernel, seqs, groups, half, False),
        (me, after(keep, gate_grad), other, pair_decay, *arrived),
        halves_out,
        seqs,
        "unpair_back",
    )
    end_other = swap(end_send, "seq", 1)
    gate_total = spread_sum(gate_grad).reshape(2, -1, own)
    gate_total = spread_sum(gate_grad).reshape(2, -1, own)
    out_odd = share_sum([(after(scaled_rows, end_mine), w_out, 0)], 1, False)
    out_even = share_sum([(after(scaled_rows, out_odd), w_out, 0)], 0, False)

    out_total = pair_sum((out_grad[0], after(out_grad[1], end_mine)))
    ins = (
        me, after(x_ssm, out_total), bc_ssm, pre_x, halo_x, pre_bc, halo_bc, d_x, d_step, d_bc, mixed, cum,
        dt_raw, aux, dot_z, state_mine, state_other, end_mine, end_other, conv_x_w, conv_bc_w,
        head_rows, expand,
    )
    per = (
        shaped((seqs, span, own), BF),
        shaped((seqs, EDGE, own), BF),
        shaped((seqs, EDGE, wide), BF),
        shaped((seqs, span, wide), BF),
        shaped((seqs, span, LANES), BF),
        shaped((seqs, 8, span), F32),
    )
    fixed = (shaped((8, own), F32), shaped((8, LANES), F32))
    d_x_pre, back_x, back_bc, d_bc, d_dt, row_dot, conv_grads, head_grads = call(
        functools.partial(leave_kernel, state),
        seqs,
        ins,
        [SMEM_SPEC] + seq_of(ins[1:19]) + whole_of(ins[19:]),
        per + fixed,
        seq_of(per) + whole_of(fixed),
        [],
        28,
        "leave",
    )
    out_near = share_sum([(after(scaled_rows, d_x_pre), w_out, 0)], 0, False)
    out_far = core_sum(out_far[0], after(out_far[1], out_near[1]))
    back = shift(jnp.concatenate([back_x, back_bc], axis=2)[:, -edge:], "seq", -1)
    back = after(back, out_near[1])
    back_x, back_bc = back[..., :own], back[..., own:]
    fix = jnp.sum(back_x.astype(F32) * pre_x[:, -edge:].astype(F32), axis=-1)
    row_dot = row_dot[:, 0] + jnp.pad(fix, ((0, 0), (span - edge, 0)))
    dot_high = row_dot.astype(BF)
    dot_low = (row_dot - dot_high.astype(F32)).astype(BF)
    dots = jnp.pad(jnp.stack([dot_high, dot_low], axis=1), ((0, 0), (0, EDGE - 2), (0, 0)))
    back_bc = jnp.pad(back_bc, ((0, 0), (EDGE - edge, 0), (0, 0)))
    d_bc = jnp.concatenate([d_bc, back_bc, dots], axis=1)
    d_bc = d_bc + swap(d_bc, "head", 1)
    d_x_pre = after(d_x_pre, d_bc, out_far).at[:, -edge:].add(back_x)
    d_x_rows = d_x_pre.reshape(rows, own)
    d_dt_rows = d_dt.reshape(rows, LANES)
    late_sides = chunk_pair(normed_rows, d_x_rows, True)

    core, middle = me_head % 2, seqs // 2
    part = lax.dynamic_slice_in_dim(d_bc, core * middle, middle, 0)
    mask = 2
    while mask < n_head:
        part = part + swap(part, "head", mask)
        mask *= 2
    part = after(part, late_sides[1])
    part_other = swap(part, "head", 1)
    d_bc_all = jnp.where(
        core == 0,
        jnp.concatenate([part, part_other], axis=0),
        jnp.concatenate([part_other, part], axis=0),
    )
    ins = (head_at, d_bc_all, pre_bc, halo_bc, aux, d_dt, conv_bc_w)
    per = (
        shaped((seqs, span, wide), BF),
        shaped((seqs, span, LANES), BF),
        shaped((seqs, 8, span), F32),
    )
    d_bc_pre, d_small, row_dot, bc_grads = call(
        functools.partial(conv_bc_kernel, n_head),
        seqs,
        ins,
        [SMEM_SPEC] + seq_of(ins[1:6]) + whole_of(ins[6:]),
        per + (shaped((8, wide), F32),),
        seq_of(per) + [whole((8, wide))],
        [],
        6.3,
        "conv_bc",
    )
    small_sides = chunk_pair(normed_rows, d_small.reshape(rows, -1), False)
    out_near = core_sum(out_near[0], after(out_near[1], d_small))
    terms = [(after(d_z_rows, small_sides[1], out_near), w_in, 0), (d_x_rows, w_in, 1)]
    terms.append((d_dt_rows, w_dt, 0))
    grad_far, norm_far = share_sum(terms, 1, True)
    own_sum = fold((out_far, after(out_near, grad_far[1])), "head", 2)
    own_sum = own_sum.reshape(seqs, span, share)
    late_total = pair_sum((late_sides[0], after(late_sides[1], own_sum)))
    grad_far = core_sum(grad_far[0], after(grad_far[1], late_total))
    terms[0] = (after(d_z_rows, grad_far), w_in, 0)
    grad_near, norm_near = share_sum(terms, 0, True)
    grad_near = core_sum(grad_near[0], after(grad_near[1], own_sum))
    small_sum = after(small_sides[1], grad_near) + swap(small_sides[0], "seq", 1)
    tokens_own = lax.dynamic_slice_in_dim(tokens, offset, share, 2).astype(F32)
    layer_out = (tokens_own + own_sum.astype(F32)).astype(BF)
    own_grad = fold((grad_far, grad_near), "head", 2).reshape(seqs, span, share).astype(F32)
    late_s = small_sum[0].astype(F32)
    for m in range(1, groups):
        late_s = late_s + swap(small_sum[m], "seq", 2 * m).astype(F32)
    part = wide // n_head
    g_w_bc, mask = late_s[:, :part], 1
    while mask < n_head:
        arrived = swap(g_w_bc, "head", mask)
        g_w_bc = jnp.where(
            (me_head // mask) % 2 == 0,
            jnp.concatenate([g_w_bc, arrived], axis=1),
            jnp.concatenate([arrived, g_w_bc], axis=1),
        )
        mask *= 2
    out_grad_own = spread_sum(out_total).astype(F32)
    x_at = lax.axis_index("seq") % 2
    gate_own = lax.dynamic_index_in_dim(gate_total, x_at, 0, False)
    gate_sent = lax.dynamic_index_in_dim(gate_total, 1 - x_at, 0, False)
    gate_grad_own = (gate_own + swap(gate_sent, "seq", 1)).astype(F32)
    late_a = spread_sum(late_total).astype(F32)

    row_dot = row_dot[:, 0]
    w_bc_own = lax.dynamic_slice_in_dim(w_bc, offset, share, 0)
    bc_term = dot(d_bc_pre, w_bc_own, ((2,), (1,)))
    rstd_in = aux[:, :, 6:7]
    unit_own = tokens_own * rstd_in
    gain_own = lax.dynamic_slice_in_dim(norm_gain, offset, share, 0)
    d_unit = (after(own_grad, gate_grad_own) + bc_term) * gain_own
    input_grad = (
        rstd_in * (d_unit - unit_own * (row_dot / model)[..., None]) + cotangent.astype(F32)
    ).astype(BF)

    taps = edge + 1
    quads = n_head // 4
    norm_odd, norm_even = [
        jnp.stack([norm_near[at, 0], norm_far[at, 0]], axis=1).reshape(-1, share)
        for at in (slice(0, quads), slice(quads, 2 * quads))
    ]
    norm_even = norm_even.at[0].add(gain_own * jnp.sum(bc_term * unit_own, axis=(0, 1)))
    narrow = jnp.concatenate([norm_odd, norm_even, jnp.zeros((8 - 4 * quads, share), F32)], axis=0)
    narrow = jnp.concatenate([bc_grads, head_grads, narrow], axis=1)
    wide_sums = conv_grads + gate_grads
    lanes = max(own, narrow.shape[1])
    sums = sum_all(
        jnp.concatenate([pad_lanes(wide_sums, lanes), pad_lanes(narrow, lanes)], axis=0), "seq"
    )
    norm_sums = sums[8 : 8 + 4 * quads, wide + LANES : wide + LANES + share]
    g_norm = fold((norm_sums[: 2 * quads], norm_sums[2 * quads :]), "head") / gain_own
    summed = (
        sums[:taps, :own],
        sums[taps, :own],
        sums[8 : 8 + taps, :wide],
        sums[8 + taps, :wide],
        sums[8, wide : wide + heads],
        sums[9, wide : wide + heads],
        jnp.sum(sums[6, :own].reshape(heads, HEAD_DIM), axis=-1),
        sums[5, :own],
    )
    g_w_zx_own = jnp.stack([gate_grad_own, late_a], axis=1)
    return (
        layer_out,
        input_grad,
        g_norm,
        g_w_zx_own,
        g_w_bc,
        late_s[:, part : part + heads],
        *summed,
        out_grad_own,
    )


def solution(mesh):
    placed = (
        P(None, "seq", None),
        P(None, "seq"),
        P(),
        P(None, None, "head"),
        P(),
        P(None, "head"),
        P(None, "head"),
        P("head"),
        P(),
        P(),
        P("head"),
        P("head"),
        P("head"),
        P("head"),
        P(None, "head"),
        P(None, "seq", "head"),
    )
    return jax.shard_map(
        local,
        mesh=mesh,
        in_specs=placed,
        out_specs=(
            P(None, "seq", "head"),
            P(None, "seq", "head"),
            P("head"),
            P("seq", None, "head"),
            P("seq", None),
            P("seq", "head"),
            P(None, "head"),
            P("head"),
            P(),
            P(),
            P("head"),
            P("head"),
            P("head"),
            P("head"),
            P("seq", "head"),
        ),
        check_vma=False,
    )
```
